256 devices in a mesh: line: 64 (over x, z, core), span: 4 (over y).
Axes of the slice: x: 4, y: 4, z: 8, core: 2. Of those that a mesh axis runs over, the one named last changes fastest.
Arguments:
- forcing: float32 [32, 2048, 256], P('span', 'line'), may hold values from -1 to 1
- blocks: float32 [2048, 256, 256], P(('line', 'span')), may hold values from -1 to 1
- upstream: float32 [2048, 256], P(('line', 'span')), may hold values from -2 to 0
Outputs:
- solution: float32 [32, 2048, 256], P('span', 'line')
The draws below stay inside these ranges and needn't reach their ends.
All inputs are finite; a program needn't handle non-finite values.
Results may differ from the reference program's by a relative error of at most 0.0003.
Values sent between devices are 32-bit elements; how exact they have to be, the bound alone decides.
No kernel may reach another device: no remote copies, remote signals or barrier semaphores. Data moves between devices by JAX's collectives and lax.ppermute only.
A program may use at most 192 MiB of HBM per device.

```python
import math
import jax
import jax.numpy as jnp
from jax import lax

LEVELS = 256
LINES = 32
CELLS = 2048


def coefficients(key):
    share = 5
    slow = jax.random.randint(jax.random.fold_in(key, 1), (LEVELS,), 0, 10) < share
    diag_part = jax.random.uniform(jax.random.fold_in(key, 2), (CELLS, LEVELS), jnp.float32, 0.5, 1.0)
    slow_base = jnp.exp(jax.random.uniform(jax.random.fold_in(key, 3), (LEVELS,), jnp.float32, math.log(0.4), math.log(1.2))) / CELLS
    fast_base = jnp.exp(jax.random.uniform(jax.random.fold_in(key, 4), (LEVELS,), jnp.float32, math.log(1.0 / 300.0), math.log(1.0 / 30.0)))
    base_rate = jnp.where(slow, slow_base, fast_base)
    where_cell = jnp.arange(CELLS).astype(jnp.float32) / CELLS
    phase = jax.random.uniform(jax.random.fold_in(key, 5), (), jnp.float32, 0.0, 2.0 * math.pi)
    region = 1.0 + 0.4 * jnp.sin(2.0 * math.pi * 3.0 * where_cell + phase)
    rough = jax.random.uniform(jax.random.fold_in(key, 6), (CELLS, LEVELS), jnp.float32, 0.7, 1.4)
    retain = 1.0 - base_rate[None, :] * region[:, None] * rough
    spots = jax.random.randint(jax.random.fold_in(key, 7), (3,), 0, CELLS)
    depth = jax.random.uniform(jax.random.fold_in(key, 8), (3,), jnp.float32, 0.5, 0.8)
    hits = jnp.where(jnp.arange(CELLS)[:, None] == spots[None, :], depth[None, :], 1.0)
    retain = retain * jnp.prod(hits, axis=1)[:, None]
    off_diag = ~jnp.eye(LEVELS, dtype=bool)
    same_class = (slow[:, None] == slow[None, :]) & off_diag
    cross_pick = jax.random.randint(jax.random.fold_in(key, 10), (CELLS, LEVELS, LEVELS), 0, 10) == 0
    unit = 0.2 / math.sqrt(LEVELS / 2)
    entry_scale = jnp.where(same_class[None, :, :], unit, jnp.where(cross_pick & off_diag[None, :, :], 0.3 * unit, 0.0))
    noise = jnp.clip(jax.random.normal(jax.random.fold_in(key, 9), (CELLS, LEVELS, LEVELS), jnp.float32), -4.0, 4.0)
    off_part = noise * entry_scale
    whole = off_part + jnp.eye(LEVELS, dtype=jnp.float32)[None, :, :] * diag_part[:, :, None]
    energy = diag_part * diag_part + jnp.sum(off_part * off_part, axis=2)
    coupling = -retain / jnp.sqrt(energy)
    return (whole, coupling)


def draw_blocks(key, part):
    whole, coupling = coefficients(key)
    return whole.astype(jnp.float32)


def draw_upstream(key, part):
    whole, coupling = coefficients(key)
    return coupling.astype(jnp.float32)


def draw_forcing(key, part):
    values = 0.1 * jnp.clip(jax.random.normal(jax.random.fold_in(key, 12), (LINES, CELLS, LEVELS), jnp.float32), -6.0, 6.0)
    return values.astype(jnp.float32)


def setup_inputs(seed: int = 0) -> dict:
    key_list = jax.random.split(jax.random.key(seed), 4)
    return {
        "forcing": draw_forcing(jax.random.fold_in(key_list[3], 71), 0),
        "blocks": draw_blocks(jax.random.fold_in(key_list[3], 71), 0),
        "upstream": draw_upstream(jax.random.fold_in(key_list[3], 71), 0),
    }


def reference(forcing, blocks, upstream):
    initial = jnp.zeros((forcing.shape[0], forcing.shape[2]), jnp.float32)

    def advance(carried, cell_items):
        cell_forcing, cell_block, cell_upstream = cell_items
        updated = jnp.dot(cell_forcing - cell_upstream[None, :] * carried, cell_block,
                          precision=lax.Precision.HIGHEST, preferred_element_type=jnp.float32)
        return updated, updated

    _, history = lax.scan(advance, initial, (jnp.moveaxis(forcing, 1, 0), blocks, upstream))
    return jnp.moveaxis(history, 0, 1)
```

```python
import functools

import jax
import jax.numpy as jnp
from jax import lax
from jax.experimental import pallas as pl
from jax.experimental.pallas import tpu as pltpu
from jax.sharding import PartitionSpec as P

F32 = jnp.float32
BIG = 2.0**40
STEP = 2.0**48
VMEM_BYTES = 48 * 2**20


def dot(a, b):
    return jnp.dot(a, b, precision=lax.Precision.HIGHEST, preferred_element_type=F32)


def whole(shape):
    return pl.BlockSpec(shape, lambda *_: (0,) * len(shape))


def call(kernel, grid, in_specs, out_specs, out_shape, scratch=(), flops=0):
    return pl.pallas_call(
        kernel,
        grid=grid,
        in_specs=in_specs,
        out_specs=out_specs,
        out_shape=out_shape,
        scratch_shapes=list(scratch),
        compiler_params=pltpu.CompilerParams(vmem_limit_bytes=VMEM_BYTES),
        cost_estimate=pl.CostEstimate(flops=flops, bytes_accessed=2**21, transcendentals=0),
    )


def settle(hat, count):
    large = jnp.max(jnp.abs(hat), keepdims=True) > BIG
    return hat * jnp.where(large, 1.0 / STEP, 1.0), count + jnp.where(large, 1.0, 0.0)


def unscale(value, count):
    for done in (0.0, 2.0, 4.0):
        left = count - done
        value = value * jnp.where(left > 1.5, STEP * STEP, jnp.where(left > 0.5, STEP, 1.0))
    return value


def maps_kernel(upstream_ref, block_ref, prefix_ref, last):
    cell = pl.program_id(0)
    scale = -upstream_ref[pl.ds(cell, 1), :]

    @pl.when(cell == 0)
    def _():
        levels = block_ref.shape[-1]
        row = lax.broadcasted_iota(jnp.int32, (levels, levels), 0)
        column = lax.broadcasted_iota(jnp.int32, (levels, levels), 1)
        last[...] = jnp.where(row == column, 1.0, 0.0).astype(F32)

    product = dot(last[...] * scale, block_ref[0])
    last[...] = product
    prefix_ref[0] = product


def prefix_maps(blocks, upstream):
    cells, levels, _ = blocks.shape
    block = pl.BlockSpec((1, levels, levels), lambda i: (i, 0, 0))
    return call(
        maps_kernel,
        (cells,),
        [whole((cells, levels)), block],
        block,
        jax.ShapeDtypeStruct(blocks.shape, F32),
        [pltpu.VMEM((levels, levels), F32)],
        12 * cells * levels**3,
    )(upstream, blocks)


def states_kernel(upstream_ref, block_ref, forcing_ref, product_ref, trial_ref, message_ref, last):
    cell = pl.program_id(0)
    lines, levels = last.shape

    @pl.when(cell == 0)
    def _():
        last[...] = jnp.zeros_like(last)

    state = dot(forcing_ref[:, cell, :] - upstream_ref[pl.ds(cell, 1), :] * last[...], block_ref[0])
    last[...] = state
    trial_ref[0] = state

    @pl.when(cell == pl.num_programs(0) - 1)
    def _():
        hat, count = settle(product_ref[0], jnp.zeros((8, levels), F32))
        message_ref[:levels] = hat
        message_ref[levels : levels + lines] = state
        message_ref[levels + lines :] = count


def trial_states(blocks, upstream, forcing, prefix):
    cells, levels, _ = blocks.shape
    lines = forcing.shape[0]
    rows = levels + lines + 8
    return call(
        states_kernel,
        (cells,),
        [
            whole((cells, levels)),
            pl.BlockSpec((1, levels, levels), lambda i: (i, 0, 0)),
            whole(forcing.shape),
            pl.BlockSpec((1, levels, levels), lambda i: (cells - 1, 0, 0)),
        ],
        [pl.BlockSpec((1, lines, levels), lambda i: (i, 0, 0)), whole((rows, levels))],
        [
            jax.ShapeDtypeStruct((cells, lines, levels), F32),
            jax.ShapeDtypeStruct((rows, levels), F32),
        ],
        [pltpu.VMEM((lines, levels), F32)],
        12 * cells * lines * levels**2,
    )(upstream, blocks, forcing, prefix)


def merge_kernel(levels, upper_ref, mine_ref, theirs_ref, before_ref, total_ref, ahead_ref):
    states = mine_ref.shape[0] - 8

    def joined(left_ref, right_ref, out_ref):
        both = dot(left_ref[:states], right_ref[:levels])
        hat, count = settle(both[:levels], left_ref[states:] + right_ref[states:])
        out_ref[:levels] = hat
        out_ref[levels:states] = (
            unscale(both[levels:], right_ref[states : states + 1]) + right_ref[levels:states]
        )
        out_ref[states:] = count

    @pl.when(upper_ref[0] == 1)
    def _():
        joined(theirs_ref, mine_ref, total_ref)
        joined(theirs_ref, before_ref, ahead_ref)

    @pl.when(upper_ref[0] == 0)
    def _():
        joined(mine_ref, theirs_ref, total_ref)
        ahead_ref[...] = before_ref[...]


def merge(levels, upper, mine, theirs, before):
    spec = whole(mine.shape)
    shape = jax.ShapeDtypeStruct(mine.shape, F32)
    return call(
        functools.partial(merge_kernel, levels),
        (1,),
        [pl.BlockSpec(memory_space=pltpu.SMEM), spec, spec, spec],
        [spec, spec],
        [shape, shape],
        (),
        24 * mine.shape[0] * levels**2,
    )(upper, mine, theirs, before)


def finish_kernel(
    levels, upper_ref, theirs_ref, before_ref, prefix_ref, trial_ref, solved_ref, incoming
):
    cell = pl.program_id(0)
    states = before_ref.shape[0] - 8

    @pl.when(cell == 0)
    def _():
        incoming[...] = before_ref[levels:states]

        @pl.when(upper_ref[0] == 1)
        def _():
            incoming[...] += unscale(
                dot(theirs_ref[...], before_ref[:levels]), before_ref[states : states + 1]
            )

    solved_ref[:, cell, :] = trial_ref[0] + dot(incoming[...], prefix_ref[0])


def finish(levels, upper, theirs, before, prefix, trial):
    cells, lines, _ = trial.shape
    return call(
        functools.partial(finish_kernel, levels),
        (cells,),
        [
            pl.BlockSpec(memory_space=pltpu.SMEM),
            whole(theirs.shape),
            whole(before.shape),
            pl.BlockSpec((1, levels, levels), lambda i: (i, 0, 0)),
            pl.BlockSpec((1, lines, levels), lambda i: (i, 0, 0)),
        ],
        whole((lines, cells, levels)),
        jax.ShapeDtypeStruct((lines, cells, levels), F32),
        [pltpu.VMEM((lines, levels), F32)],
        12 * (cells + 1) * lines * levels**2,
    )(upper, theirs, before, prefix, trial)


def shards(sizes, forcing, blocks, upstream):
    line_count, span_count = sizes
    cells, levels, _ = blocks.shape
    share = forcing.shape[0]
    lines = share * span_count
    parts = forcing.reshape(share, span_count, cells, levels).swapaxes(0, 1)
    parts = lax.all_to_all(parts, "span", split_axis=0, concat_axis=0, tiled=True)
    local_forcing = parts.reshape(lines, cells, levels)
    prefix = prefix_maps(blocks, upstream)
    trial, total = trial_states(blocks, upstream, local_forcing, prefix)

    rounds = [("span", 1 << b) for b in range(span_count.bit_length() - 1)]
    rounds += [("line", 1 << b) for b in range(line_count.bit_length() - 1)]
    before = jnp.concatenate(
        [jnp.eye(levels, dtype=F32), jnp.zeros((lines + 8, levels), F32)], axis=0
    )

    def partner(value, axis, bit):
        count = lax.axis_size(axis)
        return lax.ppermute(value, axis, [(i, i ^ bit) for i in range(count)])

    def is_upper(axis, bit):
        return jnp.where((lax.axis_index(axis) & bit) != 0, 1, 0).astype(jnp.int32).reshape(1)

    for axis, bit in rounds[:-1]:
        theirs = partner(total, axis, bit)
        total, before = merge(levels, is_upper(axis, bit), total, theirs, before)
    axis, bit = rounds[-1]
    theirs = partner(total[levels : levels + lines], axis, bit)
    solved = finish(levels, is_upper(axis, bit), theirs, before, prefix, trial)
    parts = solved.reshape(span_count, share, cells, levels)
    parts = lax.all_to_all(parts, "span", split_axis=0, concat_axis=0, tiled=True)
    return parts.swapaxes(0, 1).reshape(share, span_count * cells, levels)


def solution(mesh):
    placed = (P("span", "line", None), P(("line", "span"), None, None), P(("line", "span"), None))
    sizes = (mesh.shape["line"], mesh.shape["span"])
    return jax.shard_map(
        functools.partial(shards, sizes),
        mesh=mesh,
        in_specs=placed,
        out_specs=P("span", "line", None),
        check_vma=False,
    )
```

```python
import functools

import jax
import jax.numpy as jnp
from jax import lax
from jax.experimental import pallas as pl
from jax.experimental.pallas import tpu as pltpu
from jax.sharding import PartitionSpec as P

F32 = jnp.float32
BIG = 2.0**40
STEP = 2.0**48
CORE = 1
ROUNDS = (
    ("span", 1, 1, False),
    ("span", 3, 2, False),
    ("line", 1, 1, False),
    ("line", 2, 2, True),
    ("line", 4, 4, True),
    ("line", 14, 8, True),
    ("line", 16, 16, False),
    ("line", 48, 32, False),
)
VMEM_BYTES = 60 * 2**20


def dot(a, b):
    return jnp.dot(a, b, precision=lax.Precision.HIGHEST, preferred_element_type=F32)


def whole(shape):
    return pl.BlockSpec(shape, lambda *_: (0,) * len(shape))


def call(kernel, grid, in_specs, out_specs, out_shape, scratch=(), flops=0, vmem=VMEM_BYTES):
    return pl.pallas_call(
        kernel,
        grid=grid,
        in_specs=in_specs,
        out_specs=out_specs,
        out_shape=out_shape,
        scratch_shapes=list(scratch),
        compiler_params=pltpu.CompilerParams(vmem_limit_bytes=vmem),
        cost_estimate=pl.CostEstimate(flops=flops, bytes_accessed=2**21, transcendentals=0),
    )


def settle(hat, count):
    large = jnp.max(jnp.abs(hat), keepdims=True) > BIG
    return hat * jnp.where(large, 1.0 / STEP, 1.0), count + jnp.where(large, 1.0, 0.0)


def unscale(value, count):
    for done in (0.0, 2.0, 4.0):
        left = count - done
        value = value * jnp.where(left > 1.5, STEP * STEP, jnp.where(left > 0.5, STEP, 1.0))
    return value


def maps_kernel(upstream_ref, block_ref, prefix_ref, last):
    cell = pl.program_id(0)
    scale = -upstream_ref[pl.ds(cell, 1), :]

    @pl.when(cell == 0)
    def _():
        levels = block_ref.shape[-1]
        row = lax.broadcasted_iota(jnp.int32, (levels, levels), 0)
        column = lax.broadcasted_iota(jnp.int32, (levels, levels), 1)
        last[...] = jnp.where(row == column, 1.0, 0.0).astype(F32)

    product = dot(last[...] * scale, block_ref[0])
    last[...] = product
    prefix_ref[0] = product


def prefix_maps(blocks, upstream):
    cells, levels, _ = blocks.shape
    block = pl.BlockSpec((1, levels, levels), lambda i: (i, 0, 0))
    return call(
        maps_kernel,
        (cells,),
        [whole((cells, levels)), block],
        block,
        jax.ShapeDtypeStruct(blocks.shape, F32),
        [pltpu.VMEM((levels, levels), F32)],
        12 * cells * levels**3,
    )(upstream, blocks)


def states_kernel(upstream_ref, block_ref, forcing_ref, product_ref, trial_ref, message_ref, last):
    cell = pl.program_id(0)
    lines, levels = last.shape

    @pl.when(cell == 0)
    def _():
        last[...] = jnp.zeros_like(last)

    state = dot(forcing_ref[:, cell, :] - upstream_ref[pl.ds(cell, 1), :] * last[...], block_ref[0])
    last[...] = state
    trial_ref[0] = state

    @pl.when(cell == pl.num_programs(0) - 1)
    def _():
        hat, count = settle(product_ref[0], jnp.zeros((8, levels), F32))
        message_ref[:levels] = hat
        message_ref[levels : levels + lines] = state
        message_ref[levels + lines : levels + lines + 8] = count
        message_ref[levels + lines + 8 :] = jnp.zeros_like(count)


def trial_states(blocks, upstream, forcing, prefix):
    cells, levels, _ = blocks.shape
    lines = forcing.shape[0]
    rows = levels + lines + 16
    return call(
        states_kernel,
        (cells,),
        [
            whole((cells, levels)),
            pl.BlockSpec((1, levels, levels), lambda i: (i, 0, 0)),
            whole(forcing.shape),
            pl.BlockSpec((1, levels, levels), lambda i: (cells - 1, 0, 0)),
        ],
        [pl.BlockSpec((1, lines, levels), lambda i: (i, 0, 0)), whole((rows, levels))],
        [
            jax.ShapeDtypeStruct((cells, lines, levels), F32),
            jax.ShapeDtypeStruct((rows, levels), F32),
        ],
        [pltpu.VMEM((lines, levels), F32)],
        12 * cells * lines * levels**2,
        8 * 2**20,
    )(upstream, blocks, forcing, prefix)


def joined(levels, left_ref, right_ref, out_ref):
    states = right_ref.shape[0] - 16
    both = dot(left_ref[:states], right_ref[:levels])
    hat, count = settle(
        both[:levels], left_ref[states : states + 8] + right_ref[states : states + 8]
    )
    out_ref[:levels] = hat
    out_ref[levels:states] = (
        unscale(both[levels:], right_ref[states : states + 1]) + right_ref[levels:states]
    )
    out_ref[states : states + 8] = count
    out_ref[states + 8 :] = jnp.zeros_like(count)


def merge_kernel(levels, halved, flags_ref, *refs):
    if halved:
        mine_ref, here_ref, there_ref, total_ref, theirs_ref, half_ref = refs
        half = here_ref.shape[0]

        @pl.when(flags_ref[1] == 0)
        def _():
            theirs_ref[:half] = here_ref[...]
            theirs_ref[half:] = there_ref[...]

        @pl.when(flags_ref[1] == 1)
        def _():
            theirs_ref[:half] = there_ref[...]
            theirs_ref[half:] = here_ref[...]
    else:
        mine_ref, theirs_ref, total_ref, half_ref = refs
        half = half_ref.shape[0]

    @pl.when(flags_ref[0] == 1)
    def _():
        joined(levels, theirs_ref, mine_ref, total_ref)

    @pl.when(flags_ref[0] == 0)
    def _():
        joined(levels, mine_ref, theirs_ref, total_ref)

    @pl.when(flags_ref[1] == 0)
    def _():
        half_ref[...] = total_ref[:half]

    @pl.when(flags_ref[1] == 1)
    def _():
        half_ref[...] = total_ref[half:]


def merge(levels, flags, mine, *arrived):
    rows = mine.shape[0]
    spec, shape = whole(mine.shape), jax.ShapeDtypeStruct(mine.shape, F32)
    half_spec = whole((rows // 2, levels))
    half_shape = jax.ShapeDtypeStruct((rows // 2, levels), F32)
    halved = len(arrived) == 2
    got = call(
        functools.partial(merge_kernel, levels, halved),
        (1,),
        [pl.BlockSpec(memory_space=pltpu.SMEM), spec] + [whole(a.shape) for a in arrived],
        [spec] * (1 + halved) + [half_spec],
        [shape] * (1 + halved) + [half_shape],
        (),
        12 * rows * levels**2,
        8 * 2**20,
    )(flags, mine, *arrived)
    total, theirs, half = got if halved else (got[0], arrived[0], got[1])
    return total, theirs, half


def extend_kernel(levels, flags_ref, theirs_ref, before_ref, ahead_ref):
    @pl.when(flags_ref[0] == 1)
    def _():
        joined(levels, theirs_ref, before_ref, ahead_ref)

    @pl.when(flags_ref[0] == 0)
    def _():
        ahead_ref[...] = before_ref[...]


def begin_kernel(levels, flags_ref, theirs_ref, ahead_ref):
    @pl.when(flags_ref[0] == 1)
    def _():
        ahead_ref[...] = theirs_ref[...]

    @pl.when(flags_ref[0] == 0)
    def _():
        row = lax.broadcasted_iota(jnp.int32, ahead_ref.shape, 0)
        column = lax.broadcasted_iota(jnp.int32, ahead_ref.shape, 1)
        ahead_ref[...] = jnp.where(row == column, 1.0, 0.0).astype(F32)


def extend(levels, flags, theirs, *before):
    spec = whole(theirs.shape)
    return call(
        functools.partial(extend_kernel if before else begin_kernel, levels),
        (1,),
        [pl.BlockSpec(memory_space=pltpu.SMEM), spec] + [spec] * len(before),
        spec,
        jax.ShapeDtypeStruct(theirs.shape, F32),
        (),
        12 * theirs.shape[0] * levels**2,
        8 * 2**20,
    )(flags, theirs, *before)


def finish_kernel(
    levels, upper_ref, theirs_ref, before_ref, prefix_ref, trial_ref, solved_ref, incoming
):
    cell = pl.program_id(0)
    states = before_ref.shape[0] - 16

    @pl.when(cell == 0)
    def _():
        incoming[...] = before_ref[levels:states]

        @pl.when(upper_ref[0] == 1)
        def _():
            incoming[...] += unscale(
                dot(theirs_ref[...], before_ref[:levels]), before_ref[states : states + 1]
            )

    solved_ref[:, cell, :] = trial_ref[0] + dot(incoming[...], prefix_ref[0])


def finish(levels, upper, theirs, before, prefix, trial):
    cells, lines, _ = trial.shape
    return call(
        functools.partial(finish_kernel, levels),
        (cells,),
        [
            pl.BlockSpec(memory_space=pltpu.SMEM),
            whole(theirs.shape),
            whole(before.shape),
            pl.BlockSpec((1, levels, levels), lambda i: (i, 0, 0)),
            pl.BlockSpec((1, lines, levels), lambda i: (i, 0, 0)),
        ],
        whole((lines, cells, levels)),
        jax.ShapeDtypeStruct((lines, cells, levels), F32),
        [pltpu.VMEM((lines, levels), F32)],
        12 * (cells + 1) * lines * levels**2,
        8 * 2**20,
    )(upper, theirs, before, prefix, trial)


def shards(sizes, forcing, blocks, upstream):
    span_count = sizes
    cells, levels, _ = blocks.shape
    share = forcing.shape[0]
    lines = share * span_count
    parts = forcing.reshape(share, span_count, cells, levels).swapaxes(0, 1)
    parts = lax.all_to_all(parts, "span", split_axis=0, concat_axis=0, tiled=True)
    local_forcing = parts.reshape(lines, cells, levels)
    prefix = prefix_maps(blocks, upstream)
    trial, total = trial_states(blocks, upstream, local_forcing, prefix)

    def partner(value, axis, mask):
        count = lax.axis_size(axis)
        return lax.ppermute(value, axis, [(i, i ^ mask) for i in range(count)])

    def flags_of(axis, bit):
        core = lax.axis_index("line") & CORE
        upper = jnp.where((lax.axis_index(axis) & bit) != 0, 1, 0)
        return jnp.stack([upper, core]).astype(jnp.int32)

    half, before = None, ()
    for axis, mask, bit, halved in ROUNDS[:-1]:
        flags = flags_of(axis, bit)
        if halved:
            here = partner(half, axis, mask)
            arrived = (here, partner(here, "line", CORE))
        else:
            arrived = (partner(total, axis, mask),)
        total, theirs, half = merge(levels, flags, total, *arrived)
        before = (extend(levels, flags, theirs, *before),)
    axis, mask, bit, _ = ROUNDS[-1]
    theirs = partner(total[levels : levels + lines], axis, mask)
    before = before[0]
    flags = flags_of(axis, bit)
    solved = finish(levels, flags, theirs, before, prefix, trial)
    parts = solved.reshape(span_count, share, cells, levels)
    parts = lax.all_to_all(parts, "span", split_axis=0, concat_axis=0, tiled=True)
    return parts.swapaxes(0, 1).reshape(share, span_count * cells, levels)


def solution(mesh):
    placed = (P("span", "line", None), P(("line", "span"), None, None), P(("line", "span"), None))
    sizes = mesh.shape["span"]
    return jax.shard_map(
        functools.partial(shards, sizes),
        mesh=mesh,
        in_specs=placed,
        out_specs=P("span", "line", None),
        check_vma=False,
    )
```

```python
import functools

import jax
import jax.numpy as jnp
from jax import lax
from jax.experimental import pallas as pl
from jax.experimental.pallas import tpu as pltpu
from jax.sharding import PartitionSpec as P

F32 = jnp.float32
BIG = 2.0**40
STEP = 2.0**48
PAD = 16
VMEM = pl.BlockSpec(memory_space=pltpu.VMEM)
HBM = pl.BlockSpec(memory_space=pltpu.HBM)
LARGE = 125 * 2**19
SMEM = pl.BlockSpec(memory_space=pltpu.SMEM)
CORE = 1
ROUNDS = (
    ("span", 1, 1, "apart"),
    ("span", 3, 2, "apart"),
    ("line", 1, 1, "together"),
    ("line", 2, 2, "halves"),
    ("line", 4, 4, "halves"),
    ("line", 14, 8, "halves"),
    ("line", 16, 16, "together"),
    ("line", 48, 32, "states"),
)


def dot(a, b):
    return jnp.dot(a, b, precision=lax.Precision.HIGHEST, preferred_element_type=F32)


def shape(*dims):
    return jax.ShapeDtypeStruct(dims, F32)


def call(kernel, in_specs, out_shape, flops, scratch=(), out_specs=None, vmem=8 * 2**20):
    return pl.pallas_call(
        kernel,
        in_specs=in_specs,
        out_specs=out_specs or jax.tree.map(lambda _: VMEM, out_shape),
        out_shape=out_shape,
        scratch_shapes=list(scratch),
        compiler_params=pltpu.CompilerParams(vmem_limit_bytes=vmem),
        cost_estimate=pl.CostEstimate(flops=flops, bytes_accessed=2**20, transcendentals=0),
    )


def settle(hat, count):
    large = jnp.max(jnp.abs(hat), keepdims=True) > BIG
    return hat * jnp.where(large, 1.0 / STEP, 1.0), count + jnp.where(large, 1.0, 0.0)


def unscale(value, count):
    for done in (0.0, 2.0, 4.0):
        left = count - done
        value = value * jnp.where(left > 1.5, STEP * STEP, jnp.where(left > 0.5, STEP, 1.0))
    return value


def put_map(hat, count, out_ref):
    levels = hat.shape[1]
    hat, count = settle(hat, count)
    out_ref[:levels] = hat
    out_ref[levels : levels + 8] = count
    out_ref[levels + 8 : levels + PAD] = jnp.zeros_like(count)


def join_maps(left_ref, right_ref, out_ref):
    levels = out_ref.shape[1]
    count = left_ref[levels : levels + 8] + right_ref[levels : levels + 8]
    put_map(dot(left_ref[:levels], right_ref[:levels]), count, out_ref)


def move_states(states, map_ref):
    levels = map_ref.shape[1]
    return unscale(dot(states, map_ref[:levels]), map_ref[levels : levels + 1])


def fetch(blocks_ref, held_ref, arrived):
    copies = [
        pltpu.make_async_copy(blocks_ref.at[cell], held_ref.at[cell], arrived.at[cell])
        for cell in range(held_ref.shape[0])
    ]
    for copy in copies:
        copy.start()
    return copies


def maps_kernel(upstream_ref, blocks_ref, prefix_ref, map_ref, held_ref, made_ref, arrived, left):
    cells, levels, _ = held_ref.shape
    copies = fetch(blocks_ref, held_ref, arrived)
    row = lax.broadcasted_iota(jnp.int32, (levels, levels), 0)
    column = lax.broadcasted_iota(jnp.int32, (levels, levels), 1)
    first = jnp.where(row == column, -upstream_ref[0:1, :], 0.0)
    first = jnp.sum(first, axis=1, keepdims=True)
    last = None
    sent = []
    for cell in range(cells):
        copies[cell].wait()
        if cell == 0:
            last = first * held_ref[0]
        else:
            last = dot(last * -upstream_ref[cell : cell + 1, :], held_ref[cell])
        made_ref[cell] = last
        sent.append(pltpu.make_async_copy(made_ref.at[cell], prefix_ref.at[cell], left.at[cell]))
        sent[-1].start()
    put_map(last, jnp.zeros((8, levels), F32), map_ref)
    for copy in sent:
        copy.wait()


def prefix_maps(blocks, upstream):
    cells, levels, _ = blocks.shape
    return call(
        maps_kernel,
        [VMEM, HBM],
        [shape(*blocks.shape), shape(levels + PAD, levels)],
        12 * cells * levels**3,
        [
            pltpu.VMEM(blocks.shape, F32),
            pltpu.VMEM(blocks.shape, F32),
            pltpu.SemaphoreType.DMA((cells,)),
            pltpu.SemaphoreType.DMA((cells,)),
        ],
        [HBM, VMEM],
        LARGE,
    )(upstream, blocks)


def states_kernel(
    upstream_ref, blocks_ref, forcing_ref, trial_ref, states_ref, held_ref, arrived
):
    copies = fetch(blocks_ref, held_ref, arrived)
    state = None
    for cell in range(held_ref.shape[0]):
        forced = forcing_ref[:, cell, :]
        if cell:
            forced = forced - upstream_ref[cell : cell + 1, :] * state
        copies[cell].wait()
        state = dot(forced, held_ref[cell])
        trial_ref[cell] = state
    states_ref[...] = state


def trial_states(blocks, upstream, forcing):
    cells, levels, _ = blocks.shape
    lines = forcing.shape[0]
    return call(
        states_kernel,
        [VMEM, HBM, VMEM],
        [shape(cells, lines, levels), shape(lines, levels)],
        12 * cells * lines * levels**2,
        [pltpu.VMEM(blocks.shape, F32), pltpu.SemaphoreType.DMA((cells,))],
        None,
        LARGE,
    )(upstream, blocks, forcing)


def later(code_ref, then, otherwise):
    upper = lax.rem(code_ref[0], 2)
    pl.when(upper == 1)(then)
    pl.when(upper == 0)(otherwise)


def merge_maps_kernel(code_ref, mine_ref, theirs_ref, total_ref):
    later(
        code_ref,
        lambda: join_maps(theirs_ref, mine_ref, total_ref),
        lambda: join_maps(mine_ref, theirs_ref, total_ref),
    )


def merge_maps(code, mine, theirs):
    levels = mine.shape[1]
    return call(merge_maps_kernel, [SMEM, VMEM, VMEM], shape(*mine.shape), 12 * levels**3)(
        code, mine, theirs
    )


def merge_states_kernel(code_ref, mine_ref, theirs_ref, my_map_ref, their_map_ref, out_ref):
    def then():
        out_ref[...] = move_states(theirs_ref[...], my_map_ref) + mine_ref[...]

    def otherwise():
        out_ref[...] = move_states(mine_ref[...], their_map_ref) + theirs_ref[...]

    later(code_ref, then, otherwise)


def merge_states(code, mine, theirs, my_map, their_map):
    lines, levels = mine.shape
    return call(
        merge_states_kernel, [SMEM] + [VMEM] * 4, shape(lines, levels), 12 * lines * levels**2
    )(code, mine, theirs, my_map, their_map)


def merge_kernel(levels, apart, halves, half, last, code_ref, *refs):
    refs = list(refs)
    mine_map = refs.pop(0)
    start = levels + PAD
    mine_states = refs.pop(0)[...] if apart else mine_map[start:]
    if apart:
        their_map, their_states = refs.pop(0), refs.pop(0)[...]
    elif halves:
        here_ref, there_ref = refs.pop(0), refs.pop(0)
    else:
        theirs = refs.pop(0)
        their_map, their_states = theirs, theirs[start:]
    total_ref = refs.pop(0)
    core = code_ref[0] // 2
    if halves:
        theirs = refs.pop(0)
        rows = here_ref.shape[0]

        @pl.when(core == 0)
        def _():
            theirs[:rows] = here_ref[...]
            theirs[rows:] = there_ref[...]

        @pl.when(core == 1)
        def _():
            theirs[:rows] = there_ref[...]
            theirs[rows:] = here_ref[...]

        their_map, their_states = theirs, theirs[start:]

    def then():
        states = move_states(their_states, mine_map) + mine_states
        if last:
            total_ref[...] = states
        else:
            join_maps(their_map, mine_map, total_ref)
            total_ref[start:] = states

    def otherwise():
        states = move_states(mine_states, their_map) + their_states
        if last:
            total_ref[...] = states
        else:
            join_maps(mine_map, their_map, total_ref)
            total_ref[start:] = states

    later(code_ref, then, otherwise)
    if half:
        half_ref = refs.pop(0)
        rows = half_ref.shape[0]

        @pl.when(core == 0)
        def _():
            half_ref[...] = total_ref[:rows]

        @pl.when(core == 1)
        def _():
            half_ref[...] = total_ref[rows:]


def merge(code, mine, theirs, apart, halves, half, last):
    levels = mine[0].shape[1]
    rows = levels + PAD + (mine[1].shape[0] if apart else mine[0].shape[0] - levels - PAD)
    out = [shape(rows - levels - PAD if last else rows, levels)]
    if halves:
        out.append(shape(rows, levels))
    if half:
        out.append(shape(rows // 2, levels))
    operands = (*mine, *theirs)
    return call(
        functools.partial(merge_kernel, levels, apart, halves, half, last),
        [SMEM] + [VMEM] * len(operands),
        out,
        12 * (rows - levels if last else rows) * levels**2,
    )(code, *operands)


def extend_kernel(first, apart, code_ref, *refs):
    refs = list(refs)
    their_map = refs.pop(0)
    levels = their_map.shape[1]
    start = levels + PAD
    their_states = refs.pop(0)[...] if apart else their_map[start:]
    if first:
        (ahead_ref,) = refs
    else:
        before_ref, ahead_ref = refs

    def then():
        if first:
            ahead_ref[:start] = their_map[:start]
            ahead_ref[start:] = their_states
        else:
            join_maps(their_map, before_ref, ahead_ref)
            ahead_ref[start:] = move_states(their_states, before_ref) + before_ref[start:]

    def otherwise():
        if first:
            row = lax.broadcasted_iota(jnp.int32, ahead_ref.shape, 0)
            column = lax.broadcasted_iota(jnp.int32, ahead_ref.shape, 1)
            ahead_ref[...] = jnp.where(row == column, 1.0, 0.0).astype(F32)
        else:
            ahead_ref[...] = before_ref[...]

    later(code_ref, then, otherwise)


def extend(code, theirs, before):
    levels = theirs[0].shape[1]
    apart = len(theirs) == 2
    rows = levels + PAD + (theirs[1].shape[0] if apart else theirs[0].shape[0] - levels - PAD)
    first = before is None
    operands = theirs if first else (*theirs, before)
    return call(
        functools.partial(extend_kernel, first, apart),
        [SMEM] + [VMEM] * len(operands),
        shape(rows, levels),
        12 * rows * levels**2,
    )(code, *operands)


def finish_kernel(
    code_ref, theirs_ref, before_ref, prefix_ref, trial_ref, solved_ref, held_ref, incoming, arrived
):
    copies = fetch(prefix_ref, held_ref, arrived)
    start = before_ref.shape[1] + PAD

    def then():
        incoming[...] = move_states(theirs_ref[...], before_ref) + before_ref[start:]

    def otherwise():
        incoming[...] = before_ref[start:]

    later(code_ref, then, otherwise)
    for cell, copy in enumerate(copies):
        copy.wait()
        solved_ref[:, cell, :] = trial_ref[cell] + dot(incoming[...], held_ref[cell])


def finish(code, theirs, before, prefix, trial):
    cells, lines, levels = trial.shape
    return call(
        finish_kernel,
        [SMEM, VMEM, VMEM, HBM, VMEM],
        shape(lines, cells, levels),
        12 * (cells + 1) * lines * levels**2,
        [
            pltpu.VMEM(prefix.shape, F32),
            pltpu.VMEM((lines, levels), F32),
            pltpu.SemaphoreType.DMA((cells,)),
        ],
        None,
        LARGE,
    )(code, theirs, before, prefix, trial)


def shards(span_count, forcing, blocks, upstream):
    cells, levels, _ = blocks.shape
    share = forcing.shape[0]
    lines = share * span_count
    parts = forcing.reshape(share, span_count, cells, levels).swapaxes(0, 1)
    parts = lax.all_to_all(parts, "span", split_axis=0, concat_axis=0, tiled=True)
    local_forcing = parts.reshape(lines, cells, levels)
    prefix, maps = prefix_maps(blocks, upstream)
    trial, states = trial_states(blocks, upstream, local_forcing)

    def partner(value, axis, mask):
        count = lax.axis_size(axis)
        return lax.ppermute(value, axis, [(i, i ^ mask) for i in range(count)])

    def code_of(axis, bit):
        upper = jnp.where((lax.axis_index(axis) & bit) != 0, 1, 0)
        core = jnp.where((lax.axis_index("line") & CORE) != 0, 2, 0)
        return (upper + core).astype(jnp.int32).reshape(1)

    total, half, before = None, None, None
    for turn, (axis, mask, bit, how) in enumerate(ROUNDS[:-1]):
        code = code_of(axis, bit)
        after = ROUNDS[turn + 1][3]
        apart, halves = how == "apart", how == "halves"
        if apart:
            theirs = (partner(maps, axis, mask), partner(states, axis, mask))
            mine = (maps, states)
        elif halves:
            here = partner(half, axis, mask)
            theirs = (here, partner(here, "line", CORE))
            mine = (total,)
        else:
            theirs = (partner(total, axis, mask),)
            mine = (total,)
        if before is not None:
            theirs, before = lax.optimization_barrier((theirs, before))
        if apart and after == "apart":
            states = merge_states(code, states, theirs[1], maps, theirs[0])
            maps = merge_maps(code, maps, theirs[0])
        else:
            got = merge(code, mine, theirs, apart, halves, after == "halves", after == "states")
            total = got[0]
            theirs = (got[1],) if halves else theirs
            half = got[-1]
        before = extend(code, theirs, before)
    axis, mask, bit, _ = ROUNDS[-1]
    theirs = partner(total, axis, mask)
    solved = finish(code_of(axis, bit), theirs, before, prefix, trial)
    parts = solved.reshape(span_count, share, cells, levels)
    parts = lax.all_to_all(parts, "span", split_axis=0, concat_axis=0, tiled=True)
    return parts.swapaxes(0, 1).reshape(share, span_count * cells, levels)


def solution(mesh):
    placed = (P("span", "line", None), P(("line", "span"), None, None), P(("line", "span"), None))
    return jax.shard_map(
        functools.partial(shards, mesh.shape["span"]),
        mesh=mesh,
        in_specs=placed,
        out_specs=P("span", "line", None),
        check_vma=False,
    )
```

```python
import functools

import jax
import jax.numpy as jnp
from jax import lax
from jax.experimental import pallas as pl
from jax.experimental.pallas import tpu as pltpu
from jax.sharding import PartitionSpec as P

F32 = jnp.float32
BIG = 2.0**40
STEP = 2.0**48
PAD = 16
VMEM = pl.BlockSpec(memory_space=pltpu.VMEM)
HBM = pl.BlockSpec(memory_space=pltpu.HBM)
STATES_VMEM = 8 * 2**20
FINISH_VMEM = 52 * 2**20
LARGE = 52 * 2**20
SMEM = pl.BlockSpec(memory_space=pltpu.SMEM)
CORE = 1
ROUNDS = (
    ("span", 1, 1, "apart"),
    ("span", 3, 2, "apart"),
    ("line", 1, 1, "together"),
    ("line", 2, 2, "halves"),
    ("line", 4, 4, "halves"),
    ("line", 14, 8, "halves"),
    ("line", 16, 16, "together"),
    ("line", 48, 32, "states"),
)


def dot(a, b):
    return jnp.dot(a, b, precision=lax.Precision.HIGHEST, preferred_element_type=F32)


def shape(*dims):
    return jax.ShapeDtypeStruct(dims, F32)


def call(kernel, in_specs, out_shape, flops, scratch=(), out_specs=None, vmem=8 * 2**20):
    return pl.pallas_call(
        kernel,
        in_specs=in_specs,
        out_specs=out_specs or jax.tree.map(lambda _: VMEM, out_shape),
        out_shape=out_shape,
        scratch_shapes=list(scratch),
        compiler_params=pltpu.CompilerParams(vmem_limit_bytes=vmem),
        cost_estimate=pl.CostEstimate(flops=flops, bytes_accessed=2**20, transcendentals=0),
    )


def settle(hat, count):
    large = jnp.max(jnp.abs(hat), keepdims=True) > BIG
    return hat * jnp.where(large, 1.0 / STEP, 1.0), count + jnp.where(large, 1.0, 0.0)


def unscale(value, count):
    for done in (0.0, 2.0, 4.0):
        left = count - done
        value = value * jnp.where(left > 1.5, STEP * STEP, jnp.where(left > 0.5, STEP, 1.0))
    return value


def put_map(hat, count, out_ref):
    levels = hat.shape[1]
    hat, count = settle(hat, count)
    out_ref[:levels] = hat
    out_ref[levels : levels + 8] = count
    out_ref[levels + 8 : levels + PAD] = jnp.zeros_like(count)


def join_maps(left_ref, right_ref, out_ref):
    levels = out_ref.shape[1]
    count = left_ref[levels : levels + 8] + right_ref[levels : levels + 8]
    put_map(dot(left_ref[:levels], right_ref[:levels]), count, out_ref)


def move_states(states, map_ref):
    levels = map_ref.shape[1]
    return unscale(dot(states, map_ref[:levels]), map_ref[levels : levels + 1])


def block_copy(blocks_ref, held_ref, arrived, cell):
    return pltpu.make_async_copy(blocks_ref.at[cell], held_ref.at[cell], arrived.at[cell])


def fetch(blocks_ref, held_ref, arrived):
    @pl.loop(0, held_ref.shape[0])
    def _(cell):
        block_copy(blocks_ref, held_ref, arrived, cell).start()


def maps_kernel(
    upstream_ref, blocks_ref, prefix_ref, map_ref, held_ref, made_ref, last_ref, arrived, left
):
    cells, levels, _ = held_ref.shape
    fetch(blocks_ref, held_ref, arrived)
    row = lax.broadcasted_iota(jnp.int32, (levels, levels), 0)
    column = lax.broadcasted_iota(jnp.int32, (levels, levels), 1)
    last_ref[...] = jnp.where(row == column, 1.0, 0.0).astype(F32)

    @pl.loop(0, cells)
    def _(cell):
        scaled = last_ref[...] * -upstream_ref[pl.ds(cell, 1), :]
        block_copy(blocks_ref, held_ref, arrived, cell).wait()
        product = dot(scaled, held_ref[cell])
        last_ref[...] = product
        made_ref[cell] = product
        block_copy(made_ref, prefix_ref, left, cell).start()

    put_map(last_ref[...], jnp.zeros((8, levels), F32), map_ref)

    @pl.loop(0, cells)
    def _(cell):
        block_copy(made_ref, prefix_ref, left, cell).wait()


def prefix_maps(blocks, upstream):
    cells, levels, _ = blocks.shape
    return call(
        maps_kernel,
        [VMEM, HBM],
        [shape(*blocks.shape), shape(levels + PAD, levels)],
        12 * cells * levels**3,
        [
            pltpu.VMEM(blocks.shape, F32),
            pltpu.VMEM(blocks.shape, F32),
            pltpu.VMEM((levels, levels), F32),
            pltpu.SemaphoreType.DMA((cells,)),
            pltpu.SemaphoreType.DMA((cells,)),
        ],
        [HBM, VMEM],
        LARGE,
    )(upstream, blocks)


def states_kernel(
    upstream_ref, blocks_ref, forcing_ref, trial_ref, states_ref, held_ref, arrived
):
    fetch(blocks_ref, held_ref, arrived)
    states_ref[...] = jnp.zeros_like(states_ref)

    @pl.loop(0, held_ref.shape[0])
    def _(cell):
        forced = forcing_ref[:, cell, :] - upstream_ref[pl.ds(cell, 1), :] * states_ref[...]
        block_copy(blocks_ref, held_ref, arrived, cell).wait()
        state = dot(forced, held_ref[cell])
        states_ref[...] = state
        trial_ref[cell] = state


def trial_states(blocks, upstream, forcing):
    cells, levels, _ = blocks.shape
    lines = forcing.shape[0]
    return call(
        states_kernel,
        [VMEM, HBM, VMEM],
        [shape(cells, lines, levels), shape(lines, levels)],
        12 * cells * lines * levels**2,
        [pltpu.VMEM(blocks.shape, F32), pltpu.SemaphoreType.DMA((cells,))],
        None,
        STATES_VMEM,
    )(upstream, blocks, forcing)


def later(code_ref, then, otherwise):
    upper = lax.rem(code_ref[0], 2)
    pl.when(upper == 1)(then)
    pl.when(upper == 0)(otherwise)


def merge_maps_kernel(code_ref, mine_ref, theirs_ref, total_ref):
    later(
        code_ref,
        lambda: join_maps(theirs_ref, mine_ref, total_ref),
        lambda: join_maps(mine_ref, theirs_ref, total_ref),
    )


def merge_maps(code, mine, theirs):
    levels = mine.shape[1]
    return call(merge_maps_kernel, [SMEM, VMEM, VMEM], shape(*mine.shape), 12 * levels**3)(
        code, mine, theirs
    )


def merge_states_kernel(code_ref, mine_ref, theirs_ref, my_map_ref, their_map_ref, out_ref):
    def then():
        out_ref[...] = move_states(theirs_ref[...], my_map_ref) + mine_ref[...]

    def otherwise():
        out_ref[...] = move_states(mine_ref[...], their_map_ref) + theirs_ref[...]

    later(code_ref, then, otherwise)


def merge_states(code, mine, theirs, my_map, their_map):
    lines, levels = mine.shape
    return call(
        merge_states_kernel, [SMEM] + [VMEM] * 4, shape(lines, levels), 12 * lines * levels**2
    )(code, mine, theirs, my_map, their_map)


def merge_kernel(levels, apart, halves, half, last, code_ref, *refs):
    refs = list(refs)
    mine_map = refs.pop(0)
    start = levels + PAD
    mine_states = refs.pop(0)[...] if apart else mine_map[start:]
    if apart:
        their_map, their_states = refs.pop(0), refs.pop(0)[...]
    elif halves:
        here_ref, there_ref = refs.pop(0), refs.pop(0)
    else:
        theirs = refs.pop(0)
        their_map, their_states = theirs, theirs[start:]
    total_ref = refs.pop(0)
    core = code_ref[0] // 2
    if halves:
        theirs = refs.pop(0)
        rows = here_ref.shape[0]

        @pl.when(core == 0)
        def _():
            theirs[:rows] = here_ref[...]
            theirs[rows:] = there_ref[...]

        @pl.when(core == 1)
        def _():
            theirs[:rows] = there_ref[...]
            theirs[rows:] = here_ref[...]

        their_map, their_states = theirs, theirs[start:]

    def then():
        states = move_states(their_states, mine_map) + mine_states
        if last:
            total_ref[...] = states
        else:
            join_maps(their_map, mine_map, total_ref)
            total_ref[start:] = states

    def otherwise():
        states = move_states(mine_states, their_map) + their_states
        if last:
            total_ref[...] = states
        else:
            join_maps(mine_map, their_map, total_ref)
            total_ref[start:] = states

    later(code_ref, then, otherwise)
    if half:
        half_ref = refs.pop(0)
        rows = half_ref.shape[0]

        @pl.when(core == 0)
        def _():
            half_ref[...] = total_ref[:rows]

        @pl.when(core == 1)
        def _():
            half_ref[...] = total_ref[rows:]


def merge(code, mine, theirs, apart, halves, half, last):
    levels = mine[0].shape[1]
    rows = levels + PAD + (mine[1].shape[0] if apart else mine[0].shape[0] - levels - PAD)
    out = [shape(rows - levels - PAD if last else rows, levels)]
    if halves:
        out.append(shape(rows, levels))
    if half:
        out.append(shape(rows // 2, levels))
    operands = (*mine, *theirs)
    return call(
        functools.partial(merge_kernel, levels, apart, halves, half, last),
        [SMEM] + [VMEM] * len(operands),
        out,
        12 * (rows - levels if last else rows) * levels**2,
    )(code, *operands)


def extend_kernel(first, apart, code_ref, *refs):
    refs = list(refs)
    their_map = refs.pop(0)
    levels = their_map.shape[1]
    start = levels + PAD
    their_states = refs.pop(0)[...] if apart else their_map[start:]
    if first:
        (ahead_ref,) = refs
    else:
        before_ref, ahead_ref = refs

    def then():
        if first:
            ahead_ref[:start] = their_map[:start]
            ahead_ref[start:] = their_states
        else:
            join_maps(their_map, before_ref, ahead_ref)
            ahead_ref[start:] = move_states(their_states, before_ref) + before_ref[start:]

    def otherwise():
        if first:
            row = lax.broadcasted_iota(jnp.int32, ahead_ref.shape, 0)
            column = lax.broadcasted_iota(jnp.int32, ahead_ref.shape, 1)
            ahead_ref[...] = jnp.where(row == column, 1.0, 0.0).astype(F32)
        else:
            ahead_ref[...] = before_ref[...]

    later(code_ref, then, otherwise)


def extend(code, theirs, before):
    levels = theirs[0].shape[1]
    apart = len(theirs) == 2
    rows = levels + PAD + (theirs[1].shape[0] if apart else theirs[0].shape[0] - levels - PAD)
    first = before is None
    operands = theirs if first else (*theirs, before)
    return call(
        functools.partial(extend_kernel, first, apart),
        [SMEM] + [VMEM] * len(operands),
        shape(rows, levels),
        12 * rows * levels**2,
    )(code, *operands)


def finish_kernel(
    code_ref, theirs_ref, before_ref, prefix_ref, trial_ref, solved_ref, held_ref, incoming, arrived
):
    fetch(prefix_ref, held_ref, arrived)
    start = before_ref.shape[1] + PAD

    def then():
        incoming[...] = move_states(theirs_ref[...], before_ref) + before_ref[start:]

    def otherwise():
        incoming[...] = before_ref[start:]

    later(code_ref, then, otherwise)

    @pl.loop(0, held_ref.shape[0])
    def _(cell):
        block_copy(prefix_ref, held_ref, arrived, cell).wait()
        solved_ref[:, cell, :] = trial_ref[cell] + dot(incoming[...], held_ref[cell])


def finish(code, theirs, before, prefix, trial):
    cells, lines, levels = trial.shape
    return call(
        finish_kernel,
        [SMEM, VMEM, VMEM, HBM, VMEM],
        shape(lines, cells, levels),
        12 * (cells + 1) * lines * levels**2,
        [
            pltpu.VMEM(prefix.shape, F32),
            pltpu.VMEM((lines, levels), F32),
            pltpu.SemaphoreType.DMA((cells,)),
        ],
        None,
        FINISH_VMEM,
    )(code, theirs, before, prefix, trial)


def shards(span_count, forcing, blocks, upstream):
    cells, levels, _ = blocks.shape
    share = forcing.shape[0]
    lines = share * span_count
    parts = forcing.reshape(share, span_count, cells, levels).swapaxes(0, 1)
    parts = lax.all_to_all(parts, "span", split_axis=0, concat_axis=0, tiled=True)
    local_forcing = parts.reshape(lines, cells, levels)
    prefix, maps = prefix_maps(blocks, upstream)
    trial, states = trial_states(blocks, upstream, local_forcing)

    def partner(value, axis, mask):
        count = lax.axis_size(axis)
        return lax.ppermute(value, axis, [(i, i ^ mask) for i in range(count)])

    def code_of(axis, bit):
        upper = jnp.where((lax.axis_index(axis) & bit) != 0, 1, 0)
        core = jnp.where((lax.axis_index("line") & CORE) != 0, 2, 0)
        return (upper + core).astype(jnp.int32).reshape(1)

    total, half, before = None, None, None
    for turn, (axis, mask, bit, how) in enumerate(ROUNDS[:-1]):
        code = code_of(axis, bit)
        after = ROUNDS[turn + 1][3]
        apart, halves = how == "apart", how == "halves"
        if apart:
            theirs = (partner(maps, axis, mask), partner(states, axis, mask))
            mine = (maps, states)
        elif halves:
            here = partner(half, axis, mask)
            theirs = (here, partner(here, "line", CORE))
            mine = (total,)
        else:
            theirs = (partner(total, axis, mask),)
            mine = (total,)
        if before is not None:
            theirs, before = lax.optimization_barrier((theirs, before))
        if apart and after == "apart":
            states = merge_states(code, states, theirs[1], maps, theirs[0])
            maps = merge_maps(code, maps, theirs[0])
        else:
            got = merge(code, mine, theirs, apart, halves, after == "halves", after == "states")
            total = got[0]
            theirs = (got[1],) if halves else theirs
            half = got[-1]
        before = extend(code, theirs, before)
    axis, mask, bit, _ = ROUNDS[-1]
    theirs = partner(total, axis, mask)
    solved = finish(code_of(axis, bit), theirs, before, prefix, trial)
    parts = solved.reshape(span_count, share, cells, levels)
    parts = lax.all_to_all(parts, "span", split_axis=0, concat_axis=0, tiled=True)
    return parts.swapaxes(0, 1).reshape(share, span_count * cells, levels)


def solution(mesh):
    placed = (P("span", "line", None), P(("line", "span"), None, None), P(("line", "span"), None))
    return jax.shard_map(
        functools.partial(shards, mesh.shape["span"]),
        mesh=mesh,
        in_specs=placed,
        out_specs=P("span", "line", None),
        check_vma=False,
    )
```

```python
import functools

import jax
import jax.numpy as jnp
from jax import lax
from jax.experimental import pallas as pl
from jax.experimental.pallas import tpu as pltpu
from jax.sharding import PartitionSpec as P

F32 = jnp.float32
BIG = 2.0**40
STEP = 2.0**48
PAD = 16
VMEM = pl.BlockSpec(memory_space=pltpu.VMEM)
HBM = pl.BlockSpec(memory_space=pltpu.HBM)
LARGE = 52 * 2**20
SMEM = pl.BlockSpec(memory_space=pltpu.SMEM)
CORE = 1
ROUNDS = (
    ("span", 1, 1, False, True),
    ("span", 3, 2, False, False),
    ("line", 1, 1, False, False),
    ("line", 2, 2, True, False),
    ("line", 4, 4, True, False),
    ("line", 14, 8, True, False),
)
PLANE = 16


def dot(a, b):
    return jnp.dot(a, b, precision=lax.Precision.HIGHEST, preferred_element_type=F32)


def shape(*dims):
    return jax.ShapeDtypeStruct(dims, F32)


def call(kernel, in_specs, out_shape, flops, scratch=(), out_specs=None, vmem=8 * 2**20):
    return pl.pallas_call(
        kernel,
        in_specs=in_specs,
        out_specs=out_specs or jax.tree.map(lambda _: VMEM, out_shape),
        out_shape=out_shape,
        scratch_shapes=list(scratch),
        compiler_params=pltpu.CompilerParams(vmem_limit_bytes=vmem),
        cost_estimate=pl.CostEstimate(flops=flops, bytes_accessed=2**20, transcendentals=0),
    )


def settle(hat, count):
    large = jnp.max(jnp.abs(hat), keepdims=True) > BIG
    return hat * jnp.where(large, 1.0 / STEP, 1.0), count + jnp.where(large, 1.0, 0.0)


def unscale(value, count):
    for done in (0.0, 2.0, 4.0):
        left = count - done
        value = value * jnp.where(left > 1.5, STEP * STEP, jnp.where(left > 0.5, STEP, 1.0))
    return value


def put_map(hat, count, out_ref):
    levels = hat.shape[1]
    hat, count = settle(hat, count)
    out_ref[:levels] = hat
    out_ref[levels : levels + 8] = count
    out_ref[levels + 8 : levels + PAD] = jnp.zeros_like(count)


def join_maps(left_ref, right_ref, out_ref):
    levels = out_ref.shape[1]
    count = left_ref[levels : levels + 8] + right_ref[levels : levels + 8]
    put_map(dot(left_ref[:levels], right_ref[:levels]), count, out_ref)


def move_states(states, map_ref):
    levels = map_ref.shape[1]
    return unscale(dot(states, map_ref[:levels]), map_ref[levels : levels + 1])


def block_copy(blocks_ref, held_ref, arrived, cell):
    return pltpu.make_async_copy(blocks_ref.at[cell], held_ref.at[cell], arrived.at[cell])


def fetch(blocks_ref, held_ref, arrived):
    @pl.loop(0, held_ref.shape[0])
    def _(cell):
        block_copy(blocks_ref, held_ref, arrived, cell).start()


def maps_kernel(
    upstream_ref, blocks_ref, prefix_ref, map_ref, held_ref, made_ref, last_ref, arrived, left
):
    cells, levels, _ = held_ref.shape
    fetch(blocks_ref, held_ref, arrived)
    row = lax.broadcasted_iota(jnp.int32, (levels, levels), 0)
    column = lax.broadcasted_iota(jnp.int32, (levels, levels), 1)
    last_ref[...] = jnp.where(row == column, 1.0, 0.0).astype(F32)

    @pl.loop(0, cells)
    def _(cell):
        scaled = last_ref[...] * -upstream_ref[pl.ds(cell, 1), :]
        block_copy(blocks_ref, held_ref, arrived, cell).wait()
        product = dot(scaled, held_ref[cell])
        last_ref[...] = product
        made_ref[cell] = product
        block_copy(made_ref, prefix_ref, left, cell).start()

    put_map(last_ref[...], jnp.zeros((8, levels), F32), map_ref)

    @pl.loop(0, cells)
    def _(cell):
        block_copy(made_ref, prefix_ref, left, cell).wait()


def prefix_maps(blocks, upstream):
    cells, levels, _ = blocks.shape
    return call(
        maps_kernel,
        [VMEM, HBM],
        [shape(*blocks.shape), shape(levels + PAD, levels)],
        12 * cells * levels**3,
        [
            pltpu.VMEM(blocks.shape, F32),
            pltpu.VMEM(blocks.shape, F32),
            pltpu.VMEM((levels, levels), F32),
            pltpu.SemaphoreType.DMA((cells,)),
            pltpu.SemaphoreType.DMA((cells,)),
        ],
        [HBM, VMEM],
        LARGE,
    )(upstream, blocks)


def states_kernel(upstream_ref, blocks_ref, forcing_ref, trial_ref, states_ref):
    states_ref[...] = jnp.zeros_like(states_ref)

    @pl.loop(0, blocks_ref.shape[0])
    def _(cell):
        forced = forcing_ref[:, cell, :] - upstream_ref[pl.ds(cell, 1), :] * states_ref[...]
        state = dot(forced, blocks_ref[cell])
        states_ref[...] = state
        trial_ref[cell] = state


def trial_states(blocks, upstream, forcing):
    cells, levels, _ = blocks.shape
    lines = forcing.shape[0]
    return call(
        states_kernel,
        [VMEM] * 3,
        [shape(cells, lines, levels), shape(lines, levels)],
        12 * cells * lines * levels**2,
    )(upstream, blocks, forcing)


def later(code_ref, then, otherwise):
    upper = lax.rem(code_ref[0], 2)
    pl.when(upper == 1)(then)
    pl.when(upper == 0)(otherwise)


def merge_states_kernel(code_ref, mine_ref, theirs_ref, my_map_ref, their_map_ref, out_ref):
    def then():
        out_ref[...] = move_states(theirs_ref[...], my_map_ref) + mine_ref[...]

    def otherwise():
        out_ref[...] = move_states(mine_ref[...], their_map_ref) + theirs_ref[...]

    later(code_ref, then, otherwise)


def merge_states(code, mine, theirs, my_map, their_map):
    lines, levels = mine.shape
    return call(
        merge_states_kernel, [SMEM] + [VMEM] * 4, shape(lines, levels), 12 * lines * levels**2
    )(code, mine, theirs, my_map, their_map)


def merge_kernel(start, kind, apart, halves, half, code_ref, *refs):
    refs = list(refs)
    mine_map = refs.pop(0)
    if apart and kind != "maps":
        mine_states = refs.pop(0)
    else:
        mine_states = None if kind == "maps" else mine_map.at[start:]
    here = refs.pop(0)
    there = refs.pop(0) if halves else None
    their_states = refs.pop(0) if apart and kind != "maps" else None
    out = refs.pop(0)
    core = code_ref[0] // 2
    their_map = here
    if halves:
        their_map = refs.pop(0)
        rows = here.shape[0]

        @pl.when(core == 0)
        def _():
            their_map[:rows] = here[...]
            their_map[rows:] = there[...]

        @pl.when(core == 1)
        def _():
            their_map[:rows] = there[...]
            their_map[rows:] = here[...]

    if their_states is None and kind != "maps":
        their_states = their_map.at[start:]

    def joined(left_map, left_states, right_map, right_states):
        if kind != "states":
            join_maps(left_map, right_map, out)
        if kind == "maps":
            return
        states = move_states(left_states[...], right_map) + right_states[...]
        if kind == "both":
            out[start:] = states
        else:
            out[...] = states

    later(
        code_ref,
        lambda: joined(their_map, their_states, mine_map, mine_states),
        lambda: joined(mine_map, mine_states, their_map, their_states),
    )
    if half:
        half_ref = refs.pop(0)
        rows = half_ref.shape[0]

        @pl.when(core == 0)
        def _():
            half_ref[...] = out[:rows]

        @pl.when(core == 1)
        def _():
            half_ref[...] = out[rows:]


def merge(code, mine, theirs, kind, lines, apart, halves, half):
    levels = mine[0].shape[1]
    start = levels + PAD
    rows = {"maps": start, "both": start + lines, "states": lines}[kind]
    out = [shape(rows, levels)]
    if halves:
        out.append(shape(2 * theirs[0].shape[0], levels))
    if half:
        out.append(shape(rows // 2, levels))
    operands = (*mine, *theirs)
    got = call(
        functools.partial(merge_kernel, start, kind, apart, halves, half),
        [SMEM] + [VMEM] * len(operands),
        out,
        12 * rows * levels**2,
    )(code, *operands)
    return got[0], got[1] if halves else theirs[0], got[-1]


def extend_kernel(first, apart, code_ref, *refs):
    refs = list(refs)
    their_map = refs.pop(0)
    levels = their_map.shape[1]
    start = levels + PAD
    their_states = refs.pop(0)[...] if apart else their_map[start:]
    if first:
        (ahead_ref,) = refs
    else:
        before_ref, ahead_ref = refs

    def then():
        if first:
            ahead_ref[:start] = their_map[:start]
            ahead_ref[start:] = their_states
        else:
            join_maps(their_map, before_ref, ahead_ref)
            ahead_ref[start:] = move_states(their_states, before_ref) + before_ref[start:]

    def otherwise():
        if first:
            row = lax.broadcasted_iota(jnp.int32, ahead_ref.shape, 0)
            column = lax.broadcasted_iota(jnp.int32, ahead_ref.shape, 1)
            ahead_ref[...] = jnp.where(row == column, 1.0, 0.0).astype(F32)
        else:
            ahead_ref[...] = before_ref[...]

    later(code_ref, then, otherwise)


def extend(code, theirs, before):
    levels = theirs[0].shape[1]
    apart = len(theirs) == 2
    rows = levels + PAD + (theirs[1].shape[0] if apart else theirs[0].shape[0] - levels - PAD)
    first = before is None
    operands = theirs if first else (*theirs, before)
    return call(
        functools.partial(extend_kernel, first, apart),
        [SMEM] + [VMEM] * len(operands),
        shape(rows, levels),
        12 * rows * levels**2,
    )(code, *operands)


def enter_kernel(from_ref, map_ref, own_ref, out_ref):
    out_ref[...] = move_states(from_ref[...], map_ref) + own_ref[...]


def enter(states, total, own):
    lines, levels = own.shape
    return call(enter_kernel, [VMEM] * 3, shape(lines, levels), 12 * lines * levels**2)(
        states, total, own
    )


def settle_planes_kernel(code_ref, beside_ref, from_ref, before_ref, ahead_ref):
    start = before_ref.shape[1] + PAD

    def then():
        join_maps(beside_ref, before_ref, ahead_ref)
        ahead_ref[start:] = move_states(beside_ref[start:], before_ref) + before_ref[start:]

    def otherwise():
        ahead_ref[:start] = before_ref[:start]
        ahead_ref[start:] = move_states(from_ref[...], before_ref) + before_ref[start:]

    later(code_ref, then, otherwise)


def settle_planes(code, beside, from_first, before):
    rows, levels = before.shape
    return call(
        settle_planes_kernel, [SMEM] + [VMEM] * 3, shape(rows, levels), 12 * rows * levels**2
    )(code, beside, from_first, before)


def finish_kernel(one_ref, two_ref, before_ref, prefix_ref, trial_ref, solved_ref, incoming):
    start = before_ref.shape[1] + PAD
    entering = one_ref[...] + two_ref[...]
    incoming[...] = move_states(entering, before_ref) + before_ref[start:]

    @pl.loop(0, prefix_ref.shape[0])
    def _(cell):
        solved_ref[:, cell, :] = trial_ref[cell] + dot(incoming[...], prefix_ref[cell])


def finish(entering, before, prefix, trial):
    cells, lines, levels = trial.shape
    return call(
        finish_kernel,
        [VMEM] * 5,
        shape(lines, cells, levels),
        12 * (cells + 1) * lines * levels**2,
        [pltpu.VMEM((lines, levels), F32)],
    )(*entering, before, prefix, trial)


def shards(span_count, forcing, blocks, upstream):
    cells, levels, _ = blocks.shape
    share = forcing.shape[0]
    lines = share * span_count
    parts = forcing.reshape(share, span_count, cells, levels).swapaxes(0, 1)
    parts = lax.all_to_all(parts, "span", split_axis=0, concat_axis=0, tiled=True)
    local_forcing = parts.reshape(lines, cells, levels)
    prefix, maps = prefix_maps(blocks, upstream)
    local_forcing, maps = lax.optimization_barrier((local_forcing, maps))
    trial, states = trial_states(blocks, upstream, local_forcing)

    def partner(value, axis, mask):
        count = lax.axis_size(axis)
        return lax.ppermute(value, axis, [(i, i ^ mask) for i in range(count)])

    def code_of(axis, bit):
        upper = jnp.where((lax.axis_index(axis) & bit) != 0, 1, 0)
        core = jnp.where((lax.axis_index("line") & CORE) != 0, 2, 0)
        return (upper + core).astype(jnp.int32).reshape(1)

    total, half, before = None, None, None
    for turn, (axis, mask, bit, halves, apart) in enumerate(ROUNDS):
        code = code_of(axis, bit)
        last = turn == len(ROUNDS) - 1
        next_halves = not last and ROUNDS[turn + 1][3]
        if halves:
            here = partner(half, axis, mask)
            theirs = (here, partner(here, "line", CORE))
        else:
            theirs = (partner(maps if apart else total, axis, mask),)
        if before is not None:
            theirs, before = lax.optimization_barrier((theirs, before))
        mine = (total,)
        if apart:
            their_states = partner(states, axis, mask)
            mine, theirs = (maps, states), (*theirs, their_states)
        if last:
            plane, whole, _ = merge(code, mine, theirs, "states", lines, apart, halves, False)
            total, _, _ = merge(code, mine, (whole,), "both", lines, False, False, False)
        else:
            total, whole, half = merge(code, mine, theirs, "both", lines, apart, halves, next_halves)
        before = extend(code, (whole, their_states) if apart else (whole,), before)

    def across(value, source, target):
        shift = (target - source) * PLANE
        pairs = [(i, i + shift) for i in range(source * PLANE, (source + 1) * PLANE)]
        return lax.ppermute(value, "line", pairs)

    from_first = across(plane, 0, 1)
    beside = across(total, 2, 3)
    from_first, before = lax.optimization_barrier((from_first, before))
    joined = enter(from_first, total, plane)
    entering = (across(joined, 1, 2), across(joined, 1, 3))
    in_last = jnp.where(lax.axis_index("line") >= 3 * PLANE, 1, 0).astype(jnp.int32).reshape(1)
    before = settle_planes(in_last, beside, from_first, before)
    solved = finish(entering, before, prefix, trial)
    parts = solved.reshape(span_count, share, cells, levels)
    parts = lax.all_to_all(parts, "span", split_axis=0, concat_axis=0, tiled=True)
    return parts.swapaxes(0, 1).reshape(share, span_count * cells, levels)


def solution(mesh):
    placed = (P("span", "line", None), P(("line", "span"), None, None), P(("line", "span"), None))
    return jax.shard_map(
        functools.partial(shards, mesh.shape["span"]),
        mesh=mesh,
        in_specs=placed,
        out_specs=P("span", "line", None),
        check_vma=False,
    )
```

```python
import functools

import jax
import jax.numpy as jnp
from jax import lax
from jax.experimental import pallas as pl
from jax.experimental.pallas import tpu as pltpu
from jax.sharding import PartitionSpec as P

F32 = jnp.float32
BIG = 2.0**40
STEP = 2.0**48
PAD = 16
VMEM = pl.BlockSpec(memory_space=pltpu.VMEM)
HBM = pl.BlockSpec(memory_space=pltpu.HBM)
LARGE = 52 * 2**20
SMEM = pl.BlockSpec(memory_space=pltpu.SMEM)
CORE = 1
ROUNDS = (
    ("span", 1, 1, False, True),
    ("span", 3, 2, False, False),
    ("line", 1, 1, False, False),
    ("line", 14, 8, True, False),
)
FOUR = (2, 4)
THIRD = 6
PLANE = 16


def dot(a, b):
    return jnp.dot(a, b, precision=lax.Precision.HIGHEST, preferred_element_type=F32)


def split(a):
    high = a.astype(jnp.bfloat16)
    return high, (a - high.astype(F32)).astype(jnp.bfloat16)


def dot3(a, b):
    product = functools.partial(jnp.dot, preferred_element_type=F32)
    (a_high, a_low), (b_high, b_low) = split(a), split(b)
    return product(a_high, b_high) + (product(a_high, b_low) + product(a_low, b_high))


def shape(*dims):
    return jax.ShapeDtypeStruct(dims, F32)


def call(kernel, in_specs, out_shape, flops, scratch=(), out_specs=None, vmem=8 * 2**20):
    return pl.pallas_call(
        kernel,
        in_specs=in_specs,
        out_specs=out_specs or jax.tree.map(lambda _: VMEM, out_shape),
        out_shape=out_shape,
        scratch_shapes=list(scratch),
        compiler_params=pltpu.CompilerParams(vmem_limit_bytes=vmem),
        cost_estimate=pl.CostEstimate(flops=flops, bytes_accessed=2**20, transcendentals=0),
    )


def settle(hat, count):
    large = jnp.max(jnp.abs(hat), keepdims=True) > BIG
    return hat * jnp.where(large, 1.0 / STEP, 1.0), count + jnp.where(large, 1.0, 0.0)


def unscale(value, count):
    for done in (0.0, 2.0, 4.0):
        left = count - done
        value = value * jnp.where(left > 1.5, STEP * STEP, jnp.where(left > 0.5, STEP, 1.0))
    return value


def put_map(hat, count, out_ref):
    levels = hat.shape[1]
    hat, count = settle(hat, count)
    out_ref[:levels] = hat
    out_ref[levels : levels + 8] = count
    out_ref[levels + 8 : levels + PAD] = jnp.zeros_like(count)


def join_maps(left_ref, right_ref, out_ref):
    levels = out_ref.shape[1]
    count = left_ref[levels : levels + 8] + right_ref[levels : levels + 8]
    put_map(dot(left_ref[:levels], right_ref[:levels]), count, out_ref)


def move_states(states, map_ref):
    levels = map_ref.shape[1]
    return unscale(dot(states, map_ref[:levels]), map_ref[levels : levels + 1])


def block_copy(blocks_ref, held_ref, arrived, cell):
    return pltpu.make_async_copy(blocks_ref.at[cell], held_ref.at[cell], arrived.at[cell])


def fetch(blocks_ref, held_ref, arrived):
    @pl.loop(0, held_ref.shape[0])
    def _(cell):
        block_copy(blocks_ref, held_ref, arrived, cell).start()


def maps_kernel(
    upstream_ref, blocks_ref, prefix_ref, map_ref, held_ref, made_ref, last_ref, arrived, left
):
    cells, levels, _ = held_ref.shape
    fetch(blocks_ref, held_ref, arrived)
    row = lax.broadcasted_iota(jnp.int32, (levels, levels), 0)
    column = lax.broadcasted_iota(jnp.int32, (levels, levels), 1)
    first = jnp.where(row == column, -upstream_ref[0:1, :], 0.0)
    first = jnp.sum(first, axis=1, keepdims=True)
    block_copy(blocks_ref, held_ref, arrived, 0).wait()
    first = first * held_ref[0]
    last_ref[...] = first
    made_ref[0] = first
    block_copy(made_ref, prefix_ref, left, 0).start()

    @pl.loop(1, cells)
    def _(cell):
        scaled = last_ref[...] * -upstream_ref[pl.ds(cell, 1), :]
        block_copy(blocks_ref, held_ref, arrived, cell).wait()
        product = dot(scaled, held_ref[cell])
        last_ref[...] = product
        made_ref[cell] = product
        block_copy(made_ref, prefix_ref, left, cell).start()

    put_map(last_ref[...], jnp.zeros((8, levels), F32), map_ref)

    @pl.loop(0, cells)
    def _(cell):
        block_copy(made_ref, prefix_ref, left, cell).wait()


def prefix_maps(blocks, upstream):
    cells, levels, _ = blocks.shape
    return call(
        maps_kernel,
        [VMEM, HBM],
        [shape(*blocks.shape), shape(levels + PAD, levels)],
        12 * cells * levels**3,
        [
            pltpu.VMEM(blocks.shape, F32),
            pltpu.VMEM(blocks.shape, F32),
            pltpu.VMEM((levels, levels), F32),
            pltpu.SemaphoreType.DMA((cells,)),
            pltpu.SemaphoreType.DMA((cells,)),
        ],
        [HBM, VMEM],
        LARGE,
    )(upstream, blocks)


def states_kernel(upstream_ref, blocks_ref, forcing_ref, trial_ref, states_ref):
    states_ref[...] = jnp.zeros_like(states_ref)

    @pl.loop(0, blocks_ref.shape[0])
    def _(cell):
        forced = forcing_ref[:, cell, :] - upstream_ref[pl.ds(cell, 1), :] * states_ref[...]
        state = dot(forced, blocks_ref[cell])
        states_ref[...] = state
        trial_ref[cell] = state


def trial_states(blocks, upstream, forcing):
    cells, levels, _ = blocks.shape
    lines = forcing.shape[0]
    return call(
        states_kernel,
        [VMEM] * 3,
        [shape(cells, lines, levels), shape(lines, levels)],
        12 * cells * lines * levels**2,
    )(upstream, blocks, forcing)


def later(code_ref, then, otherwise):
    upper = lax.rem(code_ref[0], 2)
    pl.when(upper == 1)(then)
    pl.when(upper == 0)(otherwise)


def merge_states_kernel(code_ref, mine_ref, theirs_ref, my_map_ref, their_map_ref, out_ref):
    def then():
        out_ref[...] = move_states(theirs_ref[...], my_map_ref) + mine_ref[...]

    def otherwise():
        out_ref[...] = move_states(mine_ref[...], their_map_ref) + theirs_ref[...]

    later(code_ref, then, otherwise)


def merge_states(code, mine, theirs, my_map, their_map):
    lines, levels = mine.shape
    return call(
        merge_states_kernel, [SMEM] + [VMEM] * 4, shape(lines, levels), 12 * lines * levels**2
    )(code, mine, theirs, my_map, their_map)


def merge_kernel(start, kind, apart, halves, half, code_ref, *refs):
    refs = list(refs)
    mine_map = refs.pop(0)
    if apart and kind != "maps":
        mine_states = refs.pop(0)
    else:
        mine_states = None if kind == "maps" else mine_map.at[start:]
    here = refs.pop(0)
    there = refs.pop(0) if halves else None
    their_states = refs.pop(0) if apart and kind != "maps" else None
    out = refs.pop(0)
    core = code_ref[0] // 2
    their_map = here
    if halves:
        their_map = refs.pop(0)
        rows = here.shape[0]

        @pl.when(core == 0)
        def _():
            their_map[:rows] = here[...]
            their_map[rows:] = there[...]

        @pl.when(core == 1)
        def _():
            their_map[:rows] = there[...]
            their_map[rows:] = here[...]

    if their_states is None and kind != "maps":
        their_states = their_map.at[start:]

    def joined(left_map, left_states, right_map, right_states):
        if kind != "states":
            join_maps(left_map, right_map, out)
        if kind == "maps":
            return
        states = move_states(left_states[...], right_map) + right_states[...]
        if kind == "both":
            out[start:] = states
        else:
            out[...] = states

    later(
        code_ref,
        lambda: joined(their_map, their_states, mine_map, mine_states),
        lambda: joined(mine_map, mine_states, their_map, their_states),
    )
    if half:
        half_ref = refs.pop(0)
        rows = half_ref.shape[0]

        @pl.when(core == 0)
        def _():
            half_ref[...] = out[:rows]

        @pl.when(core == 1)
        def _():
            half_ref[...] = out[rows:]


def merge(code, mine, theirs, kind, lines, apart, halves, half):
    levels = mine[0].shape[1]
    start = levels + PAD
    rows = {"maps": start, "both": start + lines, "states": lines}[kind]
    out = [shape(rows, levels)]
    if halves:
        out.append(shape(2 * theirs[0].shape[0], levels))
    if half:
        out.append(shape(rows // 2, levels))
    operands = (*mine, *theirs)
    got = call(
        functools.partial(merge_kernel, start, kind, apart, halves, half),
        [SMEM] + [VMEM] * len(operands),
        out,
        12 * rows * levels**2,
    )(code, *operands)
    return got[0], got[1] if halves else theirs[0], got[-1]


def join(left_ref, right_ref, out_ref):
    start = out_ref.shape[1] + PAD
    join_maps(left_ref, right_ref, out_ref)
    out_ref[start:] = move_states(left_ref[start:], right_ref) + right_ref[start:]


def four_kernel(
    code_ref, mine_ref, here_ref, there_ref, this_ref, that_ref,
    total_ref, beside_ref, front_ref, half_ref, four_ref, back_ref,
):
    core = lax.rem(code_ref[0], 2)
    place = code_ref[0] // 2
    rows = half_ref.shape[0]
    four_ref[place] = mine_ref[...]
    four_ref[place ^ (1 + core)] = here_ref[...]
    four_ref[place ^ (2 - core)] = there_ref[...]
    four_ref[place ^ 3, pl.ds(core * rows, rows)] = this_ref[...]
    four_ref[place ^ 3, pl.ds((1 - core) * rows, rows)] = that_ref[...]
    join(four_ref.at[0], four_ref.at[1], front_ref)
    join(four_ref.at[2], four_ref.at[3], back_ref)
    join(front_ref, back_ref, total_ref)
    half_ref[...] = total_ref[pl.ds(core * rows, rows)]
    beside_ref[...] = four_ref[place ^ 1]


def join_four(code, mine, here, there, this, that):
    rows, levels = mine.shape
    whole = shape(rows, levels)
    return call(
        four_kernel,
        [SMEM] + [VMEM] * 5,
        [whole, whole, whole, shape(rows // 2, levels)],
        36 * rows * levels**2,
        [pltpu.VMEM((4, rows, levels), F32), pltpu.VMEM((rows, levels), F32)],
    )(code, mine, here, there, this, that)


def extend_kernel(first, apart, code_ref, *refs):
    refs = list(refs)
    their_map = refs.pop(0)
    levels = their_map.shape[1]
    start = levels + PAD
    their_states = refs.pop(0)[...] if apart else their_map[start:]
    if first:
        (ahead_ref,) = refs
    else:
        before_ref, ahead_ref = refs

    def then():
        if first:
            ahead_ref[:start] = their_map[:start]
            ahead_ref[start:] = their_states
        else:
            join_maps(their_map, before_ref, ahead_ref)
            ahead_ref[start:] = move_states(their_states, before_ref) + before_ref[start:]

    def otherwise():
        if first:
            row = lax.broadcasted_iota(jnp.int32, ahead_ref.shape, 0)
            column = lax.broadcasted_iota(jnp.int32, ahead_ref.shape, 1)
            ahead_ref[...] = jnp.where(row == column, 1.0, 0.0).astype(F32)
        else:
            ahead_ref[...] = before_ref[...]

    later(code_ref, then, otherwise)


def extend(code, theirs, before):
    levels = theirs[0].shape[1]
    apart = len(theirs) == 2
    rows = levels + PAD + (theirs[1].shape[0] if apart else theirs[0].shape[0] - levels - PAD)
    first = before is None
    operands = theirs if first else (*theirs, before)
    return call(
        functools.partial(extend_kernel, first, apart),
        [SMEM] + [VMEM] * len(operands),
        shape(rows, levels),
        12 * rows * levels**2,
    )(code, *operands)


def enter_kernel(from_ref, map_ref, own_ref, out_ref):
    out_ref[...] = move_states(from_ref[...], map_ref) + own_ref[...]


def enter(states, total, own):
    lines, levels = own.shape
    return call(enter_kernel, [VMEM] * 3, shape(lines, levels), 12 * lines * levels**2)(
        states, total, own
    )


def settle_planes_kernel(code_ref, beside_ref, from_ref, before_ref, ahead_ref):
    start = before_ref.shape[1] + PAD

    def then():
        join_maps(beside_ref, before_ref, ahead_ref)
        ahead_ref[start:] = move_states(beside_ref[start:], before_ref) + before_ref[start:]

    def otherwise():
        ahead_ref[:start] = before_ref[:start]
        ahead_ref[start:] = move_states(from_ref[...], before_ref) + before_ref[start:]

    later(code_ref, then, otherwise)


def settle_planes(code, beside, from_first, before):
    rows, levels = before.shape
    return call(
        settle_planes_kernel, [SMEM] + [VMEM] * 3, shape(rows, levels), 12 * rows * levels**2
    )(code, beside, from_first, before)


def finish_kernel(
    one_ref, two_ref, before_ref, prefix_ref, trial_ref, solved_ref, held_ref, incoming, arrived
):
    fetch(prefix_ref, held_ref, arrived)
    start = before_ref.shape[1] + PAD
    entering = one_ref[...] + two_ref[...]
    incoming[...] = move_states(entering, before_ref) + before_ref[start:]

    @pl.loop(0, held_ref.shape[0])
    def _(cell):
        block_copy(prefix_ref, held_ref, arrived, cell).wait()
        solved_ref[:, cell, :] = trial_ref[cell] + dot3(incoming[...], held_ref[cell])


def finish(entering, before, prefix, trial):
    cells, lines, levels = trial.shape
    return call(
        finish_kernel,
        [VMEM, VMEM, VMEM, HBM, VMEM],
        shape(lines, cells, levels),
        12 * (cells + 1) * lines * levels**2,
        [
            pltpu.VMEM(prefix.shape, F32),
            pltpu.VMEM((lines, levels), F32),
            pltpu.SemaphoreType.DMA((cells,)),
        ],
        None,
        LARGE,
    )(*entering, before, prefix, trial)


def shards(span_count, forcing, blocks, upstream):
    cells, levels, _ = blocks.shape
    share = forcing.shape[0]
    lines = share * span_count
    parts = forcing.reshape(share, span_count, cells, levels).swapaxes(0, 1)
    parts = lax.all_to_all(parts, "span", split_axis=0, concat_axis=0, tiled=True)
    local_forcing = parts.reshape(lines, cells, levels)
    prefix, maps = prefix_maps(blocks, upstream)
    local_forcing, maps = lax.optimization_barrier((local_forcing, maps))
    trial, states = trial_states(blocks, upstream, local_forcing)

    def partner(value, axis, mask):
        count = lax.axis_size(axis)
        return lax.ppermute(value, axis, [(i, i ^ mask) for i in range(count)])

    def code_of(axis, bit):
        upper = jnp.where((lax.axis_index(axis) & bit) != 0, 1, 0)
        core = jnp.where((lax.axis_index("line") & CORE) != 0, 2, 0)
        return (upper + core).astype(jnp.int32).reshape(1)

    def along_four(total, half, before):
        device = lax.axis_index("line")
        pairs = [(i, i ^ FOUR[i & CORE]) for i in range(lax.axis_size("line"))]
        here, this = lax.ppermute(total, "line", pairs), partner(half, "line", THIRD)
        here, this, before = lax.optimization_barrier((here, this, before))
        there, that = partner(here, "line", CORE), partner(this, "line", CORE)
        code = (device & (CORE | THIRD)).astype(jnp.int32).reshape(1)
        total, beside, front, half = join_four(code, total, here, there, this, that)
        before = extend(code_of("line", FOUR[0]), (beside,), before)
        before = extend(code_of("line", FOUR[1]), (front,), before)
        return total, half, before

    total, half, before = None, None, None
    for turn, (axis, mask, bit, halves, apart) in enumerate(ROUNDS):
        code = code_of(axis, bit)
        last = turn == len(ROUNDS) - 1
        if halves:
            here = partner(half, axis, mask)
            here, before = lax.optimization_barrier((here, before))
            theirs = (here, partner(here, "line", CORE))
        else:
            theirs = (partner(maps if apart else total, axis, mask),)
            if before is not None:
                theirs, before = lax.optimization_barrier((theirs, before))
        mine = (total,)
        if apart:
            their_states = partner(states, axis, mask)
            mine, theirs = (maps, states), (*theirs, their_states)
        if last:
            plane, whole, _ = merge(code, mine, theirs, "states", lines, apart, halves, False)
            total, _, _ = merge(code, mine, (whole,), "both", lines, False, False, False)
        else:
            half_too = turn == len(ROUNDS) - 2
            total, whole, half = merge(code, mine, theirs, "both", lines, apart, halves, half_too)
        before = extend(code, (whole, their_states) if apart else (whole,), before)
        if turn == len(ROUNDS) - 2:
            total, half, before = along_four(total, half, before)

    def across(value, source, target):
        shift = (target - source) * PLANE
        pairs = [(i, i + shift) for i in range(source * PLANE, (source + 1) * PLANE)]
        return lax.ppermute(value, "line", pairs)

    from_first = across(plane, 0, 1)
    beside = across(total, 2, 3)
    from_first, before = lax.optimization_barrier((from_first, before))
    joined = enter(from_first, total, plane)
    two_on = across(joined, 1, 3)
    entering = (two_on, across(joined, 1, 2))
    in_last = jnp.where(lax.axis_index("line") >= 3 * PLANE, 1, 0).astype(jnp.int32).reshape(1)
    before = settle_planes(in_last, beside, from_first, before)
    solved = finish(entering, before, prefix, trial)
    parts = solved.reshape(span_count, share, cells, levels)
    parts = lax.all_to_all(parts, "span", split_axis=0, concat_axis=0, tiled=True)
    return parts.swapaxes(0, 1).reshape(share, span_count * cells, levels)


def solution(mesh):
    placed = (P("span", "line", None), P(("line", "span"), None, None), P(("line", "span"), None))
    return jax.shard_map(
        functools.partial(shards, mesh.shape["span"]),
        mesh=mesh,
        in_specs=placed,
        out_specs=P("span", "line", None),
        check_vma=False,
    )
```

```python
import functools

import jax
import jax.numpy as jnp
from jax import lax
from jax.experimental import pallas as pl
from jax.experimental.pallas import tpu as pltpu
from jax.sharding import PartitionSpec as P

F32 = jnp.float32
BIG = 2.0**40
STEP = 2.0**48
PAD = 16
VMEM = pl.BlockSpec(memory_space=pltpu.VMEM)
HBM = pl.BlockSpec(memory_space=pltpu.HBM)
LARGE = 52 * 2**20
SMEM = pl.BlockSpec(memory_space=pltpu.SMEM)
CORE = 1
ROUNDS = (
    ("span", 1, 1, False, True),
    ("span", 3, 2, False, False),
    ("line", 1, 1, False, False),
    ("line", 12, 8, True, False),
)
FOUR = (2, 4)
THIRD = 6
PLANE = 16


def dot(a, b):
    return jnp.dot(a, b, precision=lax.Precision.HIGHEST, preferred_element_type=F32)


def split(a):
    high = a.astype(jnp.bfloat16)
    return high, (a - high.astype(F32)).astype(jnp.bfloat16)


def dot3(a, b):
    product = functools.partial(jnp.dot, preferred_element_type=F32)
    (a_high, a_low), (b_high, b_low) = split(a), split(b)
    return product(a_high, b_high) + (product(a_high, b_low) + product(a_low, b_high))


def shape(*dims):
    return jax.ShapeDtypeStruct(dims, F32)


def call(kernel, in_specs, out_shape, flops, scratch=(), out_specs=None, vmem=8 * 2**20):
    return pl.pallas_call(
        kernel,
        in_specs=in_specs,
        out_specs=out_specs or jax.tree.map(lambda _: VMEM, out_shape),
        out_shape=out_shape,
        scratch_shapes=list(scratch),
        compiler_params=pltpu.CompilerParams(vmem_limit_bytes=vmem),
        cost_estimate=pl.CostEstimate(flops=flops, bytes_accessed=2**20, transcendentals=0),
    )


def settle(hat, count):
    large = jnp.max(jnp.abs(hat), keepdims=True) > BIG
    return hat * jnp.where(large, 1.0 / STEP, 1.0), count + jnp.where(large, 1.0, 0.0)


def unscale(value, count):
    for done in (0.0, 2.0, 4.0):
        left = count - done
        value = value * jnp.where(left > 1.5, STEP * STEP, jnp.where(left > 0.5, STEP, 1.0))
    return value


def put_map(hat, count, out_ref):
    levels = hat.shape[1]
    hat, count = settle(hat, count)
    out_ref[:levels] = hat
    out_ref[levels : levels + 8] = count
    out_ref[levels + 8 : levels + PAD] = jnp.zeros_like(count)


def join_maps(left_ref, right_ref, out_ref):
    levels = out_ref.shape[1]
    count = left_ref[levels : levels + 8] + right_ref[levels : levels + 8]
    put_map(dot(left_ref[:levels], right_ref[:levels]), count, out_ref)


def move_states(states, map_ref):
    levels = map_ref.shape[1]
    return unscale(dot(states, map_ref[:levels]), map_ref[levels : levels + 1])


def block_copy(blocks_ref, held_ref, arrived, cell):
    return pltpu.make_async_copy(blocks_ref.at[cell], held_ref.at[cell], arrived.at[cell])


def fetch(blocks_ref, held_ref, arrived):
    @pl.loop(0, held_ref.shape[0])
    def _(cell):
        block_copy(blocks_ref, held_ref, arrived, cell).start()


def maps_kernel(
    upstream_ref, blocks_ref, prefix_ref, map_ref, held_ref, made_ref, last_ref, arrived, left
):
    cells, levels, _ = held_ref.shape
    fetch(blocks_ref, held_ref, arrived)
    row = lax.broadcasted_iota(jnp.int32, (levels, levels), 0)
    column = lax.broadcasted_iota(jnp.int32, (levels, levels), 1)
    first = jnp.where(row == column, -upstream_ref[0:1, :], 0.0)
    first = jnp.sum(first, axis=1, keepdims=True)
    block_copy(blocks_ref, held_ref, arrived, 0).wait()
    first = first * held_ref[0]
    last_ref[...] = first
    made_ref[0] = first
    block_copy(made_ref, prefix_ref, left, 0).start()

    @pl.loop(1, cells)
    def _(cell):
        scaled = last_ref[...] * -upstream_ref[pl.ds(cell, 1), :]
        block_copy(blocks_ref, held_ref, arrived, cell).wait()
        product = dot(scaled, held_ref[cell])
        last_ref[...] = product
        made_ref[cell] = product
        block_copy(made_ref, prefix_ref, left, cell).start()

    put_map(last_ref[...], jnp.zeros((8, levels), F32), map_ref)

    @pl.loop(0, cells)
    def _(cell):
        block_copy(made_ref, prefix_ref, left, cell).wait()


def prefix_maps(blocks, upstream):
    cells, levels, _ = blocks.shape
    return call(
        maps_kernel,
        [VMEM, HBM],
        [shape(*blocks.shape), shape(levels + PAD, levels)],
        12 * cells * levels**3,
        [
            pltpu.VMEM(blocks.shape, F32),
            pltpu.VMEM(blocks.shape, F32),
            pltpu.VMEM((levels, levels), F32),
            pltpu.SemaphoreType.DMA((cells,)),
            pltpu.SemaphoreType.DMA((cells,)),
        ],
        [HBM, VMEM],
        LARGE,
    )(upstream, blocks)


def states_kernel(upstream_ref, blocks_ref, forcing_ref, trial_ref, states_ref):
    states_ref[...] = jnp.zeros_like(states_ref)

    @pl.loop(0, blocks_ref.shape[0])
    def _(cell):
        forced = forcing_ref[:, cell, :] - upstream_ref[pl.ds(cell, 1), :] * states_ref[...]
        state = dot(forced, blocks_ref[cell])
        states_ref[...] = state
        trial_ref[cell] = state


def trial_states(blocks, upstream, forcing):
    cells, levels, _ = blocks.shape
    lines = forcing.shape[0]
    return call(
        states_kernel,
        [VMEM] * 3,
        [shape(cells, lines, levels), shape(lines, levels)],
        12 * cells * lines * levels**2,
    )(upstream, blocks, forcing)


def later(code_ref, then, otherwise):
    upper = lax.rem(code_ref[0], 2)
    pl.when(upper == 1)(then)
    pl.when(upper == 0)(otherwise)


def merge_states_kernel(code_ref, mine_ref, theirs_ref, my_map_ref, their_map_ref, out_ref):
    def then():
        out_ref[...] = move_states(theirs_ref[...], my_map_ref) + mine_ref[...]

    def otherwise():
        out_ref[...] = move_states(mine_ref[...], their_map_ref) + theirs_ref[...]

    later(code_ref, then, otherwise)


def merge_states(code, mine, theirs, my_map, their_map):
    lines, levels = mine.shape
    return call(
        merge_states_kernel, [SMEM] + [VMEM] * 4, shape(lines, levels), 12 * lines * levels**2
    )(code, mine, theirs, my_map, their_map)


def merge_kernel(start, kind, apart, halves, half, code_ref, *refs):
    refs = list(refs)
    mine_map = refs.pop(0)
    if apart and kind != "maps":
        mine_states = refs.pop(0)
    else:
        mine_states = None if kind == "maps" else mine_map.at[start:]
    here = refs.pop(0)
    there = refs.pop(0) if halves else None
    their_states = refs.pop(0) if apart and kind != "maps" else None
    out = refs.pop(0)
    core = code_ref[0] // 2
    their_map = here
    if halves:
        their_map = refs.pop(0)
        rows = here.shape[0]

        @pl.when(core == 0)
        def _():
            their_map[:rows] = here[...]
            their_map[rows:] = there[...]

        @pl.when(core == 1)
        def _():
            their_map[:rows] = there[...]
            their_map[rows:] = here[...]

    if their_states is None and kind != "maps":
        their_states = their_map.at[start:]

    def joined(left_map, left_states, right_map, right_states):
        if kind != "states":
            join_maps(left_map, right_map, out)
        if kind == "maps":
            return
        states = move_states(left_states[...], right_map) + right_states[...]
        if kind == "both":
            out[start:] = states
        else:
            out[...] = states

    later(
        code_ref,
        lambda: joined(their_map, their_states, mine_map, mine_states),
        lambda: joined(mine_map, mine_states, their_map, their_states),
    )
    if half:
        half_ref = refs.pop(0)
        rows = half_ref.shape[0]

        @pl.when(core == 0)
        def _():
            half_ref[...] = out[:rows]

        @pl.when(core == 1)
        def _():
            half_ref[...] = out[rows:]


def merge(code, mine, theirs, kind, lines, apart, halves, half):
    levels = mine[0].shape[1]
    start = levels + PAD
    rows = {"maps": start, "both": start + lines, "states": lines}[kind]
    out = [shape(rows, levels)]
    if halves:
        out.append(shape(2 * theirs[0].shape[0], levels))
    if half:
        out.append(shape(rows // 2, levels))
    operands = (*mine, *theirs)
    got = call(
        functools.partial(merge_kernel, start, kind, apart, halves, half),
        [SMEM] + [VMEM] * len(operands),
        out,
        12 * rows * levels**2,
    )(code, *operands)
    return got[0], got[1] if halves else theirs[0], got[-1]


def join(left_ref, right_ref, out_ref):
    start = out_ref.shape[1] + PAD
    join_maps(left_ref, right_ref, out_ref)
    out_ref[start:] = move_states(left_ref[start:], right_ref) + right_ref[start:]


def four_kernel(
    code_ref, mine_ref, here_ref, there_ref, this_ref, that_ref,
    total_ref, beside_ref, front_ref, half_ref, four_ref, back_ref,
):
    core = lax.rem(code_ref[0], 2)
    place = code_ref[0] // 2
    rows = half_ref.shape[0]
    four_ref[place] = mine_ref[...]
    four_ref[place ^ (1 + core)] = here_ref[...]
    four_ref[place ^ (2 - core)] = there_ref[...]
    four_ref[place ^ 3, pl.ds(core * rows, rows)] = this_ref[...]
    four_ref[place ^ 3, pl.ds((1 - core) * rows, rows)] = that_ref[...]
    join(four_ref.at[0], four_ref.at[1], front_ref)
    join(four_ref.at[2], four_ref.at[3], back_ref)
    join(front_ref, back_ref, total_ref)
    half_ref[...] = total_ref[pl.ds(core * rows, rows)]
    beside_ref[...] = four_ref[place ^ 1]


def join_four(code, mine, here, there, this, that):
    rows, levels = mine.shape
    whole = shape(rows, levels)
    return call(
        four_kernel,
        [SMEM] + [VMEM] * 5,
        [whole, whole, whole, shape(rows // 2, levels)],
        36 * rows * levels**2,
        [pltpu.VMEM((4, rows, levels), F32), pltpu.VMEM((rows, levels), F32)],
    )(code, mine, here, there, this, that)


def extend_kernel(first, apart, code_ref, *refs):
    refs = list(refs)
    their_map = refs.pop(0)
    levels = their_map.shape[1]
    start = levels + PAD
    their_states = refs.pop(0)[...] if apart else their_map[start:]
    if first:
        (ahead_ref,) = refs
    else:
        before_ref, ahead_ref = refs

    def then():
        if first:
            ahead_ref[:start] = their_map[:start]
            ahead_ref[start:] = their_states
        else:
            join_maps(their_map, before_ref, ahead_ref)
            ahead_ref[start:] = move_states(their_states, before_ref) + before_ref[start:]

    def otherwise():
        if first:
            row = lax.broadcasted_iota(jnp.int32, ahead_ref.shape, 0)
            column = lax.broadcasted_iota(jnp.int32, ahead_ref.shape, 1)
            ahead_ref[...] = jnp.where(row == column, 1.0, 0.0).astype(F32)
        else:
            ahead_ref[...] = before_ref[...]

    later(code_ref, then, otherwise)


def extend(code, theirs, before):
    levels = theirs[0].shape[1]
    apart = len(theirs) == 2
    rows = levels + PAD + (theirs[1].shape[0] if apart else theirs[0].shape[0] - levels - PAD)
    first = before is None
    operands = theirs if first else (*theirs, before)
    return call(
        functools.partial(extend_kernel, first, apart),
        [SMEM] + [VMEM] * len(operands),
        shape(rows, levels),
        12 * rows * levels**2,
    )(code, *operands)


def enter_kernel(code_ref, from_ref, mine_ref, theirs_ref, out_ref):
    start = mine_ref.shape[1] + PAD

    def through(first_ref, second_ref):
        middle = move_states(from_ref[...], first_ref) + first_ref[start:]
        out_ref[...] = move_states(middle, second_ref) + second_ref[start:]

    later(
        code_ref,
        lambda: through(theirs_ref, mine_ref),
        lambda: through(mine_ref, theirs_ref),
    )


def enter(code, states, mine, theirs):
    lines, levels = states.shape
    return call(
        enter_kernel, [SMEM] + [VMEM] * 3, shape(lines, levels), 24 * lines * levels**2
    )(code, states, mine, theirs)


def plane_half_kernel(code_ref, mine_ref, theirs_ref, half_ref, total_ref):
    rows = half_ref.shape[0]
    core = lax.rem(code_ref[0] // 2, 2)

    @pl.when(code_ref[0] < 4)
    def _():
        half_ref[...] = jnp.zeros_like(half_ref)

    @pl.when(code_ref[0] >= 4)
    def _():
        later(
            code_ref,
            lambda: join(theirs_ref, mine_ref, total_ref),
            lambda: join(mine_ref, theirs_ref, total_ref),
        )
        half_ref[...] = total_ref[pl.ds(core * rows, rows)]


def plane_half(code, mine, theirs):
    rows, levels = mine.shape
    return call(
        plane_half_kernel,
        [SMEM, VMEM, VMEM],
        shape(rows // 2, levels),
        12 * rows * levels**2,
        [pltpu.VMEM((rows, levels), F32)],
    )(code, mine, theirs)


def settle_planes_kernel(
    code_ref, here_ref, there_ref, from_ref, before_ref, ahead_ref, beside_ref
):
    start = before_ref.shape[1] + PAD
    rows = here_ref.shape[0]
    core = code_ref[0] // 2

    def then():
        beside_ref[pl.ds(core * rows, rows)] = here_ref[...]
        beside_ref[pl.ds((1 - core) * rows, rows)] = there_ref[...]
        join(beside_ref, before_ref, ahead_ref)

    def otherwise():
        ahead_ref[:start] = before_ref[:start]
        ahead_ref[start:] = move_states(from_ref[...], before_ref) + before_ref[start:]

    later(code_ref, then, otherwise)


def settle_planes(code, here, there, from_first, before):
    rows, levels = before.shape
    return call(
        settle_planes_kernel,
        [SMEM] + [VMEM] * 4,
        shape(rows, levels),
        12 * rows * levels**2,
        [pltpu.VMEM((rows, levels), F32)],
    )(code, here, there, from_first, before)


def finish_kernel(
    one_ref, two_ref, before_ref, prefix_ref, trial_ref, solved_ref, held_ref, incoming, arrived
):
    fetch(prefix_ref, held_ref, arrived)
    start = before_ref.shape[1] + PAD
    entering = one_ref[...] + two_ref[...]
    incoming[...] = move_states(entering, before_ref) + before_ref[start:]

    @pl.loop(0, held_ref.shape[0])
    def _(cell):
        block_copy(prefix_ref, held_ref, arrived, cell).wait()
        solved_ref[:, cell, :] = trial_ref[cell] + dot3(incoming[...], held_ref[cell])


def finish(entering, before, prefix, trial):
    cells, lines, levels = trial.shape
    return call(
        finish_kernel,
        [VMEM, VMEM, VMEM, HBM, VMEM],
        shape(lines, cells, levels),
        12 * (cells + 1) * lines * levels**2,
        [
            pltpu.VMEM(prefix.shape, F32),
            pltpu.VMEM((lines, levels), F32),
            pltpu.SemaphoreType.DMA((cells,)),
        ],
        None,
        LARGE,
    )(*entering, before, prefix, trial)


def shards(span_count, forcing, blocks, upstream):
    cells, levels, _ = blocks.shape
    share = forcing.shape[0]
    lines = share * span_count
    parts = forcing.reshape(share, span_count, cells, levels).swapaxes(0, 1)
    parts = lax.all_to_all(parts, "span", split_axis=0, concat_axis=0, tiled=True)
    local_forcing = parts.reshape(lines, cells, levels)
    prefix, maps = prefix_maps(blocks, upstream)
    local_forcing, maps = lax.optimization_barrier((local_forcing, maps))
    trial, states = trial_states(blocks, upstream, local_forcing)

    def partner(value, axis, mask):
        count = lax.axis_size(axis)
        return lax.ppermute(value, axis, [(i, i ^ mask) for i in range(count)])

    def code_of(axis, bit):
        upper = jnp.where((lax.axis_index(axis) & bit) != 0, 1, 0)
        core = jnp.where((lax.axis_index("line") & CORE) != 0, 2, 0)
        return (upper + core).astype(jnp.int32).reshape(1)

    def along_four(total, half, before):
        device = lax.axis_index("line")
        pairs = [(i, i ^ FOUR[i & CORE]) for i in range(lax.axis_size("line"))]
        here, this = lax.ppermute(total, "line", pairs), partner(half, "line", THIRD)
        here, this, before = lax.optimization_barrier((here, this, before))
        there, that = partner(here, "line", CORE), partner(this, "line", CORE)
        code = (device & (CORE | THIRD)).astype(jnp.int32).reshape(1)
        total, beside, front, half = join_four(code, total, here, there, this, that)
        before = extend(code_of("line", FOUR[0]), (beside,), before)
        before = extend(code_of("line", FOUR[1]), (front,), before)
        return total, half, before

    total, half, before = None, None, None
    for turn, (axis, mask, bit, halves, apart) in enumerate(ROUNDS):
        code = code_of(axis, bit)
        last = turn == len(ROUNDS) - 1
        if halves:
            here = partner(half, axis, mask)
            here, before = lax.optimization_barrier((here, before))
            theirs = (here, partner(here, "line", CORE))
        else:
            theirs = (partner(maps if apart else total, axis, mask),)
            if before is not None:
                theirs, before = lax.optimization_barrier((theirs, before))
        mine = (total,)
        if apart:
            their_states = partner(states, axis, mask)
            mine, theirs = (maps, states), (*theirs, their_states)
        if last:
            plane, whole, _ = merge(code, mine, theirs, "states", lines, apart, halves, False)
        else:
            half_too = turn == len(ROUNDS) - 2
            total, whole, half = merge(code, mine, theirs, "both", lines, apart, halves, half_too)
        before = extend(code, (whole, their_states) if apart else (whole,), before)
        if turn == len(ROUNDS) - 2:
            total, half, before = along_four(total, half, before)

    def across(value, source, target):
        shift = (target - source) * PLANE
        pairs = [(i, i + shift) for i in range(source * PLANE, (source + 1) * PLANE)]
        return lax.ppermute(value, "line", pairs)

    from_first = across(plane, 0, 1)
    joined = enter(code, from_first, total, whole)
    joined, total, whole = lax.optimization_barrier((joined, total, whole))
    in_third = jnp.where(lax.axis_index("line") // PLANE == 2, 4, 0).astype(jnp.int32)
    beside = across(plane_half(code + in_third, total, whole), 2, 3)
    two_on = across(joined, 1, 3)
    entering = (two_on, across(joined, 1, 2))
    other = partner(beside, "line", CORE)
    in_last = jnp.where(lax.axis_index("line") >= 3 * PLANE, 1, 0)
    core = jnp.where((lax.axis_index("line") & CORE) != 0, 2, 0)
    in_last = (in_last + core).astype(jnp.int32).reshape(1)
    before = settle_planes(in_last, beside, other, from_first, before)
    solved = finish(entering, before, prefix, trial)
    parts = solved.reshape(span_count, share, cells, levels)
    parts = lax.all_to_all(parts, "span", split_axis=0, concat_axis=0, tiled=True)
    return parts.swapaxes(0, 1).reshape(share, span_count * cells, levels)


def solution(mesh):
    placed = (P("span", "line", None), P(("line", "span"), None, None), P(("line", "span"), None))
    return jax.shard_map(
        functools.partial(shards, mesh.shape["span"]),
        mesh=mesh,
        in_specs=placed,
        out_specs=P("span", "line", None),
        check_vma=False,
    )
```

```python
import functools

import jax
import jax.numpy as jnp
from jax import lax
from jax.experimental import pallas as pl
from jax.experimental.pallas import tpu as pltpu
from jax.sharding import PartitionSpec as P

F32 = jnp.float32
BIG = 2.0**40
STEP = 2.0**48
PAD = 16
VMEM = pl.BlockSpec(memory_space=pltpu.VMEM)
HBM = pl.BlockSpec(memory_space=pltpu.HBM)
LARGE = 52 * 2**20
SMEM = pl.BlockSpec(memory_space=pltpu.SMEM)
CORE = 1
ROUNDS = (
    ("span", 1, 1, False, True),
    ("span", 3, 2, False, False),
    ("line", 1, 1, False, False),
    ("line", 14, 8, True, False),
)
FOUR = (2, 4)
THIRD = 6
PLANE = 16


def dot(a, b):
    return jnp.dot(a, b, precision=lax.Precision.HIGHEST, preferred_element_type=F32)


def split(a):
    high = a.astype(jnp.bfloat16)
    return high, (a - high.astype(F32)).astype(jnp.bfloat16)


def dot3(a, b):
    product = functools.partial(jnp.dot, preferred_element_type=F32)
    (a_high, a_low), (b_high, b_low) = split(a), split(b)
    return product(a_high, b_high) + (product(a_high, b_low) + product(a_low, b_high))


def shape(*dims):
    return jax.ShapeDtypeStruct(dims, F32)


def call(kernel, in_specs, out_shape, flops, scratch=(), out_specs=None, vmem=8 * 2**20):
    return pl.pallas_call(
        kernel,
        in_specs=in_specs,
        out_specs=out_specs or jax.tree.map(lambda _: VMEM, out_shape),
        out_shape=out_shape,
        scratch_shapes=list(scratch),
        compiler_params=pltpu.CompilerParams(vmem_limit_bytes=vmem),
        cost_estimate=pl.CostEstimate(flops=flops, bytes_accessed=2**20, transcendentals=0),
    )


def settle(hat, count):
    large = jnp.max(jnp.abs(hat), keepdims=True) > BIG
    return hat * jnp.where(large, 1.0 / STEP, 1.0), count + jnp.where(large, 1.0, 0.0)


def unscale(value, count):
    for done in (0.0, 2.0, 4.0):
        left = count - done
        value = value * jnp.where(left > 1.5, STEP * STEP, jnp.where(left > 0.5, STEP, 1.0))
    return value


def put_map(hat, count, out_ref):
    levels = hat.shape[1]
    hat, count = settle(hat, count)
    out_ref[:levels] = hat
    out_ref[levels : levels + 8] = count
    out_ref[levels + 8 : levels + PAD] = jnp.zeros_like(count)


def join_maps(left_ref, right_ref, out_ref):
    levels = out_ref.shape[1]
    count = left_ref[levels : levels + 8] + right_ref[levels : levels + 8]
    put_map(dot(left_ref[:levels], right_ref[:levels]), count, out_ref)


def move_states(states, map_ref):
    levels = map_ref.shape[1]
    return unscale(dot(states, map_ref[:levels]), map_ref[levels : levels + 1])


def block_copy(blocks_ref, held_ref, arrived, cell):
    return pltpu.make_async_copy(blocks_ref.at[cell], held_ref.at[cell], arrived.at[cell])


def fetch(blocks_ref, held_ref, arrived):
    @pl.loop(0, held_ref.shape[0])
    def _(cell):
        block_copy(blocks_ref, held_ref, arrived, cell).start()


def maps_kernel(
    upstream_ref, blocks_ref, prefix_ref, map_ref, held_ref, made_ref, last_ref, arrived, left
):
    cells, levels, _ = held_ref.shape
    fetch(blocks_ref, held_ref, arrived)
    row = lax.broadcasted_iota(jnp.int32, (levels, levels), 0)
    column = lax.broadcasted_iota(jnp.int32, (levels, levels), 1)
    first = jnp.where(row == column, -upstream_ref[0:1, :], 0.0)
    first = jnp.sum(first, axis=1, keepdims=True)
    block_copy(blocks_ref, held_ref, arrived, 0).wait()
    first = first * held_ref[0]
    last_ref[...] = first
    made_ref[0] = first
    block_copy(made_ref, prefix_ref, left, 0).start()

    @pl.loop(1, cells)
    def _(cell):
        scaled = last_ref[...] * -upstream_ref[pl.ds(cell, 1), :]
        block_copy(blocks_ref, held_ref, arrived, cell).wait()
        product = dot(scaled, held_ref[cell])
        last_ref[...] = product
        made_ref[cell] = product
        block_copy(made_ref, prefix_ref, left, cell).start()

    put_map(last_ref[...], jnp.zeros((8, levels), F32), map_ref)

    @pl.loop(0, cells)
    def _(cell):
        block_copy(made_ref, prefix_ref, left, cell).wait()


def prefix_maps(blocks, upstream):
    cells, levels, _ = blocks.shape
    return call(
        maps_kernel,
        [VMEM, HBM],
        [shape(*blocks.shape), shape(levels + PAD, levels)],
        12 * cells * levels**3,
        [
            pltpu.VMEM(blocks.shape, F32),
            pltpu.VMEM(blocks.shape, F32),
            pltpu.VMEM((levels, levels), F32),
            pltpu.SemaphoreType.DMA((cells,)),
            pltpu.SemaphoreType.DMA((cells,)),
        ],
        [HBM, VMEM],
        LARGE,
    )(upstream, blocks)


def cut_kernel(code_ref, forcing_ref, *part_refs):
    cells = part_refs[0].shape[1]
    for turn, part_ref in enumerate(part_refs):
        first = pl.multiple_of((code_ref[0] ^ turn) * cells, cells)
        part_ref[...] = forcing_ref[:, pl.ds(first, cells), :]


def cut(here, forcing, parts):
    share, length, levels = forcing.shape
    return call(cut_kernel, [SMEM, VMEM], [shape(share, length // parts, levels)] * parts, 1)(
        here, forcing
    )


def assemble_kernel(code_ref, *refs):
    *part_refs, whole_ref = refs
    cells = part_refs[0].shape[1]
    for turn, part_ref in enumerate(part_refs):
        first = pl.multiple_of((code_ref[0] ^ turn) * cells, cells)
        whole_ref[:, pl.ds(first, cells), :] = part_ref[...]


def assemble(here, parts):
    share, cells, levels = parts[0].shape
    return call(
        assemble_kernel, [SMEM] + [VMEM] * len(parts), shape(share, len(parts) * cells, levels), 1
    )(here, *parts)


def states_kernel(code_ref, upstream_ref, blocks_ref, *refs):
    *part_refs, trial_ref, states_ref, forcing_ref = refs
    share = part_refs[0].shape[0]
    for turn, part_ref in enumerate(part_refs):
        forcing_ref[pl.ds((code_ref[0] ^ turn) * share, share)] = part_ref[...]
    states_ref[...] = jnp.zeros_like(states_ref)

    @pl.loop(0, blocks_ref.shape[0])
    def _(cell):
        forced = forcing_ref[:, cell, :] - upstream_ref[pl.ds(cell, 1), :] * states_ref[...]
        state = dot(forced, blocks_ref[cell])
        states_ref[...] = state
        trial_ref[cell] = state


def trial_states(here, blocks, upstream, parts):
    cells, levels, _ = blocks.shape
    lines = len(parts) * parts[0].shape[0]
    return call(
        states_kernel,
        [SMEM] + [VMEM] * (2 + len(parts)),
        [shape(cells, lines, levels), shape(lines, levels)],
        12 * cells * lines * levels**2,
        [pltpu.VMEM((lines, cells, levels), F32)],
    )(here, upstream, blocks, *parts)


def later(code_ref, then, otherwise):
    upper = lax.rem(code_ref[0], 2)
    pl.when(upper == 1)(then)
    pl.when(upper == 0)(otherwise)


def merge_states_kernel(code_ref, mine_ref, theirs_ref, my_map_ref, their_map_ref, out_ref):
    def then():
        out_ref[...] = move_states(theirs_ref[...], my_map_ref) + mine_ref[...]

    def otherwise():
        out_ref[...] = move_states(mine_ref[...], their_map_ref) + theirs_ref[...]

    later(code_ref, then, otherwise)


def merge_states(code, mine, theirs, my_map, their_map):
    lines, levels = mine.shape
    return call(
        merge_states_kernel, [SMEM] + [VMEM] * 4, shape(lines, levels), 12 * lines * levels**2
    )(code, mine, theirs, my_map, their_map)


def merge_kernel(start, kind, apart, halves, half, code_ref, *refs):
    refs = list(refs)
    mine_map = refs.pop(0)
    if apart and kind != "maps":
        mine_states = refs.pop(0)
    else:
        mine_states = None if kind == "maps" else mine_map.at[start:]
    here = refs.pop(0)
    there = refs.pop(0) if halves else None
    their_states = refs.pop(0) if apart and kind != "maps" else None
    out = refs.pop(0)
    core = code_ref[0] // 2
    their_map = here
    if halves:
        their_map = refs.pop(0)
        rows = here.shape[0]

        @pl.when(core == 0)
        def _():
            their_map[:rows] = here[...]
            their_map[rows:] = there[...]

        @pl.when(core == 1)
        def _():
            their_map[:rows] = there[...]
            their_map[rows:] = here[...]

    if their_states is None and kind != "maps":
        their_states = their_map.at[start:]

    def joined(left_map, left_states, right_map, right_states):
        if kind != "states":
            join_maps(left_map, right_map, out)
        if kind == "maps":
            return
        states = move_states(left_states[...], right_map) + right_states[...]
        if kind == "both":
            out[start:] = states
        else:
            out[...] = states

    later(
        code_ref,
        lambda: joined(their_map, their_states, mine_map, mine_states),
        lambda: joined(mine_map, mine_states, their_map, their_states),
    )
    if half:
        half_ref = refs.pop(0)
        rows = half_ref.shape[0]

        @pl.when(core == 0)
        def _():
            half_ref[...] = out[:rows]

        @pl.when(core == 1)
        def _():
            half_ref[...] = out[rows:]


def merge(code, mine, theirs, kind, lines, apart, halves, half):
    levels = mine[0].shape[1]
    start = levels + PAD
    rows = {"maps": start, "both": start + lines, "states": lines}[kind]
    out = [shape(rows, levels)]
    if halves:
        out.append(shape(2 * theirs[0].shape[0], levels))
    if half:
        out.append(shape(rows // 2, levels))
    operands = (*mine, *theirs)
    got = call(
        functools.partial(merge_kernel, start, kind, apart, halves, half),
        [SMEM] + [VMEM] * len(operands),
        out,
        12 * rows * levels**2,
    )(code, *operands)
    return got[0], got[1] if halves else theirs[0], got[-1]


def join(left_ref, right_ref, out_ref):
    start = out_ref.shape[1] + PAD
    join_maps(left_ref, right_ref, out_ref)
    out_ref[start:] = move_states(left_ref[start:], right_ref) + right_ref[start:]


def four_kernel(
    code_ref, mine_ref, here_ref, there_ref, this_ref, that_ref,
    total_ref, beside_ref, front_ref, half_ref, four_ref, back_ref,
):
    core = lax.rem(code_ref[0], 2)
    place = code_ref[0] // 2
    rows = half_ref.shape[0]
    four_ref[place] = mine_ref[...]
    four_ref[place ^ (1 + core)] = here_ref[...]
    four_ref[place ^ (2 - core)] = there_ref[...]
    four_ref[place ^ 3, pl.ds(core * rows, rows)] = this_ref[...]
    four_ref[place ^ 3, pl.ds((1 - core) * rows, rows)] = that_ref[...]
    join(four_ref.at[0], four_ref.at[1], front_ref)
    join(four_ref.at[2], four_ref.at[3], back_ref)
    join(front_ref, back_ref, total_ref)
    half_ref[...] = total_ref[pl.ds(core * rows, rows)]
    beside_ref[...] = four_ref[place ^ 1]


def join_four(code, mine, here, there, this, that):
    rows, levels = mine.shape
    whole = shape(rows, levels)
    return call(
        four_kernel,
        [SMEM] + [VMEM] * 5,
        [whole, whole, whole, shape(rows // 2, levels)],
        36 * rows * levels**2,
        [pltpu.VMEM((4, rows, levels), F32), pltpu.VMEM((rows, levels), F32)],
    )(code, mine, here, there, this, that)


def extend_kernel(first, apart, code_ref, *refs):
    refs = list(refs)
    their_map = refs.pop(0)
    levels = their_map.shape[1]
    start = levels + PAD
    their_states = refs.pop(0)[...] if apart else their_map[start:]
    if first:
        (ahead_ref,) = refs
    else:
        before_ref, ahead_ref = refs

    def then():
        if first:
            ahead_ref[:start] = their_map[:start]
            ahead_ref[start:] = their_states
        else:
            join_maps(their_map, before_ref, ahead_ref)
            ahead_ref[start:] = move_states(their_states, before_ref) + before_ref[start:]

    def otherwise():
        if first:
            row = lax.broadcasted_iota(jnp.int32, ahead_ref.shape, 0)
            column = lax.broadcasted_iota(jnp.int32, ahead_ref.shape, 1)
            ahead_ref[...] = jnp.where(row == column, 1.0, 0.0).astype(F32)
        else:
            ahead_ref[...] = before_ref[...]

    later(code_ref, then, otherwise)


def extend(code, theirs, before):
    levels = theirs[0].shape[1]
    apart = len(theirs) == 2
    rows = levels + PAD + (theirs[1].shape[0] if apart else theirs[0].shape[0] - levels - PAD)
    first = before is None
    operands = theirs if first else (*theirs, before)
    return call(
        functools.partial(extend_kernel, first, apart),
        [SMEM] + [VMEM] * len(operands),
        shape(rows, levels),
        12 * rows * levels**2,
    )(code, *operands)


def enter_kernel(from_ref, map_ref, own_ref, out_ref):
    out_ref[...] = move_states(from_ref[...], map_ref) + own_ref[...]


def enter(states, total, own):
    lines, levels = own.shape
    return call(enter_kernel, [VMEM] * 3, shape(lines, levels), 12 * lines * levels**2)(
        states, total, own
    )


def plane_total_kernel(code_ref, mine_ref, theirs_ref, total_ref):
    @pl.when(code_ref[0] < 4)
    def _():
        total_ref[...] = jnp.zeros_like(total_ref)

    @pl.when(code_ref[0] >= 4)
    def _():
        later(
            code_ref,
            lambda: join(theirs_ref, mine_ref, total_ref),
            lambda: join(mine_ref, theirs_ref, total_ref),
        )


def plane_total(code, mine, theirs):
    rows, levels = mine.shape
    return call(
        plane_total_kernel, [SMEM, VMEM, VMEM], shape(rows, levels), 12 * rows * levels**2
    )(code, mine, theirs)


def settle_planes_kernel(code_ref, beside_ref, from_ref, before_ref, ahead_ref):
    start = before_ref.shape[1] + PAD

    def then():
        join_maps(beside_ref, before_ref, ahead_ref)
        ahead_ref[start:] = move_states(beside_ref[start:], before_ref) + before_ref[start:]

    def otherwise():
        ahead_ref[:start] = before_ref[:start]
        ahead_ref[start:] = move_states(from_ref[...], before_ref) + before_ref[start:]

    later(code_ref, then, otherwise)


def settle_planes(code, beside, from_first, before):
    rows, levels = before.shape
    return call(
        settle_planes_kernel, [SMEM] + [VMEM] * 3, shape(rows, levels), 12 * rows * levels**2
    )(code, beside, from_first, before)


def finish_kernel(code_ref, one_ref, two_ref, before_ref, prefix_ref, trial_ref, *refs):
    *part_refs, solved_ref, held_ref, incoming, arrived = refs
    fetch(prefix_ref, held_ref, arrived)
    start = before_ref.shape[1] + PAD
    entering = one_ref[...] + two_ref[...]
    incoming[...] = move_states(entering, before_ref) + before_ref[start:]

    @pl.loop(0, held_ref.shape[0])
    def _(cell):
        block_copy(prefix_ref, held_ref, arrived, cell).wait()
        solved_ref[:, cell, :] = trial_ref[cell] + dot3(incoming[...], held_ref[cell])

    share = part_refs[0].shape[0]
    for turn, part_ref in enumerate(part_refs):
        part_ref[...] = solved_ref[pl.ds((code_ref[0] ^ turn) * share, share)]


def finish(here, entering, before, prefix, trial, parts):
    cells, lines, levels = trial.shape
    return call(
        finish_kernel,
        [SMEM, VMEM, VMEM, VMEM, HBM, VMEM],
        [shape(lines // parts, cells, levels)] * parts,
        12 * (cells + 1) * lines * levels**2,
        [
            pltpu.VMEM((lines, cells, levels), F32),
            pltpu.VMEM(prefix.shape, F32),
            pltpu.VMEM((lines, levels), F32),
            pltpu.SemaphoreType.DMA((cells,)),
        ],
        None,
        LARGE,
    )(here, *entering, before, prefix, trial)


def shards(span_count, forcing, blocks, upstream):
    cells, levels, _ = blocks.shape
    share = forcing.shape[0]
    lines = share * span_count
    here = lax.axis_index("span").astype(jnp.int32).reshape(1)

    def trade(parts):
        kept, *sent = parts
        return [kept] + [partner(part, "span", k + 1) for k, part in enumerate(sent)]

    def partner(value, axis, mask):
        count = lax.axis_size(axis)
        return lax.ppermute(value, axis, [(i, i ^ mask) for i in range(count)])

    forcing_parts = trade(cut(here, forcing, span_count))
    prefix, maps = prefix_maps(blocks, upstream)
    forcing_parts, maps = lax.optimization_barrier((forcing_parts, maps))
    trial, states = trial_states(here, blocks, upstream, forcing_parts)

    def code_of(axis, bit):
        upper = jnp.where((lax.axis_index(axis) & bit) != 0, 1, 0)
        core = jnp.where((lax.axis_index("line") & CORE) != 0, 2, 0)
        return (upper + core).astype(jnp.int32).reshape(1)

    def along_four(total, half, before):
        device = lax.axis_index("line")
        pairs = [(i, i ^ FOUR[i & CORE]) for i in range(lax.axis_size("line"))]
        here, this = lax.ppermute(total, "line", pairs), partner(half, "line", THIRD)
        here, this, before = lax.optimization_barrier((here, this, before))
        there, that = partner(here, "line", CORE), partner(this, "line", CORE)
        code = (device & (CORE | THIRD)).astype(jnp.int32).reshape(1)
        total, beside, front, half = join_four(code, total, here, there, this, that)
        before = extend(code_of("line", FOUR[0]), (beside,), before)
        before = extend(code_of("line", FOUR[1]), (front,), before)
        return total, half, before

    total, half, before = None, None, None
    for turn, (axis, mask, bit, halves, apart) in enumerate(ROUNDS):
        code = code_of(axis, bit)
        last = turn == len(ROUNDS) - 1
        if halves:
            mine_half = partner(half, axis, mask)
            mine_half, before = lax.optimization_barrier((mine_half, before))
            theirs = (mine_half, partner(mine_half, "line", CORE))
        else:
            theirs = (partner(maps if apart else total, axis, mask),)
            if before is not None:
                theirs, before = lax.optimization_barrier((theirs, before))
        mine = (total,)
        if apart:
            their_states = partner(states, axis, mask)
            mine, theirs = (maps, states), (*theirs, their_states)
        if last:
            plane, whole, _ = merge(code, mine, theirs, "states", lines, apart, halves, False)
            inner = (lax.axis_index("line") // PLANE + 1) // 2 == 1
            total = plane_total(code + jnp.where(inner, 4, 0).astype(jnp.int32), total, whole)
        else:
            half_too = turn == len(ROUNDS) - 2
            total, whole, half = merge(code, mine, theirs, "both", lines, apart, halves, half_too)
        before = extend(code, (whole, their_states) if apart else (whole,), before)
        if turn == len(ROUNDS) - 2:
            total, half, before = along_four(total, half, before)

    def across(value, source, target):
        shift = (target - source) * PLANE
        pairs = [(i, i + shift) for i in range(source * PLANE, (source + 1) * PLANE)]
        return lax.ppermute(value, "line", pairs)

    from_first = across(plane, 0, 1)
    beside = across(total, 2, 3)
    from_first, before = lax.optimization_barrier((from_first, before))
    joined = enter(from_first, total, plane)
    two_on = across(joined, 1, 3)
    entering = (two_on, across(joined, 1, 2))
    in_last = jnp.where(lax.axis_index("line") >= 3 * PLANE, 1, 0).astype(jnp.int32).reshape(1)
    before = settle_planes(in_last, beside, from_first, before)
    return assemble(here, trade(finish(here, entering, before, prefix, trial, span_count)))


def solution(mesh):
    placed = (P("span", "line", None), P(("line", "span"), None, None), P(("line", "span"), None))
    return jax.shard_map(
        functools.partial(shards, mesh.shape["span"]),
        mesh=mesh,
        in_specs=placed,
        out_specs=P("span", "line", None),
        check_vma=False,
    )
```

```python
import functools

import jax
import jax.numpy as jnp
from jax import lax
from jax.experimental import pallas as pl
from jax.experimental.pallas import tpu as pltpu
from jax.sharding import PartitionSpec as P

F32 = jnp.float32
BIG = 2.0**40
STEP = 2.0**48
PAD = 16
VMEM = pl.BlockSpec(memory_space=pltpu.VMEM)
HBM = pl.BlockSpec(memory_space=pltpu.HBM)
LARGE = 52 * 2**20
SMEM = pl.BlockSpec(memory_space=pltpu.SMEM)
CORE = 1
ROUNDS = (
    ("span", 1, 1, False, True),
    ("span", 3, 2, False, False),
    ("line", 1, 1, False, False),
    ("line", 14, 8, True, False),
)
FOUR = (2, 4)
THIRD = 6
PLANE = 16


def dot(a, b):
    return jnp.dot(a, b, precision=lax.Precision.HIGHEST, preferred_element_type=F32)


def split(a):
    high = a.astype(jnp.bfloat16)
    return high, (a - high.astype(F32)).astype(jnp.bfloat16)


def shape(*dims):
    return jax.ShapeDtypeStruct(dims, F32)


def call(kernel, in_specs, out_shape, flops, scratch=(), out_specs=None, vmem=8 * 2**20):
    return pl.pallas_call(
        kernel,
        in_specs=in_specs,
        out_specs=out_specs or jax.tree.map(lambda _: VMEM, out_shape),
        out_shape=out_shape,
        scratch_shapes=list(scratch),
        compiler_params=pltpu.CompilerParams(vmem_limit_bytes=vmem),
        cost_estimate=pl.CostEstimate(flops=flops, bytes_accessed=2**20, transcendentals=0),
    )


def settle(hat, count):
    large = jnp.max(jnp.abs(hat), keepdims=True) > BIG
    return hat * jnp.where(large, 1.0 / STEP, 1.0), count + jnp.where(large, 1.0, 0.0)


def unscale(value, count):
    for done in (0.0, 2.0, 4.0):
        left = count - done
        value = value * jnp.where(left > 1.5, STEP * STEP, jnp.where(left > 0.5, STEP, 1.0))
    return value


def put_map(hat, count, out_ref):
    levels = hat.shape[1]
    hat, count = settle(hat, count)
    out_ref[:levels] = hat
    out_ref[levels : levels + 8] = count
    out_ref[levels + 8 : levels + PAD] = jnp.zeros_like(count)


def join_maps(left_ref, right_ref, out_ref):
    levels = out_ref.shape[1]
    count = left_ref[levels : levels + 8] + right_ref[levels : levels + 8]
    put_map(dot(left_ref[:levels], right_ref[:levels]), count, out_ref)


def move_states(states, map_ref):
    levels = map_ref.shape[1]
    return unscale(dot(states, map_ref[:levels]), map_ref[levels : levels + 1])


def block_copy(blocks_ref, held_ref, arrived, cell):
    return pltpu.make_async_copy(blocks_ref.at[cell], held_ref.at[cell], arrived.at[cell])


def fetch(blocks_ref, held_ref, arrived):
    @pl.loop(0, held_ref.shape[0])
    def _(cell):
        block_copy(blocks_ref, held_ref, arrived, cell).start()


def maps_kernel(
    upstream_ref, blocks_ref, prefix_ref, map_ref, held_ref, made_ref, last_ref, arrived, left
):
    cells, levels, _ = held_ref.shape
    fetch(blocks_ref, held_ref, arrived)
    row = lax.broadcasted_iota(jnp.int32, (levels, levels), 0)
    column = lax.broadcasted_iota(jnp.int32, (levels, levels), 1)
    first = jnp.where(row == column, -upstream_ref[0:1, :], 0.0)
    first = jnp.sum(first, axis=1, keepdims=True)
    block_copy(blocks_ref, held_ref, arrived, 0).wait()
    first = first * held_ref[0]
    last_ref[...] = first
    made_ref[0] = first
    block_copy(made_ref, prefix_ref, left, 0).start()

    def extend_by(cell):
        scaled = last_ref[...] * -upstream_ref[pl.ds(cell, 1), :]
        block_copy(blocks_ref, held_ref, arrived, cell).wait()
        product = dot(scaled, held_ref[cell])
        last_ref[...] = product
        made_ref[cell] = product
        block_copy(made_ref, prefix_ref, left, cell).start()

    extend_by(1)

    @pl.loop(1, cells // 2)
    def _(pair):
        extend_by(2 * pair)
        extend_by(2 * pair + 1)

    put_map(last_ref[...], jnp.zeros((8, levels), F32), map_ref)

    @pl.loop(0, cells)
    def _(cell):
        block_copy(made_ref, prefix_ref, left, cell).wait()


def prefix_maps(blocks, upstream):
    cells, levels, _ = blocks.shape
    return call(
        maps_kernel,
        [VMEM, HBM],
        [shape(*blocks.shape), shape(levels + PAD, levels)],
        12 * cells * levels**3,
        [
            pltpu.VMEM(blocks.shape, F32),
            pltpu.VMEM(blocks.shape, F32),
            pltpu.VMEM((levels, levels), F32),
            pltpu.SemaphoreType.DMA((cells,)),
            pltpu.SemaphoreType.DMA((cells,)),
        ],
        [HBM, VMEM],
        LARGE,
    )(upstream, blocks)


def cut_kernel(code_ref, forcing_ref, *part_refs):
    cells = part_refs[0].shape[1]
    for turn, part_ref in enumerate(part_refs):
        first = pl.multiple_of((code_ref[0] ^ turn) * cells, cells)
        part_ref[...] = forcing_ref[:, pl.ds(first, cells), :]


def cut(here, forcing, parts):
    share, length, levels = forcing.shape
    return call(cut_kernel, [SMEM, VMEM], [shape(share, length // parts, levels)] * parts, 1)(
        here, forcing
    )


def assemble_kernel(code_ref, *refs):
    *part_refs, whole_ref = refs
    cells = part_refs[0].shape[1]
    for turn, part_ref in enumerate(part_refs):
        first = pl.multiple_of((code_ref[0] ^ turn) * cells, cells)
        whole_ref[:, pl.ds(first, cells), :] = part_ref[...]


def assemble(here, parts):
    share, cells, levels = parts[0].shape
    return call(
        assemble_kernel, [SMEM] + [VMEM] * len(parts), shape(share, len(parts) * cells, levels), 1
    )(here, *parts)


def states_kernel(code_ref, upstream_ref, blocks_ref, *refs):
    *part_refs, trial_ref, states_ref, forcing_ref = refs
    share = part_refs[0].shape[0]
    for turn, part_ref in enumerate(part_refs):
        forcing_ref[pl.ds((code_ref[0] ^ turn) * share, share)] = part_ref[...]
    states_ref[...] = jnp.zeros_like(states_ref)

    @pl.loop(0, blocks_ref.shape[0] // 2)
    def _(pair):
        state = states_ref[...]
        for cell in (2 * pair, 2 * pair + 1):
            forced = forcing_ref[:, cell, :] - upstream_ref[pl.ds(cell, 1), :] * state
            state = dot(forced, blocks_ref[cell])
            trial_ref[cell] = state
        states_ref[...] = state


def trial_states(here, blocks, upstream, parts):
    cells, levels, _ = blocks.shape
    lines = len(parts) * parts[0].shape[0]
    return call(
        states_kernel,
        [SMEM] + [VMEM] * (2 + len(parts)),
        [shape(cells, lines, levels), shape(lines, levels)],
        12 * cells * lines * levels**2,
        [pltpu.VMEM((lines, cells, levels), F32)],
    )(here, upstream, blocks, *parts)


def later(code_ref, then, otherwise):
    upper = lax.rem(code_ref[0], 2)
    pl.when(upper == 1)(then)
    pl.when(upper == 0)(otherwise)


def merge_states_kernel(code_ref, mine_ref, theirs_ref, my_map_ref, their_map_ref, out_ref):
    def then():
        out_ref[...] = move_states(theirs_ref[...], my_map_ref) + mine_ref[...]

    def otherwise():
        out_ref[...] = move_states(mine_ref[...], their_map_ref) + theirs_ref[...]

    later(code_ref, then, otherwise)


def merge_states(code, mine, theirs, my_map, their_map):
    lines, levels = mine.shape
    return call(
        merge_states_kernel, [SMEM] + [VMEM] * 4, shape(lines, levels), 12 * lines * levels**2
    )(code, mine, theirs, my_map, their_map)


def merge_kernel(start, kind, apart, halves, half, code_ref, *refs):
    refs = list(refs)
    mine_map = refs.pop(0)
    if apart and kind != "maps":
        mine_states = refs.pop(0)
    else:
        mine_states = None if kind == "maps" else mine_map.at[start:]
    here = refs.pop(0)
    there = refs.pop(0) if halves else None
    their_states = refs.pop(0) if apart and kind != "maps" else None
    out = refs.pop(0)
    core = code_ref[0] // 2
    their_map = here
    if halves:
        their_map = refs.pop(0)
        rows = here.shape[0]

        @pl.when(core == 0)
        def _():
            their_map[:rows] = here[...]
            their_map[rows:] = there[...]

        @pl.when(core == 1)
        def _():
            their_map[:rows] = there[...]
            their_map[rows:] = here[...]

    if their_states is None and kind != "maps":
        their_states = their_map.at[start:]

    def joined(left_map, left_states, right_map, right_states):
        if kind != "states":
            join_maps(left_map, right_map, out)
        if kind == "maps":
            return
        states = move_states(left_states[...], right_map) + right_states[...]
        if kind == "both":
            out[start:] = states
        else:
            out[...] = states

    later(
        code_ref,
        lambda: joined(their_map, their_states, mine_map, mine_states),
        lambda: joined(mine_map, mine_states, their_map, their_states),
    )
    if half:
        half_ref = refs.pop(0)
        rows = half_ref.shape[0]

        @pl.when(core == 0)
        def _():
            half_ref[...] = out[:rows]

        @pl.when(core == 1)
        def _():
            half_ref[...] = out[rows:]


def merge(code, mine, theirs, kind, lines, apart, halves, half):
    levels = mine[0].shape[1]
    start = levels + PAD
    rows = {"maps": start, "both": start + lines, "states": lines}[kind]
    out = [shape(rows, levels)]
    if halves:
        out.append(shape(2 * theirs[0].shape[0], levels))
    if half:
        out.append(shape(rows // 2, levels))
    operands = (*mine, *theirs)
    got = call(
        functools.partial(merge_kernel, start, kind, apart, halves, half),
        [SMEM] + [VMEM] * len(operands),
        out,
        12 * rows * levels**2,
    )(code, *operands)
    return got[0], got[1] if halves else theirs[0], got[-1]


def join(left_ref, right_ref, out_ref):
    start = out_ref.shape[1] + PAD
    join_maps(left_ref, right_ref, out_ref)
    out_ref[start:] = move_states(left_ref[start:], right_ref) + right_ref[start:]


def four_kernel(
    code_ref, mine_ref, here_ref, there_ref, this_ref, that_ref,
    total_ref, beside_ref, front_ref, half_ref, four_ref, back_ref,
):
    core = lax.rem(code_ref[0], 2)
    place = code_ref[0] // 2
    rows = half_ref.shape[0]
    four_ref[place] = mine_ref[...]
    four_ref[place ^ (1 + core)] = here_ref[...]
    four_ref[place ^ (2 - core)] = there_ref[...]
    four_ref[place ^ 3, pl.ds(core * rows, rows)] = this_ref[...]
    four_ref[place ^ 3, pl.ds((1 - core) * rows, rows)] = that_ref[...]
    join(four_ref.at[0], four_ref.at[1], front_ref)
    join(four_ref.at[2], four_ref.at[3], back_ref)
    join(front_ref, back_ref, total_ref)
    half_ref[...] = total_ref[pl.ds(core * rows, rows)]
    beside_ref[...] = four_ref[place ^ 1]


def join_four(code, mine, here, there, this, that):
    rows, levels = mine.shape
    whole = shape(rows, levels)
    return call(
        four_kernel,
        [SMEM] + [VMEM] * 5,
        [whole, whole, whole, shape(rows // 2, levels)],
        36 * rows * levels**2,
        [pltpu.VMEM((4, rows, levels), F32), pltpu.VMEM((rows, levels), F32)],
    )(code, mine, here, there, this, that)


def extend_kernel(first, apart, code_ref, *refs):
    refs = list(refs)
    their_map = refs.pop(0)
    levels = their_map.shape[1]
    start = levels + PAD
    their_states = refs.pop(0)[...] if apart else their_map[start:]
    if first:
        (ahead_ref,) = refs
    else:
        before_ref, ahead_ref = refs

    def then():
        if first:
            ahead_ref[:start] = their_map[:start]
            ahead_ref[start:] = their_states
        else:
            join_maps(their_map, before_ref, ahead_ref)
            ahead_ref[start:] = move_states(their_states, before_ref) + before_ref[start:]

    def otherwise():
        if first:
            row = lax.broadcasted_iota(jnp.int32, ahead_ref.shape, 0)
            column = lax.broadcasted_iota(jnp.int32, ahead_ref.shape, 1)
            ahead_ref[...] = jnp.where(row == column, 1.0, 0.0).astype(F32)
        else:
            ahead_ref[...] = before_ref[...]

    later(code_ref, then, otherwise)


def extend(code, theirs, before):
    levels = theirs[0].shape[1]
    apart = len(theirs) == 2
    rows = levels + PAD + (theirs[1].shape[0] if apart else theirs[0].shape[0] - levels - PAD)
    first = before is None
    operands = theirs if first else (*theirs, before)
    return call(
        functools.partial(extend_kernel, first, apart),
        [SMEM] + [VMEM] * len(operands),
        shape(rows, levels),
        12 * rows * levels**2,
    )(code, *operands)


def enter_kernel(from_ref, map_ref, own_ref, out_ref):
    out_ref[...] = move_states(from_ref[...], map_ref) + own_ref[...]


def enter(states, total, own):
    lines, levels = own.shape
    return call(enter_kernel, [VMEM] * 3, shape(lines, levels), 12 * lines * levels**2)(
        states, total, own
    )


def plane_total_kernel(code_ref, mine_ref, theirs_ref, total_ref):
    @pl.when(code_ref[0] < 4)
    def _():
        total_ref[...] = jnp.zeros_like(total_ref)

    @pl.when(code_ref[0] >= 4)
    def _():
        later(
            code_ref,
            lambda: join(theirs_ref, mine_ref, total_ref),
            lambda: join(mine_ref, theirs_ref, total_ref),
        )


def plane_total(code, mine, theirs):
    rows, levels = mine.shape
    return call(
        plane_total_kernel, [SMEM, VMEM, VMEM], shape(rows, levels), 12 * rows * levels**2
    )(code, mine, theirs)


def settle_planes_kernel(code_ref, beside_ref, from_ref, before_ref, ahead_ref):
    start = before_ref.shape[1] + PAD

    def then():
        join_maps(beside_ref, before_ref, ahead_ref)
        ahead_ref[start:] = move_states(beside_ref[start:], before_ref) + before_ref[start:]

    def otherwise():
        ahead_ref[:start] = before_ref[:start]
        ahead_ref[start:] = move_states(from_ref[...], before_ref) + before_ref[start:]

    later(code_ref, then, otherwise)


def settle_planes(code, beside, from_first, before):
    rows, levels = before.shape
    return call(
        settle_planes_kernel, [SMEM] + [VMEM] * 3, shape(rows, levels), 12 * rows * levels**2
    )(code, beside, from_first, before)


def finish_kernel(code_ref, one_ref, two_ref, before_ref, prefix_ref, trial_ref, *refs):
    *part_refs, solved_ref, held_ref, incoming, arrived = refs
    fetch(prefix_ref, held_ref, arrived)
    start = before_ref.shape[1] + PAD
    entering = one_ref[...] + two_ref[...]
    high, low = split(move_states(entering, before_ref) + before_ref[start:])
    lines = high.shape[0]
    incoming[:lines] = high
    incoming[lines:] = low
    product = functools.partial(jnp.dot, preferred_element_type=F32)

    @pl.loop(0, held_ref.shape[0] // 2)
    def _(pair):
        for turn in range(2):
            cell = 2 * pair + turn
            block_copy(prefix_ref, held_ref, arrived, cell).wait()
            map_high, map_low = split(held_ref[cell])
            both = product(incoming[...], map_high)
            rest = both[lines:] + product(incoming[:lines], map_low)
            solved_ref[:, cell, :] = trial_ref[cell] + (both[:lines] + rest)

    share = part_refs[0].shape[0]
    for turn, part_ref in enumerate(part_refs):
        part_ref[...] = solved_ref[pl.ds((code_ref[0] ^ turn) * share, share)]


def finish(here, entering, before, prefix, trial, parts):
    cells, lines, levels = trial.shape
    return call(
        finish_kernel,
        [SMEM, VMEM, VMEM, VMEM, HBM, VMEM],
        [shape(lines // parts, cells, levels)] * parts,
        12 * (cells + 1) * lines * levels**2,
        [
            pltpu.VMEM((lines, cells, levels), F32),
            pltpu.VMEM(prefix.shape, F32),
            pltpu.VMEM((2 * lines, levels), jnp.bfloat16),
            pltpu.SemaphoreType.DMA((cells,)),
        ],
        None,
        LARGE,
    )(here, *entering, before, prefix, trial)


def shards(span_count, forcing, blocks, upstream):
    cells, levels, _ = blocks.shape
    share = forcing.shape[0]
    lines = share * span_count
    here = lax.axis_index("span").astype(jnp.int32).reshape(1)

    def trade(parts):
        kept, *sent = parts
        return [kept] + [partner(part, "span", k + 1) for k, part in enumerate(sent)]

    def partner(value, axis, mask):
        count = lax.axis_size(axis)
        return lax.ppermute(value, axis, [(i, i ^ mask) for i in range(count)])

    forcing_parts = trade(cut(here, forcing, span_count))
    prefix, maps = prefix_maps(blocks, upstream)
    forcing_parts, maps = lax.optimization_barrier((forcing_parts, maps))
    trial, states = trial_states(here, blocks, upstream, forcing_parts)

    def code_of(axis, bit):
        upper = jnp.where((lax.axis_index(axis) & bit) != 0, 1, 0)
        core = jnp.where((lax.axis_index("line") & CORE) != 0, 2, 0)
        return (upper + core).astype(jnp.int32).reshape(1)

    def along_four(total, half, before):
        device = lax.axis_index("line")
        pairs = [(i, i ^ FOUR[i & CORE]) for i in range(lax.axis_size("line"))]
        here, this = lax.ppermute(total, "line", pairs), partner(half, "line", THIRD)
        here, this, before = lax.optimization_barrier((here, this, before))
        there, that = partner(here, "line", CORE), partner(this, "line", CORE)
        code = (device & (CORE | THIRD)).astype(jnp.int32).reshape(1)
        total, beside, front, half = join_four(code, total, here, there, this, that)
        before = extend(code_of("line", FOUR[0]), (beside,), before)
        before = extend(code_of("line", FOUR[1]), (front,), before)
        return total, half, before

    total, half, before = None, None, None
    for turn, (axis, mask, bit, halves, apart) in enumerate(ROUNDS):
        code = code_of(axis, bit)
        last = turn == len(ROUNDS) - 1
        if halves:
            mine_half = partner(half, axis, mask)
            mine_half, before = lax.optimization_barrier((mine_half, before))
            theirs = (mine_half, partner(mine_half, "line", CORE))
        else:
            theirs = (partner(maps if apart else total, axis, mask),)
            if before is not None:
                theirs, before = lax.optimization_barrier((theirs, before))
        mine = (total,)
        if apart:
            their_states = partner(states, axis, mask)
            mine, theirs = (maps, states), (*theirs, their_states)
        if last:
            plane, whole, _ = merge(code, mine, theirs, "states", lines, apart, halves, False)
            inner = (lax.axis_index("line") // PLANE + 1) // 2 == 1
            total = plane_total(code + jnp.where(inner, 4, 0).astype(jnp.int32), total, whole)
        else:
            half_too = turn == len(ROUNDS) - 2
            total, whole, half = merge(code, mine, theirs, "both", lines, apart, halves, half_too)
        before = extend(code, (whole, their_states) if apart else (whole,), before)
        if turn == len(ROUNDS) - 2:
            total, half, before = along_four(total, half, before)

    def across(value, source, target):
        shift = (target - source) * PLANE
        pairs = [(i, i + shift) for i in range(source * PLANE, (source + 1) * PLANE)]
        return lax.ppermute(value, "line", pairs)

    from_first = across(plane, 0, 1)
    beside = across(total, 2, 3)
    from_first, before = lax.optimization_barrier((from_first, before))
    joined = enter(from_first, total, plane)
    two_on = across(joined, 1, 3)
    entering = (two_on, across(joined, 1, 2))
    in_last = jnp.where(lax.axis_index("line") >= 3 * PLANE, 1, 0).astype(jnp.int32).reshape(1)
    before = settle_planes(in_last, beside, from_first, before)
    return assemble(here, trade(finish(here, entering, before, prefix, trial, span_count)))


def solution(mesh):
    placed = (P("span", "line", None), P(("line", "span"), None, None), P(("line", "span"), None))
    return jax.shard_map(
        functools.partial(shards, mesh.shape["span"]),
        mesh=mesh,
        in_specs=placed,
        out_specs=P("span", "line", None),
        check_vma=False,
    )
```

```python
import functools

import jax
import jax.numpy as jnp
from jax import lax
from jax.experimental import pallas as pl
from jax.experimental.pallas import tpu as pltpu
from jax.sharding import PartitionSpec as P

F32 = jnp.float32
BIG = 2.0**40
STEP = 2.0**48
PAD = 16
VMEM = pl.BlockSpec(memory_space=pltpu.VMEM)
HBM = pl.BlockSpec(memory_space=pltpu.HBM)
LARGE = 52 * 2**20
SMEM = pl.BlockSpec(memory_space=pltpu.SMEM)
CORE = 1
ROUNDS = (
    ("span", 1, 1, False, True),
    ("span", 3, 2, False, False),
    ("line", 1, 1, False, False),
    ("line", 14, 8, True, False),
)
FOUR = (2, 4)
THIRD = 6
PLANE = 16


def dot(a, b):
    return jnp.dot(a, b, precision=lax.Precision.HIGHEST, preferred_element_type=F32)


def split(a):
    high = a.astype(jnp.bfloat16)
    return high, (a - high.astype(F32)).astype(jnp.bfloat16)


def dot3(a, b):
    product = functools.partial(jnp.dot, preferred_element_type=F32)
    (a_high, a_low), (b_high, b_low) = split(a), split(b)
    return product(a_high, b_high) + (product(a_high, b_low) + product(a_low, b_high))


def shape(*dims):
    return jax.ShapeDtypeStruct(dims, F32)


def call(kernel, in_specs, out_shape, flops, scratch=(), out_specs=None, vmem=8 * 2**20):
    return pl.pallas_call(
        kernel,
        in_specs=in_specs,
        out_specs=out_specs or jax.tree.map(lambda _: VMEM, out_shape),
        out_shape=out_shape,
        scratch_shapes=list(scratch),
        compiler_params=pltpu.CompilerParams(vmem_limit_bytes=vmem),
        cost_estimate=pl.CostEstimate(flops=flops, bytes_accessed=2**20, transcendentals=0),
    )


def settle(hat, count):
    large = jnp.max(jnp.abs(hat), keepdims=True) > BIG
    return hat * jnp.where(large, 1.0 / STEP, 1.0), count + jnp.where(large, 1.0, 0.0)


def unscale(value, count):
    for done in (0.0, 2.0, 4.0):
        left = count - done
        value = value * jnp.where(left > 1.5, STEP * STEP, jnp.where(left > 0.5, STEP, 1.0))
    return value


def put_map(hat, count, out_ref):
    levels = hat.shape[1]
    hat, count = settle(hat, count)
    out_ref[:levels] = hat
    out_ref[levels : levels + 8] = count
    out_ref[levels + 8 : levels + PAD] = jnp.zeros_like(count)


def join_maps(left_ref, right_ref, out_ref):
    levels = out_ref.shape[1]
    count = left_ref[levels : levels + 8] + right_ref[levels : levels + 8]
    put_map(dot3(left_ref[:levels], right_ref[:levels]), count, out_ref)


def move_states(states, map_ref):
    levels = map_ref.shape[1]
    return unscale(dot(states, map_ref[:levels]), map_ref[levels : levels + 1])


def block_copy(blocks_ref, held_ref, arrived, cell):
    return pltpu.make_async_copy(blocks_ref.at[cell], held_ref.at[cell], arrived.at[cell])


def fetch(blocks_ref, held_ref, arrived):
    @pl.loop(0, held_ref.shape[0])
    def _(cell):
        block_copy(blocks_ref, held_ref, arrived, cell).start()


def maps_kernel(
    upstream_ref, blocks_ref, prefix_ref, map_ref, held_ref, made_ref, last_ref, arrived, left
):
    cells, levels, _ = held_ref.shape
    fetch(blocks_ref, held_ref, arrived)
    row = lax.broadcasted_iota(jnp.int32, (levels, levels), 0)
    column = lax.broadcasted_iota(jnp.int32, (levels, levels), 1)
    first = jnp.where(row == column, -upstream_ref[0:1, :], 0.0)
    first = jnp.sum(first, axis=1, keepdims=True)
    block_copy(blocks_ref, held_ref, arrived, 0).wait()
    first = first * held_ref[0]
    last_ref[...] = first
    made_ref[0] = first
    block_copy(made_ref, prefix_ref, left, 0).start()

    @pl.loop(1, cells)
    def _(cell):
        scaled = last_ref[...] * -upstream_ref[pl.ds(cell, 1), :]
        block_copy(blocks_ref, held_ref, arrived, cell).wait()
        product = dot(scaled, held_ref[cell])
        last_ref[...] = product
        made_ref[cell] = product
        block_copy(made_ref, prefix_ref, left, cell).start()

    put_map(last_ref[...], jnp.zeros((8, levels), F32), map_ref)

    @pl.loop(0, cells)
    def _(cell):
        block_copy(made_ref, prefix_ref, left, cell).wait()


def prefix_maps(blocks, upstream):
    cells, levels, _ = blocks.shape
    return call(
        maps_kernel,
        [VMEM, HBM],
        [shape(*blocks.shape), shape(levels + PAD, levels)],
        12 * cells * levels**3,
        [
            pltpu.VMEM(blocks.shape, F32),
            pltpu.VMEM(blocks.shape, F32),
            pltpu.VMEM((levels, levels), F32),
            pltpu.SemaphoreType.DMA((cells,)),
            pltpu.SemaphoreType.DMA((cells,)),
        ],
        [HBM, VMEM],
        LARGE,
    )(upstream, blocks)


def cut_kernel(code_ref, forcing_ref, *part_refs):
    cells = part_refs[0].shape[1]
    for turn, part_ref in enumerate(part_refs):
        first = pl.multiple_of((code_ref[0] ^ turn) * cells, cells)
        part_ref[...] = forcing_ref[:, pl.ds(first, cells), :]


def cut(here, forcing, parts):
    share, length, levels = forcing.shape
    return call(cut_kernel, [SMEM, VMEM], [shape(share, length // parts, levels)] * parts, 1)(
        here, forcing
    )


def assemble_kernel(code_ref, *refs):
    *part_refs, whole_ref = refs
    cells = part_refs[0].shape[1]
    for turn, part_ref in enumerate(part_refs):
        first = pl.multiple_of((code_ref[0] ^ turn) * cells, cells)
        whole_ref[:, pl.ds(first, cells), :] = part_ref[...]


def assemble(here, parts):
    share, cells, levels = parts[0].shape
    return call(
        assemble_kernel, [SMEM] + [VMEM] * len(parts), shape(share, len(parts) * cells, levels), 1
    )(here, *parts)


def states_kernel(code_ref, upstream_ref, blocks_ref, *refs):
    *part_refs, trial_ref, states_ref, forcing_ref = refs
    share = part_refs[0].shape[0]
    for turn, part_ref in enumerate(part_refs):
        forcing_ref[pl.ds((code_ref[0] ^ turn) * share, share)] = part_ref[...]
    states_ref[...] = jnp.zeros_like(states_ref)

    @pl.loop(0, blocks_ref.shape[0])
    def _(cell):
        forced = forcing_ref[:, cell, :] - upstream_ref[pl.ds(cell, 1), :] * states_ref[...]
        state = dot(forced, blocks_ref[cell])
        states_ref[...] = state
        trial_ref[cell] = state


def trial_states(here, blocks, upstream, parts):
    cells, levels, _ = blocks.shape
    lines = len(parts) * parts[0].shape[0]
    return call(
        states_kernel,
        [SMEM] + [VMEM] * (2 + len(parts)),
        [shape(cells, lines, levels), shape(lines, levels)],
        12 * cells * lines * levels**2,
        [pltpu.VMEM((lines, cells, levels), F32)],
    )(here, upstream, blocks, *parts)


def later(code_ref, then, otherwise):
    upper = lax.rem(code_ref[0], 2)
    pl.when(upper == 1)(then)
    pl.when(upper == 0)(otherwise)


def merge_states_kernel(code_ref, mine_ref, theirs_ref, my_map_ref, their_map_ref, out_ref):
    def then():
        out_ref[...] = move_states(theirs_ref[...], my_map_ref) + mine_ref[...]

    def otherwise():
        out_ref[...] = move_states(mine_ref[...], their_map_ref) + theirs_ref[...]

    later(code_ref, then, otherwise)


def merge_states(code, mine, theirs, my_map, their_map):
    lines, levels = mine.shape
    return call(
        merge_states_kernel, [SMEM] + [VMEM] * 4, shape(lines, levels), 12 * lines * levels**2
    )(code, mine, theirs, my_map, their_map)


def merge_kernel(start, kind, apart, halves, half, code_ref, *refs):
    refs = list(refs)
    mine_map = refs.pop(0)
    if apart and kind != "maps":
        mine_states = refs.pop(0)
    else:
        mine_states = None if kind == "maps" else mine_map.at[start:]
    here = refs.pop(0)
    there = refs.pop(0) if halves else None
    their_states = refs.pop(0) if apart and kind != "maps" else None
    out = refs.pop(0)
    core = code_ref[0] // 2
    their_map = here
    if halves:
        their_map = refs.pop(0)
        rows = here.shape[0]

        @pl.when(core == 0)
        def _():
            their_map[:rows] = here[...]
            their_map[rows:] = there[...]

        @pl.when(core == 1)
        def _():
            their_map[:rows] = there[...]
            their_map[rows:] = here[...]

    if their_states is None and kind != "maps":
        their_states = their_map.at[start:]

    def joined(left_map, left_states, right_map, right_states):
        if kind != "states":
            join_maps(left_map, right_map, out)
        if kind == "maps":
            return
        states = move_states(left_states[...], right_map) + right_states[...]
        if kind == "both":
            out[start:] = states
        else:
            out[...] = states

    later(
        code_ref,
        lambda: joined(their_map, their_states, mine_map, mine_states),
        lambda: joined(mine_map, mine_states, their_map, their_states),
    )
    if half:
        half_ref = refs.pop(0)
        rows = half_ref.shape[0]

        @pl.when(core == 0)
        def _():
            half_ref[...] = out[:rows]

        @pl.when(core == 1)
        def _():
            half_ref[...] = out[rows:]


def merge(code, mine, theirs, kind, lines, apart, halves, half):
    levels = mine[0].shape[1]
    start = levels + PAD
    rows = {"maps": start, "both": start + lines, "states": lines}[kind]
    out = [shape(rows, levels)]
    if halves:
        out.append(shape(2 * theirs[0].shape[0], levels))
    if half:
        out.append(shape(rows // 2, levels))
    operands = (*mine, *theirs)
    got = call(
        functools.partial(merge_kernel, start, kind, apart, halves, half),
        [SMEM] + [VMEM] * len(operands),
        out,
        12 * rows * levels**2,
    )(code, *operands)
    return got[0], got[1] if halves else theirs[0], got[-1]


def join(left_ref, right_ref, out_ref):
    start = out_ref.shape[1] + PAD
    join_maps(left_ref, right_ref, out_ref)
    out_ref[start:] = move_states(left_ref[start:], right_ref) + right_ref[start:]


def four_kernel(
    code_ref, mine_ref, here_ref, there_ref, this_ref, that_ref,
    total_ref, beside_ref, front_ref, half_ref, four_ref,
):
    core = lax.rem(code_ref[0], 2)
    place = code_ref[0] // 2
    rows = half_ref.shape[0]
    four_ref[place] = mine_ref[...]
    four_ref[place ^ (1 + core)] = here_ref[...]
    four_ref[place ^ (2 - core)] = there_ref[...]
    four_ref[place ^ 3, pl.ds(core * rows, rows)] = this_ref[...]
    four_ref[place ^ 3, pl.ds((1 - core) * rows, rows)] = that_ref[...]

    @pl.loop(0, 3)
    def _(turn):
        join(four_ref.at[2 * turn], four_ref.at[2 * turn + 1], four_ref.at[4 + turn])

    front_ref[...] = four_ref[4]
    total_ref[...] = four_ref[6]
    half_ref[...] = four_ref[6, pl.ds(core * rows, rows)]
    beside_ref[...] = four_ref[place ^ 1]


def join_four(code, mine, here, there, this, that):
    rows, levels = mine.shape
    whole = shape(rows, levels)
    return call(
        four_kernel,
        [SMEM] + [VMEM] * 5,
        [whole, whole, whole, shape(rows // 2, levels)],
        36 * rows * levels**2,
        [pltpu.VMEM((7, rows, levels), F32)],
    )(code, mine, here, there, this, that)


def extend_kernel(first, apart, code_ref, *refs):
    refs = list(refs)
    their_map = refs.pop(0)
    levels = their_map.shape[1]
    start = levels + PAD
    their_states = refs.pop(0)[...] if apart else their_map[start:]
    if first:
        (ahead_ref,) = refs
    else:
        before_ref, ahead_ref = refs

    def then():
        if first:
            ahead_ref[:start] = their_map[:start]
            ahead_ref[start:] = their_states
        else:
            join_maps(their_map, before_ref, ahead_ref)
            ahead_ref[start:] = move_states(their_states, before_ref) + before_ref[start:]

    def otherwise():
        if first:
            row = lax.broadcasted_iota(jnp.int32, ahead_ref.shape, 0)
            column = lax.broadcasted_iota(jnp.int32, ahead_ref.shape, 1)
            ahead_ref[...] = jnp.where(row == column, 1.0, 0.0).astype(F32)
        else:
            ahead_ref[...] = before_ref[...]

    later(code_ref, then, otherwise)


def extend(code, theirs, before):
    levels = theirs[0].shape[1]
    apart = len(theirs) == 2
    rows = levels + PAD + (theirs[1].shape[0] if apart else theirs[0].shape[0] - levels - PAD)
    first = before is None
    operands = theirs if first else (*theirs, before)
    return call(
        functools.partial(extend_kernel, first, apart),
        [SMEM] + [VMEM] * len(operands),
        shape(rows, levels),
        12 * rows * levels**2,
    )(code, *operands)


def enter_kernel(from_ref, map_ref, own_ref, out_ref):
    out_ref[...] = move_states(from_ref[...], map_ref) + own_ref[...]


def enter(states, total, own):
    lines, levels = own.shape
    return call(enter_kernel, [VMEM] * 3, shape(lines, levels), 12 * lines * levels**2)(
        states, total, own
    )


def plane_total_kernel(code_ref, mine_ref, theirs_ref, total_ref):
    @pl.when(code_ref[0] < 4)
    def _():
        total_ref[...] = jnp.zeros_like(total_ref)

    @pl.when(code_ref[0] >= 4)
    def _():
        later(
            code_ref,
            lambda: join(theirs_ref, mine_ref, total_ref),
            lambda: join(mine_ref, theirs_ref, total_ref),
        )


def plane_total(code, mine, theirs):
    rows, levels = mine.shape
    return call(
        plane_total_kernel, [SMEM, VMEM, VMEM], shape(rows, levels), 12 * rows * levels**2
    )(code, mine, theirs)


def settle_planes_kernel(code_ref, beside_ref, from_ref, before_ref, ahead_ref):
    start = before_ref.shape[1] + PAD

    def then():
        join_maps(beside_ref, before_ref, ahead_ref)
        ahead_ref[start:] = move_states(beside_ref[start:], before_ref) + before_ref[start:]

    def otherwise():
        ahead_ref[:start] = before_ref[:start]
        ahead_ref[start:] = move_states(from_ref[...], before_ref) + before_ref[start:]

    later(code_ref, then, otherwise)


def settle_planes(code, beside, from_first, before):
    rows, levels = before.shape
    return call(
        settle_planes_kernel, [SMEM] + [VMEM] * 3, shape(rows, levels), 12 * rows * levels**2
    )(code, beside, from_first, before)


def finish_kernel(code_ref, one_ref, two_ref, before_ref, prefix_ref, trial_ref, *refs):
    *part_refs, solved_ref, held_ref, incoming, arrived = refs
    fetch(prefix_ref, held_ref, arrived)
    start = before_ref.shape[1] + PAD
    entering = one_ref[...] + two_ref[...]
    high, low = split(move_states(entering, before_ref) + before_ref[start:])
    lines = high.shape[0]
    incoming[:lines] = high
    incoming[lines:] = low
    product = functools.partial(jnp.dot, preferred_element_type=F32)

    @pl.loop(0, held_ref.shape[0])
    def _(cell):
        block_copy(prefix_ref, held_ref, arrived, cell).wait()
        map_high, map_low = split(held_ref[cell])
        both = product(incoming[...], map_high)
        rest = both[lines:] + product(incoming[:lines], map_low)
        solved_ref[:, cell, :] = trial_ref[cell] + (both[:lines] + rest)

    share = part_refs[0].shape[0]
    for turn, part_ref in enumerate(part_refs):
        part_ref[...] = solved_ref[pl.ds((code_ref[0] ^ turn) * share, share)]


def finish(here, entering, before, prefix, trial, parts):
    cells, lines, levels = trial.shape
    return call(
        finish_kernel,
        [SMEM, VMEM, VMEM, VMEM, HBM, VMEM],
        [shape(lines // parts, cells, levels)] * parts,
        12 * (cells + 1) * lines * levels**2,
        [
            pltpu.VMEM((lines, cells, levels), F32),
            pltpu.VMEM(prefix.shape, F32),
            pltpu.VMEM((2 * lines, levels), jnp.bfloat16),
            pltpu.SemaphoreType.DMA((cells,)),
        ],
        None,
        LARGE,
    )(here, *entering, before, prefix, trial)


def shards(span_count, forcing, blocks, upstream):
    cells, levels, _ = blocks.shape
    share = forcing.shape[0]
    lines = share * span_count
    here = lax.axis_index("span").astype(jnp.int32).reshape(1)

    def trade(parts):
        kept, *sent = parts
        return [kept] + [partner(part, "span", k + 1) for k, part in enumerate(sent)]

    def partner(value, axis, mask):
        count = lax.axis_size(axis)
        return lax.ppermute(value, axis, [(i, i ^ mask) for i in range(count)])

    forcing_parts = trade(cut(here, forcing, span_count))
    prefix, maps = prefix_maps(blocks, upstream)
    forcing_parts, maps = lax.optimization_barrier((forcing_parts, maps))
    trial, states = trial_states(here, blocks, upstream, forcing_parts)

    def code_of(axis, bit):
        upper = jnp.where((lax.axis_index(axis) & bit) != 0, 1, 0)
        core = jnp.where((lax.axis_index("line") & CORE) != 0, 2, 0)
        return (upper + core).astype(jnp.int32).reshape(1)

    def along_four(total, half, before):
        device = lax.axis_index("line")
        pairs = [(i, i ^ FOUR[i & CORE]) for i in range(lax.axis_size("line"))]
        here, this = lax.ppermute(total, "line", pairs), partner(half, "line", THIRD)
        here, this, before = lax.optimization_barrier((here, this, before))
        there, that = partner(here, "line", CORE), partner(this, "line", CORE)
        code = (device & (CORE | THIRD)).astype(jnp.int32).reshape(1)
        total, beside, front, half = join_four(code, total, here, there, this, that)
        before = extend(code_of("line", FOUR[0]), (beside,), before)
        before = extend(code_of("line", FOUR[1]), (front,), before)
        return total, half, before

    total, half, before = None, None, None
    for turn, (axis, mask, bit, halves, apart) in enumerate(ROUNDS):
        code = code_of(axis, bit)
        last = turn == len(ROUNDS) - 1
        if halves:
            mine_half = partner(half, axis, mask)
            mine_half, before = lax.optimization_barrier((mine_half, before))
            theirs = (mine_half, partner(mine_half, "line", CORE))
        else:
            theirs = (partner(maps if apart else total, axis, mask),)
            if before is not None:
                theirs, before = lax.optimization_barrier((theirs, before))
        mine = (total,)
        if apart:
            their_states = partner(states, axis, mask)
            mine, theirs = (maps, states), (*theirs, their_states)
        if last:
            plane, whole, _ = merge(code, mine, theirs, "states", lines, apart, halves, False)
            inner = (lax.axis_index("line") // PLANE + 1) // 2 == 1
            total = plane_total(code + jnp.where(inner, 4, 0).astype(jnp.int32), total, whole)
        else:
            half_too = turn == len(ROUNDS) - 2
            total, whole, half = merge(code, mine, theirs, "both", lines, apart, halves, half_too)
        before = extend(code, (whole, their_states) if apart else (whole,), before)
        if turn == len(ROUNDS) - 2:
            total, half, before = along_four(total, half, before)

    def across(value, source, target):
        shift = (target - source) * PLANE
        pairs = [(i, i + shift) for i in range(source * PLANE, (source + 1) * PLANE)]
        return lax.ppermute(value, "line", pairs)

    from_first = across(plane, 0, 1)
    beside = across(total, 2, 3)
    from_first, before = lax.optimization_barrier((from_first, before))
    joined = enter(from_first, total, plane)
    two_on = across(joined, 1, 3)
    entering = (two_on, across(joined, 1, 2))
    in_last = jnp.where(lax.axis_index("line") >= 3 * PLANE, 1, 0).astype(jnp.int32).reshape(1)
    before = settle_planes(in_last, beside, from_first, before)
    return assemble(here, trade(finish(here, entering, before, prefix, trial, span_count)))


def solution(mesh):
    placed = (P("span", "line", None), P(("line", "span"), None, None), P(("line", "span"), None))
    return jax.shard_map(
        functools.partial(shards, mesh.shape["span"]),
        mesh=mesh,
        in_specs=placed,
        out_specs=P("span", "line", None),
        check_vma=False,
    )
```

```python
import functools

import jax
import jax.numpy as jnp
from jax import lax
from jax.experimental import pallas as pl
from jax.experimental.pallas import tpu as pltpu
from jax.sharding import PartitionSpec as P

F32 = jnp.float32
BIG = 2.0**40
STEP = 2.0**48
PAD = 16
VMEM = pl.BlockSpec(memory_space=pltpu.VMEM)
HBM = pl.BlockSpec(memory_space=pltpu.HBM)
LARGE = 52 * 2**20
SMEM = pl.BlockSpec(memory_space=pltpu.SMEM)
CORE = 1
ROUNDS = (
    ("span", 1, 1, False, True),
    ("span", 3, 2, False, False),
    ("line", 1, 1, False, False),
    ("line", 14, 8, True, False),
)
FOUR = (2, 4)
THIRD = 6
PLANE = 16


def dot(a, b):
    return jnp.dot(a, b, precision=lax.Precision.HIGHEST, preferred_element_type=F32)


def split(a):
    high = a.astype(jnp.bfloat16)
    return high, (a - high.astype(F32)).astype(jnp.bfloat16)


def dot3(a, b):
    product = functools.partial(jnp.dot, preferred_element_type=F32)
    (a_high, a_low), (b_high, b_low) = split(a), split(b)
    return product(a_high, b_high) + (product(a_high, b_low) + product(a_low, b_high))


def shape(*dims):
    return jax.ShapeDtypeStruct(dims, F32)


def call(kernel, in_specs, out_shape, flops, scratch=(), out_specs=None, vmem=8 * 2**20):
    return pl.pallas_call(
        kernel,
        in_specs=in_specs,
        out_specs=out_specs or jax.tree.map(lambda _: VMEM, out_shape),
        out_shape=out_shape,
        scratch_shapes=list(scratch),
        compiler_params=pltpu.CompilerParams(vmem_limit_bytes=vmem),
        cost_estimate=pl.CostEstimate(flops=flops, bytes_accessed=2**20, transcendentals=0),
    )


def settle(hat, count):
    large = jnp.max(jnp.abs(hat), keepdims=True) > BIG
    return hat * jnp.where(large, 1.0 / STEP, 1.0), count + jnp.where(large, 1.0, 0.0)


def unscale(value, count):
    for done in (0.0, 2.0, 4.0):
        left = count - done
        value = value * jnp.where(left > 1.5, STEP * STEP, jnp.where(left > 0.5, STEP, 1.0))
    return value


def put_map(hat, count, out_ref):
    levels = hat.shape[1]
    hat, count = settle(hat, count)
    out_ref[:levels] = hat
    out_ref[levels : levels + 8] = count
    out_ref[levels + 8 : levels + PAD] = jnp.zeros_like(count)


def join_maps(left_ref, right_ref, out_ref):
    levels = out_ref.shape[1]
    count = left_ref[levels : levels + 8] + right_ref[levels : levels + 8]
    put_map(dot3(left_ref[:levels], right_ref[:levels]), count, out_ref)


def move_states(states, map_ref):
    levels = map_ref.shape[1]
    return unscale(dot(states, map_ref[:levels]), map_ref[levels : levels + 1])


def block_copy(blocks_ref, held_ref, arrived, cell):
    return pltpu.make_async_copy(blocks_ref.at[cell], held_ref.at[cell], arrived.at[cell])


def fetch(blocks_ref, held_ref, arrived):
    @pl.loop(0, held_ref.shape[0])
    def _(cell):
        block_copy(blocks_ref, held_ref, arrived, cell).start()


def maps_kernel(
    upstream_ref, blocks_ref, prefix_ref, map_ref, held_ref, made_ref, last_ref, arrived, left
):
    cells, levels, _ = held_ref.shape
    fetch(blocks_ref, held_ref, arrived)
    row = lax.broadcasted_iota(jnp.int32, (levels, levels), 0)
    column = lax.broadcasted_iota(jnp.int32, (levels, levels), 1)
    first = jnp.where(row == column, -upstream_ref[0:1, :], 0.0)
    first = jnp.sum(first, axis=1, keepdims=True)
    block_copy(blocks_ref, held_ref, arrived, 0).wait()
    first = first * held_ref[0]
    last_ref[...] = first
    made_ref[0] = first
    block_copy(made_ref, prefix_ref, left, 0).start()

    @pl.loop(1, cells)
    def _(cell):
        scaled = last_ref[...] * -upstream_ref[pl.ds(cell, 1), :]
        block_copy(blocks_ref, held_ref, arrived, cell).wait()
        product = dot(scaled, held_ref[cell])
        last_ref[...] = product
        made_ref[cell] = product
        block_copy(made_ref, prefix_ref, left, cell).start()

    put_map(last_ref[...], jnp.zeros((8, levels), F32), map_ref)

    @pl.loop(0, cells)
    def _(cell):
        block_copy(made_ref, prefix_ref, left, cell).wait()


def prefix_maps(blocks, upstream):
    cells, levels, _ = blocks.shape
    return call(
        maps_kernel,
        [VMEM, HBM],
        [shape(*blocks.shape), shape(levels + PAD, levels)],
        12 * cells * levels**3,
        [
            pltpu.VMEM(blocks.shape, F32),
            pltpu.VMEM(blocks.shape, F32),
            pltpu.VMEM((levels, levels), F32),
            pltpu.SemaphoreType.DMA((cells,)),
            pltpu.SemaphoreType.DMA((cells,)),
        ],
        [HBM, VMEM],
        LARGE,
    )(upstream, blocks)


def cut_kernel(code_ref, forcing_ref, *part_refs):
    cells = part_refs[0].shape[1]
    for turn, part_ref in enumerate(part_refs):
        first = pl.multiple_of((code_ref[0] ^ turn) * cells, cells)
        part_ref[...] = forcing_ref[:, pl.ds(first, cells), :]


def cut(here, forcing, parts):
    share, length, levels = forcing.shape
    return call(cut_kernel, [SMEM, VMEM], [shape(share, length // parts, levels)] * parts, 1)(
        here, forcing
    )


def assemble_kernel(code_ref, *refs):
    *part_refs, whole_ref = refs
    cells = part_refs[0].shape[1]
    for turn, part_ref in enumerate(part_refs):
        first = pl.multiple_of((code_ref[0] ^ turn) * cells, cells)
        whole_ref[:, pl.ds(first, cells), :] = part_ref[...]


def assemble(here, parts):
    share, cells, levels = parts[0].shape
    return call(
        assemble_kernel, [SMEM] + [VMEM] * len(parts), shape(share, len(parts) * cells, levels), 1
    )(here, *parts)


def states_kernel(code_ref, upstream_ref, blocks_ref, *refs):
    *part_refs, trial_ref, states_ref, forcing_ref = refs
    share = part_refs[0].shape[0]
    for turn, part_ref in enumerate(part_refs):
        forcing_ref[pl.ds((code_ref[0] ^ turn) * share, share)] = part_ref[...]
    states_ref[...] = jnp.zeros_like(states_ref)

    @pl.loop(0, blocks_ref.shape[0])
    def _(cell):
        forced = forcing_ref[:, cell, :] - upstream_ref[pl.ds(cell, 1), :] * states_ref[...]
        state = dot(forced, blocks_ref[cell])
        states_ref[...] = state
        trial_ref[cell] = state


def trial_states(here, blocks, upstream, parts):
    cells, levels, _ = blocks.shape
    lines = len(parts) * parts[0].shape[0]
    return call(
        states_kernel,
        [SMEM] + [VMEM] * (2 + len(parts)),
        [shape(cells, lines, levels), shape(lines, levels)],
        12 * cells * lines * levels**2,
        [pltpu.VMEM((lines, cells, levels), F32)],
    )(here, upstream, blocks, *parts)


def later(code_ref, then, otherwise):
    upper = lax.rem(code_ref[0], 2)
    pl.when(upper == 1)(then)
    pl.when(upper == 0)(otherwise)


def merge_states_kernel(code_ref, mine_ref, theirs_ref, my_map_ref, their_map_ref, out_ref):
    def then():
        out_ref[...] = move_states(theirs_ref[...], my_map_ref) + mine_ref[...]

    def otherwise():
        out_ref[...] = move_states(mine_ref[...], their_map_ref) + theirs_ref[...]

    later(code_ref, then, otherwise)


def merge_states(code, mine, theirs, my_map, their_map):
    lines, levels = mine.shape
    return call(
        merge_states_kernel, [SMEM] + [VMEM] * 4, shape(lines, levels), 12 * lines * levels**2
    )(code, mine, theirs, my_map, their_map)


def merge_kernel(start, kind, apart, halves, half, code_ref, *refs):
    refs = list(refs)
    mine_map = refs.pop(0)
    if apart and kind != "maps":
        mine_states = refs.pop(0)
    else:
        mine_states = None if kind == "maps" else mine_map.at[start:]
    here = refs.pop(0)
    there = refs.pop(0) if halves else None
    their_states = refs.pop(0) if apart and kind != "maps" else None
    out = refs.pop(0)
    core = code_ref[0] // 2
    their_map = here
    if halves:
        their_map = refs.pop(0)
        rows = here.shape[0]

        @pl.when(core == 0)
        def _():
            their_map[:rows] = here[...]
            their_map[rows:] = there[...]

        @pl.when(core == 1)
        def _():
            their_map[:rows] = there[...]
            their_map[rows:] = here[...]

    if their_states is None and kind != "maps":
        their_states = their_map.at[start:]

    def joined(left_map, left_states, right_map, right_states):
        if kind != "states":
            join_maps(left_map, right_map, out)
        if kind == "maps":
            return
        states = move_states(left_states[...], right_map) + right_states[...]
        if kind == "both":
            out[start:] = states
        else:
            out[...] = states

    later(
        code_ref,
        lambda: joined(their_map, their_states, mine_map, mine_states),
        lambda: joined(mine_map, mine_states, their_map, their_states),
    )
    if half:
        half_ref = refs.pop(0)
        rows = half_ref.shape[0]

        @pl.when(core == 0)
        def _():
            half_ref[...] = out[:rows]

        @pl.when(core == 1)
        def _():
            half_ref[...] = out[rows:]


def merge(code, mine, theirs, kind, lines, apart, halves, half):
    levels = mine[0].shape[1]
    start = levels + PAD
    rows = {"maps": start, "both": start + lines, "states": lines}[kind]
    out = [shape(rows, levels)]
    if halves:
        out.append(shape(2 * theirs[0].shape[0], levels))
    if half:
        out.append(shape(rows // 2, levels))
    operands = (*mine, *theirs)
    got = call(
        functools.partial(merge_kernel, start, kind, apart, halves, half),
        [SMEM] + [VMEM] * len(operands),
        out,
        12 * rows * levels**2,
    )(code, *operands)
    return got[0], got[1] if halves else theirs[0], got[-1]


def join(left_ref, right_ref, out_ref):
    start = out_ref.shape[1] + PAD
    join_maps(left_ref, right_ref, out_ref)
    out_ref[start:] = move_states(left_ref[start:], right_ref) + right_ref[start:]


def four_kernel(
    code_ref, mine_ref, here_ref, there_ref, this_ref, that_ref,
    total_ref, beside_ref, front_ref, half_ref, four_ref, back_ref,
):
    core = lax.rem(code_ref[0], 2)
    place = code_ref[0] // 2
    rows = half_ref.shape[0]
    four_ref[place] = mine_ref[...]
    four_ref[place ^ (1 + core)] = here_ref[...]
    four_ref[place ^ (2 - core)] = there_ref[...]
    four_ref[place ^ 3, pl.ds(core * rows, rows)] = this_ref[...]
    four_ref[place ^ 3, pl.ds((1 - core) * rows, rows)] = that_ref[...]
    join(four_ref.at[0], four_ref.at[1], front_ref)
    join(four_ref.at[2], four_ref.at[3], back_ref)
    join(front_ref, back_ref, total_ref)
    half_ref[...] = total_ref[pl.ds(core * rows, rows)]
    beside_ref[...] = four_ref[place ^ 1]


def join_four(code, mine, here, there, this, that):
    rows, levels = mine.shape
    whole = shape(rows, levels)
    return call(
        four_kernel,
        [SMEM] + [VMEM] * 5,
        [whole, whole, whole, shape(rows // 2, levels)],
        36 * rows * levels**2,
        [pltpu.VMEM((4, rows, levels), F32), pltpu.VMEM((rows, levels), F32)],
    )(code, mine, here, there, this, that)


def extend_kernel(first, apart, code_ref, *refs):
    refs = list(refs)
    their_map = refs.pop(0)
    levels = their_map.shape[1]
    start = levels + PAD
    their_states = refs.pop(0)[...] if apart else their_map[start:]
    if first:
        (ahead_ref,) = refs
    else:
        before_ref, ahead_ref = refs

    def then():
        if first:
            ahead_ref[:start] = their_map[:start]
            ahead_ref[start:] = their_states
        else:
            join_maps(their_map, before_ref, ahead_ref)
            ahead_ref[start:] = move_states(their_states, before_ref) + before_ref[start:]

    def otherwise():
        if first:
            row = lax.broadcasted_iota(jnp.int32, ahead_ref.shape, 0)
            column = lax.broadcasted_iota(jnp.int32, ahead_ref.shape, 1)
            ahead_ref[...] = jnp.where(row == column, 1.0, 0.0).astype(F32)
        else:
            ahead_ref[...] = before_ref[...]

    later(code_ref, then, otherwise)


def extend(code, theirs, before):
    levels = theirs[0].shape[1]
    apart = len(theirs) == 2
    rows = levels + PAD + (theirs[1].shape[0] if apart else theirs[0].shape[0] - levels - PAD)
    first = before is None
    operands = theirs if first else (*theirs, before)
    return call(
        functools.partial(extend_kernel, first, apart),
        [SMEM] + [VMEM] * len(operands),
        shape(rows, levels),
        12 * rows * levels**2,
    )(code, *operands)


def enter_kernel(from_ref, map_ref, own_ref, out_ref):
    out_ref[...] = move_states(from_ref[...], map_ref) + own_ref[...]


def enter(states, total, own):
    lines, levels = own.shape
    return call(enter_kernel, [VMEM] * 3, shape(lines, levels), 12 * lines * levels**2)(
        states, total, own
    )


def plane_total_kernel(code_ref, mine_ref, theirs_ref, total_ref):
    @pl.when(code_ref[0] < 4)
    def _():
        total_ref[...] = jnp.zeros_like(total_ref)

    @pl.when(code_ref[0] >= 4)
    def _():
        later(
            code_ref,
            lambda: join(theirs_ref, mine_ref, total_ref),
            lambda: join(mine_ref, theirs_ref, total_ref),
        )


def plane_total(code, mine, theirs):
    rows, levels = mine.shape
    return call(
        plane_total_kernel, [SMEM, VMEM, VMEM], shape(rows, levels), 12 * rows * levels**2
    )(code, mine, theirs)


def settle_planes_kernel(code_ref, beside_ref, from_ref, before_ref, ahead_ref):
    start = before_ref.shape[1] + PAD

    def then():
        join_maps(beside_ref, before_ref, ahead_ref)
        ahead_ref[start:] = move_states(beside_ref[start:], before_ref) + before_ref[start:]

    def otherwise():
        ahead_ref[:start] = before_ref[:start]
        ahead_ref[start:] = move_states(from_ref[...], before_ref) + before_ref[start:]

    later(code_ref, then, otherwise)


def settle_planes(code, beside, from_first, before):
    rows, levels = before.shape
    return call(
        settle_planes_kernel, [SMEM] + [VMEM] * 3, shape(rows, levels), 12 * rows * levels**2
    )(code, beside, from_first, before)


def finish_kernel(code_ref, one_ref, two_ref, before_ref, prefix_ref, trial_ref, *refs):
    *part_refs, solved_ref, held_ref, incoming, arrived = refs
    fetch(prefix_ref, held_ref, arrived)
    start = before_ref.shape[1] + PAD
    entering = one_ref[...] + two_ref[...]
    high, low = split(move_states(entering, before_ref) + before_ref[start:])
    lines = high.shape[0]
    incoming[:lines] = high
    incoming[lines:] = low
    product = functools.partial(jnp.dot, preferred_element_type=F32)

    @pl.loop(0, held_ref.shape[0])
    def _(cell):
        block_copy(prefix_ref, held_ref, arrived, cell).wait()
        map_high, map_low = split(held_ref[cell])
        both = product(incoming[...], map_high)
        rest = both[lines:] + product(incoming[:lines], map_low)
        solved_ref[:, cell, :] = trial_ref[cell] + (both[:lines] + rest)

    share = part_refs[0].shape[0]
    for turn, part_ref in enumerate(part_refs):
        part_ref[...] = solved_ref[pl.ds((code_ref[0] ^ turn) * share, share)]


def finish(here, entering, before, prefix, trial, parts):
    cells, lines, levels = trial.shape
    return call(
        finish_kernel,
        [SMEM, VMEM, VMEM, VMEM, HBM, VMEM],
        [shape(lines // parts, cells, levels)] * parts,
        12 * (cells + 1) * lines * levels**2,
        [
            pltpu.VMEM((lines, cells, levels), F32),
            pltpu.VMEM(prefix.shape, F32),
            pltpu.VMEM((2 * lines, levels), jnp.bfloat16),
            pltpu.SemaphoreType.DMA((cells,)),
        ],
        None,
        LARGE,
    )(here, *entering, before, prefix, trial)


def shards(span_count, forcing, blocks, upstream):
    cells, levels, _ = blocks.shape
    share = forcing.shape[0]
    lines = share * span_count
    here = lax.axis_index("span").astype(jnp.int32).reshape(1)

    def trade(parts):
        kept, *sent = parts
        return [kept] + [partner(part, "span", k + 1) for k, part in enumerate(sent)]

    def partner(value, axis, mask):
        count = lax.axis_size(axis)
        return lax.ppermute(value, axis, [(i, i ^ mask) for i in range(count)])

    forcing_parts = trade(cut(here, forcing, span_count))
    prefix, maps = prefix_maps(blocks, upstream)
    forcing_parts, maps = lax.optimization_barrier((forcing_parts, maps))
    trial, states = trial_states(here, blocks, upstream, forcing_parts)

    def code_of(axis, bit):
        upper = jnp.where((lax.axis_index(axis) & bit) != 0, 1, 0)
        core = jnp.where((lax.axis_index("line") & CORE) != 0, 2, 0)
        return (upper + core).astype(jnp.int32).reshape(1)

    def along_four(total, half, before):
        device = lax.axis_index("line")
        pairs = [(i, i ^ FOUR[i & CORE]) for i in range(lax.axis_size("line"))]
        here, this = lax.ppermute(total, "line", pairs), partner(half, "line", THIRD)
        here, this, before = lax.optimization_barrier((here, this, before))
        there, that = partner(here, "line", CORE), partner(this, "line", CORE)
        code = (device & (CORE | THIRD)).astype(jnp.int32).reshape(1)
        total, beside, front, half = join_four(code, total, here, there, this, that)
        before = extend(code_of("line", FOUR[0]), (beside,), before)
        before = extend(code_of("line", FOUR[1]), (front,), before)
        return total, half, before

    total, half, before = None, None, None
    for turn, (axis, mask, bit, halves, apart) in enumerate(ROUNDS):
        code = code_of(axis, bit)
        last = turn == len(ROUNDS) - 1
        if halves:
            mine_half = partner(half, axis, mask)
            mine_half, before = lax.optimization_barrier((mine_half, before))
            theirs = (mine_half, partner(mine_half, "line", CORE))
        else:
            theirs = (partner(maps if apart else total, axis, mask),)
            if before is not None:
                theirs, before = lax.optimization_barrier((theirs, before))
        mine = (total,)
        if apart:
            their_states = partner(states, axis, mask)
            mine, theirs = (maps, states), (*theirs, their_states)
        if last:
            plane, whole, _ = merge(code, mine, theirs, "states", lines, apart, halves, False)
            inner = (lax.axis_index("line") // PLANE + 1) // 2 == 1
            total = plane_total(code + jnp.where(inner, 4, 0).astype(jnp.int32), total, whole)
        else:
            half_too = turn == len(ROUNDS) - 2
            total, whole, half = merge(code, mine, theirs, "both", lines, apart, halves, half_too)
        before = extend(code, (whole, their_states) if apart else (whole,), before)
        if turn == len(ROUNDS) - 2:
            total, half, before = along_four(total, half, before)

    def across(value, source, target):
        shift = (target - source) * PLANE
        pairs = [(i, i + shift) for i in range(source * PLANE, (source + 1) * PLANE)]
        return lax.ppermute(value, "line", pairs)

    from_first = across(plane, 0, 1)
    beside = across(total, 2, 3)
    from_first, before = lax.optimization_barrier((from_first, before))
    joined = enter(from_first, total, plane)
    two_on = across(joined, 1, 3)
    entering = (two_on, across(joined, 1, 2))
    in_last = jnp.where(lax.axis_index("line") >= 3 * PLANE, 1, 0).astype(jnp.int32).reshape(1)
    before = settle_planes(in_last, beside, from_first, before)
    return assemble(here, trade(finish(here, entering, before, prefix, trial, span_count)))


def solution(mesh):
    placed = (P("span", "line", None), P(("line", "span"), None, None), P(("line", "span"), None))
    return jax.shard_map(
        functools.partial(shards, mesh.shape["span"]),
        mesh=mesh,
        in_specs=placed,
        out_specs=P("span", "line", None),
        check_vma=False,
    )
```

```python
import functools

import jax
import jax.numpy as jnp
from jax import lax
from jax.experimental import pallas as pl
from jax.experimental.pallas import tpu as pltpu
from jax.sharding import PartitionSpec as P

F32 = jnp.float32
BIG = 2.0**40
STEP = 2.0**48
PAD = 16
VMEM = pl.BlockSpec(memory_space=pltpu.VMEM)
HBM = pl.BlockSpec(memory_space=pltpu.HBM)
LARGE = 52 * 2**20
SMEM = pl.BlockSpec(memory_space=pltpu.SMEM)
CORE = 1
ROUNDS = (
    ("span", 1, 1, False, True),
    ("span", 3, 2, False, False),
    ("line", 1, 1, False, False),
    ("line", 14, 8, True, False),
)
FOUR = (2, 4)
THIRD = 6
PLANE = 16


def dot(a, b):
    return jnp.dot(a, b, precision=lax.Precision.HIGHEST, preferred_element_type=F32)


def split(a):
    high = a.astype(jnp.bfloat16)
    return high, (a - high.astype(F32)).astype(jnp.bfloat16)


def dot3(a, b):
    product = functools.partial(jnp.dot, preferred_element_type=F32)
    (a_high, a_low), (b_high, b_low) = split(a), split(b)
    return product(a_high, b_high) + (product(a_high, b_low) + product(a_low, b_high))


def shape(*dims):
    return jax.ShapeDtypeStruct(dims, F32)


def call(kernel, in_specs, out_shape, flops, scratch=(), out_specs=None, vmem=8 * 2**20):
    return pl.pallas_call(
        kernel,
        in_specs=in_specs,
        out_specs=out_specs or jax.tree.map(lambda _: VMEM, out_shape),
        out_shape=out_shape,
        scratch_shapes=list(scratch),
        compiler_params=pltpu.CompilerParams(vmem_limit_bytes=vmem),
        cost_estimate=pl.CostEstimate(flops=flops, bytes_accessed=2**20, transcendentals=0),
    )


def settle(hat, count):
    large = jnp.max(jnp.abs(hat), keepdims=True) > BIG
    return hat * jnp.where(large, 1.0 / STEP, 1.0), count + jnp.where(large, 1.0, 0.0)


def unscale(value, count):
    for done in (0.0, 2.0, 4.0):
        left = count - done
        value = value * jnp.where(left > 1.5, STEP * STEP, jnp.where(left > 0.5, STEP, 1.0))
    return value


def put_map(hat, count, out_ref):
    levels = hat.shape[1]
    hat, count = settle(hat, count)
    out_ref[:levels] = hat
    out_ref[levels : levels + 8] = count
    out_ref[levels + 8 : levels + PAD] = jnp.zeros_like(count)


def join_maps(left_ref, right_ref, out_ref):
    levels = out_ref.shape[1]
    count = left_ref[levels : levels + 8] + right_ref[levels : levels + 8]
    put_map(dot3(left_ref[:levels], right_ref[:levels]), count, out_ref)


def move_states(states, map_ref):
    levels = map_ref.shape[1]
    return unscale(dot3(states, map_ref[:levels]), map_ref[levels : levels + 1])


def join(left_ref, right_ref, out_ref):
    levels = out_ref.shape[1]
    start = levels + PAD
    both = dot3(left_ref[...], right_ref[:levels])
    count = left_ref[levels : levels + 8] + right_ref[levels : levels + 8]
    put_map(both[:levels], count, out_ref)
    out_ref[start:] = unscale(both[start:], right_ref[levels : levels + 1]) + right_ref[start:]


def block_copy(blocks_ref, held_ref, arrived, cell):
    return pltpu.make_async_copy(blocks_ref.at[cell], held_ref.at[cell], arrived.at[cell])


def fetch(blocks_ref, held_ref, arrived):
    @pl.loop(0, held_ref.shape[0])
    def _(cell):
        block_copy(blocks_ref, held_ref, arrived, cell).start()


def maps_kernel(
    upstream_ref, blocks_ref, prefix_ref, map_ref, held_ref, made_ref, last_ref, arrived, left
):
    cells, levels, _ = held_ref.shape
    fetch(blocks_ref, held_ref, arrived)
    row = lax.broadcasted_iota(jnp.int32, (levels, levels), 0)
    column = lax.broadcasted_iota(jnp.int32, (levels, levels), 1)
    first = jnp.where(row == column, -upstream_ref[0:1, :], 0.0)
    first = jnp.sum(first, axis=1, keepdims=True)
    block_copy(blocks_ref, held_ref, arrived, 0).wait()
    first = first * held_ref[0]
    last_ref[...] = first
    made_ref[0] = first
    block_copy(made_ref, prefix_ref, left, 0).start()

    @pl.loop(1, cells)
    def _(cell):
        scaled = last_ref[...] * -upstream_ref[pl.ds(cell, 1), :]
        block_copy(blocks_ref, held_ref, arrived, cell).wait()
        product = dot(scaled, held_ref[cell])
        last_ref[...] = product
        made_ref[cell] = product
        block_copy(made_ref, prefix_ref, left, cell).start()

    put_map(last_ref[...], jnp.zeros((8, levels), F32), map_ref)

    @pl.loop(0, cells)
    def _(cell):
        block_copy(made_ref, prefix_ref, left, cell).wait()


def prefix_maps(blocks, upstream):
    cells, levels, _ = blocks.shape
    return call(
        maps_kernel,
        [VMEM, HBM],
        [shape(*blocks.shape), shape(levels + PAD, levels)],
        12 * cells * levels**3,
        [
            pltpu.VMEM(blocks.shape, F32),
            pltpu.VMEM(blocks.shape, F32),
            pltpu.VMEM((levels, levels), F32),
            pltpu.SemaphoreType.DMA((cells,)),
            pltpu.SemaphoreType.DMA((cells,)),
        ],
        [HBM, VMEM],
        LARGE,
    )(upstream, blocks)


def cut_kernel(code_ref, forcing_ref, *part_refs):
    cells = part_refs[0].shape[1]
    for turn, part_ref in enumerate(part_refs):
        first = pl.multiple_of((code_ref[0] ^ turn) * cells, cells)
        part_ref[...] = forcing_ref[:, pl.ds(first, cells), :]


def cut(here, forcing, parts):
    share, length, levels = forcing.shape
    return call(cut_kernel, [SMEM, VMEM], [shape(share, length // parts, levels)] * parts, 1)(
        here, forcing
    )


def assemble_kernel(code_ref, *refs):
    *part_refs, whole_ref = refs
    cells = part_refs[0].shape[1]
    for turn, part_ref in enumerate(part_refs):
        first = pl.multiple_of((code_ref[0] ^ turn) * cells, cells)
        whole_ref[:, pl.ds(first, cells), :] = part_ref[...]


def assemble(here, parts):
    share, cells, levels = parts[0].shape
    return call(
        assemble_kernel, [SMEM] + [VMEM] * len(parts), shape(share, len(parts) * cells, levels), 1
    )(here, *parts)


def states_kernel(code_ref, upstream_ref, blocks_ref, *refs):
    *part_refs, trial_ref, states_ref, forcing_ref = refs
    share = part_refs[0].shape[0]
    for turn, part_ref in enumerate(part_refs):
        forcing_ref[pl.ds((code_ref[0] ^ turn) * share, share)] = part_ref[...]
    states_ref[...] = jnp.zeros_like(states_ref)

    @pl.loop(0, blocks_ref.shape[0])
    def _(cell):
        forced = forcing_ref[:, cell, :] - upstream_ref[pl.ds(cell, 1), :] * states_ref[...]
        state = dot3(forced, blocks_ref[cell])
        states_ref[...] = state
        trial_ref[cell] = state


def trial_states(here, blocks, upstream, parts):
    cells, levels, _ = blocks.shape
    lines = len(parts) * parts[0].shape[0]
    return call(
        states_kernel,
        [SMEM] + [VMEM] * (2 + len(parts)),
        [shape(cells, lines, levels), shape(lines, levels)],
        12 * cells * lines * levels**2,
        [pltpu.VMEM((lines, cells, levels), F32)],
    )(here, upstream, blocks, *parts)


def later(code_ref, then, otherwise):
    upper = lax.rem(code_ref[0], 2)
    pl.when(upper == 1)(then)
    pl.when(upper == 0)(otherwise)


def merge_states_kernel(code_ref, mine_ref, theirs_ref, my_map_ref, their_map_ref, out_ref):
    def then():
        out_ref[...] = move_states(theirs_ref[...], my_map_ref) + mine_ref[...]

    def otherwise():
        out_ref[...] = move_states(mine_ref[...], their_map_ref) + theirs_ref[...]

    later(code_ref, then, otherwise)


def merge_states(code, mine, theirs, my_map, their_map):
    lines, levels = mine.shape
    return call(
        merge_states_kernel, [SMEM] + [VMEM] * 4, shape(lines, levels), 12 * lines * levels**2
    )(code, mine, theirs, my_map, their_map)


def merge_kernel(start, kind, apart, halves, half, code_ref, *refs):
    refs = list(refs)
    mine_map = refs.pop(0)
    if apart and kind != "maps":
        mine_states = refs.pop(0)
    else:
        mine_states = None if kind == "maps" else mine_map.at[start:]
    here = refs.pop(0)
    there = refs.pop(0) if halves else None
    their_states = refs.pop(0) if apart and kind != "maps" else None
    out = refs.pop(0)
    core = code_ref[0] // 2
    their_map = here
    if halves:
        their_map = refs.pop(0)
        rows = here.shape[0]

        @pl.when(core == 0)
        def _():
            their_map[:rows] = here[...]
            their_map[rows:] = there[...]

        @pl.when(core == 1)
        def _():
            their_map[:rows] = there[...]
            their_map[rows:] = here[...]

    if their_states is None and kind != "maps":
        their_states = their_map.at[start:]

    def joined(left_map, left_states, right_map, right_states):
        if kind == "both" and not apart:
            join(left_map, right_map, out)
            return
        if kind != "states":
            join_maps(left_map, right_map, out)
        if kind == "maps":
            return
        states = move_states(left_states[...], right_map) + right_states[...]
        if kind == "both":
            out[start:] = states
        else:
            out[...] = states

    later(
        code_ref,
        lambda: joined(their_map, their_states, mine_map, mine_states),
        lambda: joined(mine_map, mine_states, their_map, their_states),
    )
    if half:
        half_ref = refs.pop(0)
        rows = half_ref.shape[0]

        @pl.when(core == 0)
        def _():
            half_ref[...] = out[:rows]

        @pl.when(core == 1)
        def _():
            half_ref[...] = out[rows:]


def merge(code, mine, theirs, kind, lines, apart, halves, half):
    levels = mine[0].shape[1]
    start = levels + PAD
    rows = {"maps": start, "both": start + lines, "states": lines}[kind]
    out = [shape(rows, levels)]
    if halves:
        out.append(shape(2 * theirs[0].shape[0], levels))
    if half:
        out.append(shape(rows // 2, levels))
    operands = (*mine, *theirs)
    got = call(
        functools.partial(merge_kernel, start, kind, apart, halves, half),
        [SMEM] + [VMEM] * len(operands),
        out,
        12 * rows * levels**2,
    )(code, *operands)
    return got[0], got[1] if halves else theirs[0], got[-1]


def four_kernel(
    code_ref, mine_ref, here_ref, there_ref, this_ref, that_ref,
    total_ref, beside_ref, front_ref, half_ref, four_ref, back_ref,
):
    core = lax.rem(code_ref[0], 2)
    place = code_ref[0] // 2
    rows = half_ref.shape[0]
    four_ref[place] = mine_ref[...]
    four_ref[place ^ (1 + core)] = here_ref[...]
    four_ref[place ^ (2 - core)] = there_ref[...]
    four_ref[place ^ 3, pl.ds(core * rows, rows)] = this_ref[...]
    four_ref[place ^ 3, pl.ds((1 - core) * rows, rows)] = that_ref[...]
    join(four_ref.at[0], four_ref.at[1], front_ref)
    join(four_ref.at[2], four_ref.at[3], back_ref)
    join(front_ref, back_ref, total_ref)
    half_ref[...] = total_ref[pl.ds(core * rows, rows)]
    beside_ref[...] = four_ref[place ^ 1]


def join_four(code, mine, here, there, this, that):
    rows, levels = mine.shape
    whole = shape(rows, levels)
    return call(
        four_kernel,
        [SMEM] + [VMEM] * 5,
        [whole, whole, whole, shape(rows // 2, levels)],
        36 * rows * levels**2,
        [pltpu.VMEM((4, rows, levels), F32), pltpu.VMEM((rows, levels), F32)],
    )(code, mine, here, there, this, that)


def extend_kernel(first, apart, code_ref, *refs):
    refs = list(refs)
    their_map = refs.pop(0)
    levels = their_map.shape[1]
    start = levels + PAD
    their_states = refs.pop(0)[...] if apart else their_map[start:]
    if first:
        (ahead_ref,) = refs
    else:
        before_ref, ahead_ref = refs

    def then():
        if first:
            ahead_ref[:start] = their_map[:start]
            ahead_ref[start:] = their_states
        else:
            join(their_map, before_ref, ahead_ref)

    def otherwise():
        if first:
            row = lax.broadcasted_iota(jnp.int32, ahead_ref.shape, 0)
            column = lax.broadcasted_iota(jnp.int32, ahead_ref.shape, 1)
            ahead_ref[...] = jnp.where(row == column, 1.0, 0.0).astype(F32)
        else:
            ahead_ref[...] = before_ref[...]

    later(code_ref, then, otherwise)


def extend(code, theirs, before):
    levels = theirs[0].shape[1]
    apart = len(theirs) == 2
    rows = levels + PAD + (theirs[1].shape[0] if apart else theirs[0].shape[0] - levels - PAD)
    first = before is None
    operands = theirs if first else (*theirs, before)
    return call(
        functools.partial(extend_kernel, first, apart),
        [SMEM] + [VMEM] * len(operands),
        shape(rows, levels),
        12 * rows * levels**2,
    )(code, *operands)


def enter_kernel(from_ref, map_ref, own_ref, out_ref):
    out_ref[...] = move_states(from_ref[...], map_ref) + own_ref[...]


def enter(states, total, own):
    lines, levels = own.shape
    return call(enter_kernel, [VMEM] * 3, shape(lines, levels), 12 * lines * levels**2)(
        states, total, own
    )


def plane_total_kernel(code_ref, mine_ref, theirs_ref, total_ref):
    @pl.when(code_ref[0] < 4)
    def _():
        total_ref[...] = jnp.zeros_like(total_ref)

    @pl.when(code_ref[0] >= 4)
    def _():
        later(
            code_ref,
            lambda: join(theirs_ref, mine_ref, total_ref),
            lambda: join(mine_ref, theirs_ref, total_ref),
        )


def plane_total(code, mine, theirs):
    rows, levels = mine.shape
    return call(
        plane_total_kernel, [SMEM, VMEM, VMEM], shape(rows, levels), 12 * rows * levels**2
    )(code, mine, theirs)


def settle_planes_kernel(code_ref, beside_ref, from_ref, before_ref, ahead_ref):
    start = before_ref.shape[1] + PAD

    def then():
        join(beside_ref, before_ref, ahead_ref)

    def otherwise():
        ahead_ref[:start] = before_ref[:start]
        ahead_ref[start:] = move_states(from_ref[...], before_ref) + before_ref[start:]

    later(code_ref, then, otherwise)


def settle_planes(code, beside, from_first, before):
    rows, levels = before.shape
    return call(
        settle_planes_kernel, [SMEM] + [VMEM] * 3, shape(rows, levels), 12 * rows * levels**2
    )(code, beside, from_first, before)


def finish_kernel(code_ref, one_ref, two_ref, before_ref, prefix_ref, trial_ref, *refs):
    *part_refs, solved_ref, held_ref, incoming, arrived = refs
    fetch(prefix_ref, held_ref, arrived)
    start = before_ref.shape[1] + PAD
    entering = one_ref[...] + two_ref[...]
    high, low = split(move_states(entering, before_ref) + before_ref[start:])
    lines = high.shape[0]
    incoming[:lines] = high
    incoming[lines:] = low
    product = functools.partial(jnp.dot, preferred_element_type=F32)

    @pl.loop(0, held_ref.shape[0])
    def _(cell):
        block_copy(prefix_ref, held_ref, arrived, cell).wait()
        map_high, map_low = split(held_ref[cell])
        both = product(incoming[...], map_high)
        rest = both[lines:] + product(incoming[:lines], map_low)
        solved_ref[:, cell, :] = trial_ref[cell] + (both[:lines] + rest)

    share = part_refs[0].shape[0]
    for turn, part_ref in enumerate(part_refs):
        part_ref[...] = solved_ref[pl.ds((code_ref[0] ^ turn) * share, share)]


def finish(here, entering, before, prefix, trial, parts):
    cells, lines, levels = trial.shape
    return call(
        finish_kernel,
        [SMEM, VMEM, VMEM, VMEM, HBM, VMEM],
        [shape(lines // parts, cells, levels)] * parts,
        12 * (cells + 1) * lines * levels**2,
        [
            pltpu.VMEM((lines, cells, levels), F32),
            pltpu.VMEM(prefix.shape, F32),
            pltpu.VMEM((2 * lines, levels), jnp.bfloat16),
            pltpu.SemaphoreType.DMA((cells,)),
        ],
        None,
        LARGE,
    )(here, *entering, before, prefix, trial)


def shards(span_count, forcing, blocks, upstream):
    cells, levels, _ = blocks.shape
    share = forcing.shape[0]
    lines = share * span_count
    here = lax.axis_index("span").astype(jnp.int32).reshape(1)

    def trade(parts):
        kept, *sent = parts
        return [kept] + [partner(part, "span", k + 1) for k, part in enumerate(sent)]

    def partner(value, axis, mask):
        count = lax.axis_size(axis)
        return lax.ppermute(value, axis, [(i, i ^ mask) for i in range(count)])

    forcing_parts = trade(cut(here, forcing, span_count))
    prefix, maps = prefix_maps(blocks, upstream)
    forcing_parts, maps = lax.optimization_barrier((forcing_parts, maps))
    trial, states = trial_states(here, blocks, upstream, forcing_parts)

    def code_of(axis, bit):
        upper = jnp.where((lax.axis_index(axis) & bit) != 0, 1, 0)
        core = jnp.where((lax.axis_index("line") & CORE) != 0, 2, 0)
        return (upper + core).astype(jnp.int32).reshape(1)

    def along_four(total, half, before):
        device = lax.axis_index("line")
        pairs = [(i, i ^ FOUR[i & CORE]) for i in range(lax.axis_size("line"))]
        here, this = lax.ppermute(total, "line", pairs), partner(half, "line", THIRD)
        here, this, before = lax.optimization_barrier((here, this, before))
        there, that = partner(here, "line", CORE), partner(this, "line", CORE)
        code = (device & (CORE | THIRD)).astype(jnp.int32).reshape(1)
        total, beside, front, half = join_four(code, total, here, there, this, that)
        before = extend(code_of("line", FOUR[0]), (beside,), before)
        before = extend(code_of("line", FOUR[1]), (front,), before)
        return total, half, before

    total, half, before = None, None, None
    for turn, (axis, mask, bit, halves, apart) in enumerate(ROUNDS):
        code = code_of(axis, bit)
        last = turn == len(ROUNDS) - 1
        if halves:
            mine_half = partner(half, axis, mask)
            mine_half, before = lax.optimization_barrier((mine_half, before))
            theirs = (mine_half, partner(mine_half, "line", CORE))
        else:
            theirs = (partner(maps if apart else total, axis, mask),)
            if before is not None:
                theirs, before = lax.optimization_barrier((theirs, before))
        mine = (total,)
        if apart:
            their_states = partner(states, axis, mask)
            mine, theirs = (maps, states), (*theirs, their_states)
        if last:
            plane, whole, _ = merge(code, mine, theirs, "states", lines, apart, halves, False)
            inner = (lax.axis_index("line") // PLANE + 1) // 2 == 1
            total = plane_total(code + jnp.where(inner, 4, 0).astype(jnp.int32), total, whole)
        else:
            half_too = turn == len(ROUNDS) - 2
            total, whole, half = merge(code, mine, theirs, "both", lines, apart, halves, half_too)
        before = extend(code, (whole, their_states) if apart else (whole,), before)
        if turn == len(ROUNDS) - 2:
            total, half, before = along_four(total, half, before)

    def across(value, source, target):
        shift = (target - source) * PLANE
        pairs = [(i, i + shift) for i in range(source * PLANE, (source + 1) * PLANE)]
        return lax.ppermute(value, "line", pairs)

    from_first = across(plane, 0, 1)
    beside = across(total, 2, 3)
    from_first, before = lax.optimization_barrier((from_first, before))
    joined = enter(from_first, total, plane)
    two_on = across(joined, 1, 3)
    entering = (two_on, across(joined, 1, 2))
    in_last = jnp.where(lax.axis_index("line") >= 3 * PLANE, 1, 0).astype(jnp.int32).reshape(1)
    before = settle_planes(in_last, beside, from_first, before)
    return assemble(here, trade(finish(here, entering, before, prefix, trial, span_count)))


def solution(mesh):
    placed = (P("span", "line", None), P(("line", "span"), None, None), P(("line", "span"), None))
    return jax.shard_map(
        functools.partial(shards, mesh.shape["span"]),
        mesh=mesh,
        in_specs=placed,
        out_specs=P("span", "line", None),
        check_vma=False,
    )
```

```python
import functools

import jax
import jax.numpy as jnp
from jax import lax
from jax.experimental import pallas as pl
from jax.experimental.pallas import tpu as pltpu
from jax.sharding import PartitionSpec as P

F32 = jnp.float32
BIG = 2.0**40
STEP = 2.0**48
PAD = 16
VMEM = pl.BlockSpec(memory_space=pltpu.VMEM)
HBM = pl.BlockSpec(memory_space=pltpu.HBM)
LARGE = 52 * 2**20
SMEM = pl.BlockSpec(memory_space=pltpu.SMEM)
CORE = 1
ROUNDS = (
    ("span", 1, 1, False, True),
    ("span", 3, 2, False, False),
    ("line", 1, 1, False, False),
    ("line", 14, 8, True, False),
)
FOUR = (2, 4)
THIRD = 6
PLANE = 16


def split(a):
    high = a.astype(jnp.bfloat16)
    return high, (a - high.astype(F32)).astype(jnp.bfloat16)


def dot3(a, b):
    product = functools.partial(jnp.dot, preferred_element_type=F32)
    (a_high, a_low), (b_high, b_low) = split(a), split(b)
    return product(a_high, b_high) + (product(a_high, b_low) + product(a_low, b_high))


def shape(*dims):
    return jax.ShapeDtypeStruct(dims, F32)


def call(kernel, in_specs, out_shape, flops, scratch=(), out_specs=None, vmem=8 * 2**20):
    return pl.pallas_call(
        kernel,
        in_specs=in_specs,
        out_specs=out_specs or jax.tree.map(lambda _: VMEM, out_shape),
        out_shape=out_shape,
        scratch_shapes=list(scratch),
        compiler_params=pltpu.CompilerParams(vmem_limit_bytes=vmem),
        cost_estimate=pl.CostEstimate(flops=flops, bytes_accessed=2**20, transcendentals=0),
    )


def settle(hat, count):
    large = jnp.max(jnp.abs(hat), keepdims=True) > BIG
    return hat * jnp.where(large, 1.0 / STEP, 1.0), count + jnp.where(large, 1.0, 0.0)


def unscale(value, count):
    for done in (0.0, 2.0, 4.0):
        left = count - done
        value = value * jnp.where(left > 1.5, STEP * STEP, jnp.where(left > 0.5, STEP, 1.0))
    return value


def put_map(hat, count, out_ref):
    levels = hat.shape[1]
    hat, count = settle(hat, count)
    out_ref[:levels] = hat
    out_ref[levels : levels + 8] = count
    out_ref[levels + 8 : levels + PAD] = jnp.zeros_like(count)


def join_maps(left_ref, right_ref, out_ref):
    levels = out_ref.shape[1]
    count = left_ref[levels : levels + 8] + right_ref[levels : levels + 8]
    put_map(dot3(left_ref[:levels], right_ref[:levels]), count, out_ref)


def move_states(states, map_ref):
    levels = map_ref.shape[1]
    return unscale(dot3(states, map_ref[:levels]), map_ref[levels : levels + 1])


def join(left_ref, right_ref, out_ref):
    levels = out_ref.shape[1]
    start = levels + PAD
    both = dot3(left_ref[...], right_ref[:levels])
    count = left_ref[levels : levels + 8] + right_ref[levels : levels + 8]
    put_map(both[:levels], count, out_ref)
    out_ref[start:] = unscale(both[start:], right_ref[levels : levels + 1]) + right_ref[start:]


def block_copy(blocks_ref, held_ref, arrived, cell):
    return pltpu.make_async_copy(blocks_ref.at[cell], held_ref.at[cell], arrived.at[cell])


def fetch(blocks_ref, held_ref, arrived):
    @pl.loop(0, held_ref.shape[0])
    def _(cell):
        block_copy(blocks_ref, held_ref, arrived, cell).start()


def maps_kernel(
    upstream_ref, blocks_ref, prefix_ref, map_ref, held_ref, made_ref, last_ref, arrived, left
):
    cells, levels, _ = held_ref.shape
    fetch(blocks_ref, held_ref, arrived)
    row = lax.broadcasted_iota(jnp.int32, (levels, levels), 0)
    column = lax.broadcasted_iota(jnp.int32, (levels, levels), 1)
    first = jnp.where(row == column, -upstream_ref[0:1, :], 0.0)
    first = jnp.sum(first, axis=1, keepdims=True)
    block_copy(blocks_ref, held_ref, arrived, 0).wait()
    first = first * held_ref[0]
    last_ref[...] = first
    made_ref[0] = first
    block_copy(made_ref, prefix_ref, left, 0).start()

    @pl.loop(1, cells)
    def _(cell):
        scaled = last_ref[...] * -upstream_ref[pl.ds(cell, 1), :]
        block_copy(blocks_ref, held_ref, arrived, cell).wait()
        product = dot3(scaled, held_ref[cell])
        last_ref[...] = product
        made_ref[cell] = product
        block_copy(made_ref, prefix_ref, left, cell).start()

    put_map(last_ref[...], jnp.zeros((8, levels), F32), map_ref)

    @pl.loop(0, cells)
    def _(cell):
        block_copy(made_ref, prefix_ref, left, cell).wait()


def prefix_maps(blocks, upstream):
    cells, levels, _ = blocks.shape
    return call(
        maps_kernel,
        [VMEM, HBM],
        [shape(*blocks.shape), shape(levels + PAD, levels)],
        12 * cells * levels**3,
        [
            pltpu.VMEM(blocks.shape, F32),
            pltpu.VMEM(blocks.shape, F32),
            pltpu.VMEM((levels, levels), F32),
            pltpu.SemaphoreType.DMA((cells,)),
            pltpu.SemaphoreType.DMA((cells,)),
        ],
        [HBM, VMEM],
        LARGE,
    )(upstream, blocks)


def cut_kernel(code_ref, forcing_ref, *part_refs):
    cells = part_refs[0].shape[1]
    for turn, part_ref in enumerate(part_refs):
        first = pl.multiple_of((code_ref[0] ^ turn) * cells, cells)
        part_ref[...] = forcing_ref[:, pl.ds(first, cells), :]


def cut(here, forcing, parts):
    share, length, levels = forcing.shape
    return call(cut_kernel, [SMEM, VMEM], [shape(share, length // parts, levels)] * parts, 1)(
        here, forcing
    )


def assemble_kernel(code_ref, *refs):
    *part_refs, whole_ref = refs
    cells = part_refs[0].shape[1]
    for turn, part_ref in enumerate(part_refs):
        first = pl.multiple_of((code_ref[0] ^ turn) * cells, cells)
        whole_ref[:, pl.ds(first, cells), :] = part_ref[...]


def assemble(here, parts):
    share, cells, levels = parts[0].shape
    return call(
        assemble_kernel, [SMEM] + [VMEM] * len(parts), shape(share, len(parts) * cells, levels), 1
    )(here, *parts)


def states_kernel(code_ref, upstream_ref, blocks_ref, *refs):
    *part_refs, trial_ref, states_ref, forcing_ref = refs
    share = part_refs[0].shape[0]
    for turn, part_ref in enumerate(part_refs):
        forcing_ref[pl.ds((code_ref[0] ^ turn) * share, share)] = part_ref[...]
    states_ref[...] = jnp.zeros_like(states_ref)

    @pl.loop(0, blocks_ref.shape[0])
    def _(cell):
        forced = forcing_ref[:, cell, :] - upstream_ref[pl.ds(cell, 1), :] * states_ref[...]
        state = dot3(forced, blocks_ref[cell])
        states_ref[...] = state
        trial_ref[cell] = state


def trial_states(here, blocks, upstream, parts):
    cells, levels, _ = blocks.shape
    lines = len(parts) * parts[0].shape[0]
    return call(
        states_kernel,
        [SMEM] + [VMEM] * (2 + len(parts)),
        [shape(cells, lines, levels), shape(lines, levels)],
        12 * cells * lines * levels**2,
        [pltpu.VMEM((lines, cells, levels), F32)],
    )(here, upstream, blocks, *parts)


def later(code_ref, then, otherwise):
    upper = lax.rem(code_ref[0], 2)
    pl.when(upper == 1)(then)
    pl.when(upper == 0)(otherwise)


def merge_states_kernel(code_ref, mine_ref, theirs_ref, my_map_ref, their_map_ref, out_ref):
    def then():
        out_ref[...] = move_states(theirs_ref[...], my_map_ref) + mine_ref[...]

    def otherwise():
        out_ref[...] = move_states(mine_ref[...], their_map_ref) + theirs_ref[...]

    later(code_ref, then, otherwise)


def merge_states(code, mine, theirs, my_map, their_map):
    lines, levels = mine.shape
    return call(
        merge_states_kernel, [SMEM] + [VMEM] * 4, shape(lines, levels), 12 * lines * levels**2
    )(code, mine, theirs, my_map, their_map)


def merge_kernel(start, kind, apart, halves, half, code_ref, *refs):
    refs = list(refs)
    mine_map = refs.pop(0)
    if apart and kind != "maps":
        mine_states = refs.pop(0)
    else:
        mine_states = None if kind == "maps" else mine_map.at[start:]
    here = refs.pop(0)
    there = refs.pop(0) if halves else None
    their_states = refs.pop(0) if apart and kind != "maps" else None
    out = refs.pop(0)
    core = code_ref[0] // 2
    their_map = here
    if halves:
        their_map = refs.pop(0)
        rows = here.shape[0]

        @pl.when(core == 0)
        def _():
            their_map[:rows] = here[...]
            their_map[rows:] = there[...]

        @pl.when(core == 1)
        def _():
            their_map[:rows] = there[...]
            their_map[rows:] = here[...]

    if their_states is None and kind != "maps":
        their_states = their_map.at[start:]

    def joined(left_map, left_states, right_map, right_states):
        if kind == "both" and not apart:
            join(left_map, right_map, out)
            return
        if kind != "states":
            join_maps(left_map, right_map, out)
        if kind == "maps":
            return
        states = move_states(left_states[...], right_map) + right_states[...]
        if kind == "both":
            out[start:] = states
        else:
            out[...] = states

    later(
        code_ref,
        lambda: joined(their_map, their_states, mine_map, mine_states),
        lambda: joined(mine_map, mine_states, their_map, their_states),
    )
    if half:
        half_ref = refs.pop(0)
        rows = half_ref.shape[0]

        @pl.when(core == 0)
        def _():
            half_ref[...] = out[:rows]

        @pl.when(core == 1)
        def _():
            half_ref[...] = out[rows:]


def merge(code, mine, theirs, kind, lines, apart, halves, half):
    levels = mine[0].shape[1]
    start = levels + PAD
    rows = {"maps": start, "both": start + lines, "states": lines}[kind]
    out = [shape(rows, levels)]
    if halves:
        out.append(shape(2 * theirs[0].shape[0], levels))
    if half:
        out.append(shape(rows // 2, levels))
    operands = (*mine, *theirs)
    got = call(
        functools.partial(merge_kernel, start, kind, apart, halves, half),
        [SMEM] + [VMEM] * len(operands),
        out,
        12 * rows * levels**2,
    )(code, *operands)
    return got[0], got[1] if halves else theirs[0], got[-1]


def four_kernel(
    code_ref, mine_ref, here_ref, there_ref, this_ref, that_ref,
    total_ref, beside_ref, front_ref, half_ref, four_ref, back_ref,
):
    core = lax.rem(code_ref[0], 2)
    place = code_ref[0] // 2
    rows = half_ref.shape[0]
    four_ref[place] = mine_ref[...]
    four_ref[place ^ (1 + core)] = here_ref[...]
    four_ref[place ^ (2 - core)] = there_ref[...]
    four_ref[place ^ 3, pl.ds(core * rows, rows)] = this_ref[...]
    four_ref[place ^ 3, pl.ds((1 - core) * rows, rows)] = that_ref[...]
    join(four_ref.at[0], four_ref.at[1], front_ref)
    join(four_ref.at[2], four_ref.at[3], back_ref)
    join(front_ref, back_ref, total_ref)
    half_ref[...] = total_ref[pl.ds(core * rows, rows)]
    beside_ref[...] = four_ref[place ^ 1]


def join_four(code, mine, here, there, this, that):
    rows, levels = mine.shape
    whole = shape(rows, levels)
    return call(
        four_kernel,
        [SMEM] + [VMEM] * 5,
        [whole, whole, whole, shape(rows // 2, levels)],
        36 * rows * levels**2,
        [pltpu.VMEM((4, rows, levels), F32), pltpu.VMEM((rows, levels), F32)],
    )(code, mine, here, there, this, that)


def extend_kernel(first, apart, code_ref, *refs):
    refs = list(refs)
    their_map = refs.pop(0)
    levels = their_map.shape[1]
    start = levels + PAD
    their_states = refs.pop(0)[...] if apart else their_map[start:]
    if first:
        (ahead_ref,) = refs
    else:
        before_ref, ahead_ref = refs

    def then():
        if first:
            ahead_ref[:start] = their_map[:start]
            ahead_ref[start:] = their_states
        else:
            join(their_map, before_ref, ahead_ref)

    def otherwise():
        if first:
            row = lax.broadcasted_iota(jnp.int32, ahead_ref.shape, 0)
            column = lax.broadcasted_iota(jnp.int32, ahead_ref.shape, 1)
            ahead_ref[...] = jnp.where(row == column, 1.0, 0.0).astype(F32)
        else:
            ahead_ref[...] = before_ref[...]

    later(code_ref, then, otherwise)


def extend(code, theirs, before):
    levels = theirs[0].shape[1]
    apart = len(theirs) == 2
    rows = levels + PAD + (theirs[1].shape[0] if apart else theirs[0].shape[0] - levels - PAD)
    first = before is None
    operands = theirs if first else (*theirs, before)
    return call(
        functools.partial(extend_kernel, first, apart),
        [SMEM] + [VMEM] * len(operands),
        shape(rows, levels),
        12 * rows * levels**2,
    )(code, *operands)


def enter_kernel(from_ref, map_ref, own_ref, out_ref):
    out_ref[...] = move_states(from_ref[...], map_ref) + own_ref[...]


def enter(states, total, own):
    lines, levels = own.shape
    return call(enter_kernel, [VMEM] * 3, shape(lines, levels), 12 * lines * levels**2)(
        states, total, own
    )


def plane_total_kernel(code_ref, mine_ref, theirs_ref, total_ref):
    @pl.when(code_ref[0] < 4)
    def _():
        total_ref[...] = jnp.zeros_like(total_ref)

    @pl.when(code_ref[0] >= 4)
    def _():
        later(
            code_ref,
            lambda: join(theirs_ref, mine_ref, total_ref),
            lambda: join(mine_ref, theirs_ref, total_ref),
        )


def plane_total(code, mine, theirs):
    rows, levels = mine.shape
    return call(
        plane_total_kernel, [SMEM, VMEM, VMEM], shape(rows, levels), 12 * rows * levels**2
    )(code, mine, theirs)


def settle_planes_kernel(code_ref, beside_ref, from_ref, before_ref, ahead_ref):
    start = before_ref.shape[1] + PAD

    def then():
        join(beside_ref, before_ref, ahead_ref)

    def otherwise():
        ahead_ref[:start] = before_ref[:start]
        ahead_ref[start:] = move_states(from_ref[...], before_ref) + before_ref[start:]

    later(code_ref, then, otherwise)


def settle_planes(code, beside, from_first, before):
    rows, levels = before.shape
    return call(
        settle_planes_kernel, [SMEM] + [VMEM] * 3, shape(rows, levels), 12 * rows * levels**2
    )(code, beside, from_first, before)


def finish_kernel(code_ref, one_ref, two_ref, before_ref, prefix_ref, trial_ref, *refs):
    *part_refs, solved_ref, held_ref, incoming, arrived = refs
    fetch(prefix_ref, held_ref, arrived)
    start = before_ref.shape[1] + PAD
    entering = one_ref[...] + two_ref[...]
    high, low = split(move_states(entering, before_ref) + before_ref[start:])
    lines = high.shape[0]
    incoming[:lines] = high
    incoming[lines:] = low
    product = functools.partial(jnp.dot, preferred_element_type=F32)

    @pl.loop(0, held_ref.shape[0])
    def _(cell):
        block_copy(prefix_ref, held_ref, arrived, cell).wait()
        map_high, map_low = split(held_ref[cell])
        both = product(incoming[...], map_high)
        rest = both[lines:] + product(incoming[:lines], map_low)
        solved_ref[:, cell, :] = trial_ref[cell] + (both[:lines] + rest)

    share = part_refs[0].shape[0]
    for turn, part_ref in enumerate(part_refs):
        part_ref[...] = solved_ref[pl.ds((code_ref[0] ^ turn) * share, share)]


def finish(here, entering, before, prefix, trial, parts):
    cells, lines, levels = trial.shape
    return call(
        finish_kernel,
        [SMEM, VMEM, VMEM, VMEM, HBM, VMEM],
        [shape(lines // parts, cells, levels)] * parts,
        12 * (cells + 1) * lines * levels**2,
        [
            pltpu.VMEM((lines, cells, levels), F32),
            pltpu.VMEM(prefix.shape, F32),
            pltpu.VMEM((2 * lines, levels), jnp.bfloat16),
            pltpu.SemaphoreType.DMA((cells,)),
        ],
        None,
        LARGE,
    )(here, *entering, before, prefix, trial)


def shards(span_count, forcing, blocks, upstream):
    cells, levels, _ = blocks.shape
    share = forcing.shape[0]
    lines = share * span_count
    here = lax.axis_index("span").astype(jnp.int32).reshape(1)

    def trade(parts):
        kept, *sent = parts
        return [kept] + [partner(part, "span", k + 1) for k, part in enumerate(sent)]

    def partner(value, axis, mask):
        count = lax.axis_size(axis)
        return lax.ppermute(value, axis, [(i, i ^ mask) for i in range(count)])

    forcing_parts = trade(cut(here, forcing, span_count))
    prefix, maps = prefix_maps(blocks, upstream)
    forcing_parts, maps = lax.optimization_barrier((forcing_parts, maps))
    trial, states = trial_states(here, blocks, upstream, forcing_parts)

    def code_of(axis, bit):
        upper = jnp.where((lax.axis_index(axis) & bit) != 0, 1, 0)
        core = jnp.where((lax.axis_index("line") & CORE) != 0, 2, 0)
        return (upper + core).astype(jnp.int32).reshape(1)

    def along_four(total, half, before):
        device = lax.axis_index("line")
        pairs = [(i, i ^ FOUR[i & CORE]) for i in range(lax.axis_size("line"))]
        here, this = lax.ppermute(total, "line", pairs), partner(half, "line", THIRD)
        here, this, before = lax.optimization_barrier((here, this, before))
        there, that = partner(here, "line", CORE), partner(this, "line", CORE)
        code = (device & (CORE | THIRD)).astype(jnp.int32).reshape(1)
        total, beside, front, half = join_four(code, total, here, there, this, that)
        before = extend(code_of("line", FOUR[0]), (beside,), before)
        before = extend(code_of("line", FOUR[1]), (front,), before)
        return total, half, before

    total, half, before = None, None, None
    for turn, (axis, mask, bit, halves, apart) in enumerate(ROUNDS):
        code = code_of(axis, bit)
        last = turn == len(ROUNDS) - 1
        if halves:
            mine_half = partner(half, axis, mask)
            mine_half, before = lax.optimization_barrier((mine_half, before))
            theirs = (mine_half, partner(mine_half, "line", CORE))
        else:
            theirs = (partner(maps if apart else total, axis, mask),)
            if before is not None:
                theirs, before = lax.optimization_barrier((theirs, before))
        mine = (total,)
        if apart:
            their_states = partner(states, axis, mask)
            mine, theirs = (maps, states), (*theirs, their_states)
        if last:
            plane, whole, _ = merge(code, mine, theirs, "states", lines, apart, halves, False)
            inner = (lax.axis_index("line") // PLANE + 1) // 2 == 1
            total = plane_total(code + jnp.where(inner, 4, 0).astype(jnp.int32), total, whole)
        else:
            half_too = turn == len(ROUNDS) - 2
            total, whole, half = merge(code, mine, theirs, "both", lines, apart, halves, half_too)
        before = extend(code, (whole, their_states) if apart else (whole,), before)
        if turn == len(ROUNDS) - 2:
            total, half, before = along_four(total, half, before)

    def across(value, source, target):
        shift = (target - source) * PLANE
        pairs = [(i, i + shift) for i in range(source * PLANE, (source + 1) * PLANE)]
        return lax.ppermute(value, "line", pairs)

    from_first = across(plane, 0, 1)
    beside = across(total, 2, 3)
    from_first, before = lax.optimization_barrier((from_first, before))
    joined = enter(from_first, total, plane)
    two_on = across(joined, 1, 3)
    entering = (two_on, across(joined, 1, 2))
    in_last = jnp.where(lax.axis_index("line") >= 3 * PLANE, 1, 0).astype(jnp.int32).reshape(1)
    before = settle_planes(in_last, beside, from_first, before)
    return assemble(here, trade(finish(here, entering, before, prefix, trial, span_count)))


def solution(mesh):
    placed = (P("span", "line", None), P(("line", "span"), None, None), P(("line", "span"), None))
    return jax.shard_map(
        functools.partial(shards, mesh.shape["span"]),
        mesh=mesh,
        in_specs=placed,
        out_specs=P("span", "line", None),
        check_vma=False,
    )
```

```python
import functools

import jax
import jax.numpy as jnp
from jax import lax
from jax.experimental import pallas as pl
from jax.experimental.pallas import tpu as pltpu
from jax.sharding import PartitionSpec as P

F32 = jnp.float32
BIG = 2.0**40
STEP = 2.0**48
PAD = 16
VMEM = pl.BlockSpec(memory_space=pltpu.VMEM)
HBM = pl.BlockSpec(memory_space=pltpu.HBM)
LARGE = 52 * 2**20
SMEM = pl.BlockSpec(memory_space=pltpu.SMEM)
CORE = 1
ROUNDS = (
    ("span", 1, 1, False, True),
    ("span", 3, 2, False, False),
    ("line", 1, 1, False, False),
    ("line", 14, 8, True, False),
)
FOUR = (2, 4)
THIRD = 6
PLANE = 16


def split(a):
    high = a.astype(jnp.bfloat16)
    return high, (a - high.astype(F32)).astype(jnp.bfloat16)


def dot3(a, b):
    product = functools.partial(jnp.dot, preferred_element_type=F32)
    (a_high, a_low), (b_high, b_low) = split(a), split(b)
    rows = a.shape[0]
    both = product(jnp.concatenate([a_high, a_low], axis=0), b_high)
    return both[:rows] + (product(a_high, b_low) + both[rows:])


def shape(*dims):
    return jax.ShapeDtypeStruct(dims, F32)


def call(kernel, in_specs, out_shape, flops, scratch=(), out_specs=None, vmem=8 * 2**20):
    return pl.pallas_call(
        kernel,
        in_specs=in_specs,
        out_specs=out_specs or jax.tree.map(lambda _: VMEM, out_shape),
        out_shape=out_shape,
        scratch_shapes=list(scratch),
        compiler_params=pltpu.CompilerParams(vmem_limit_bytes=vmem),
        cost_estimate=pl.CostEstimate(flops=flops, bytes_accessed=2**20, transcendentals=0),
    )


def settle(hat, count):
    large = jnp.max(jnp.abs(hat), keepdims=True) > BIG
    return hat * jnp.where(large, 1.0 / STEP, 1.0), count + jnp.where(large, 1.0, 0.0)


def unscale(value, count):
    for done in (0.0, 2.0, 4.0):
        left = count - done
        value = value * jnp.where(left > 1.5, STEP * STEP, jnp.where(left > 0.5, STEP, 1.0))
    return value


def put_map(hat, count, out_ref):
    levels = hat.shape[1]
    hat, count = settle(hat, count)
    out_ref[:levels] = hat
    out_ref[levels : levels + 8] = count
    out_ref[levels + 8 : levels + PAD] = jnp.zeros_like(count)


def join_maps(left_ref, right_ref, out_ref):
    levels = out_ref.shape[1]
    count = left_ref[levels : levels + 8] + right_ref[levels : levels + 8]
    put_map(dot3(left_ref[:levels], right_ref[:levels]), count, out_ref)


def move_states(states, map_ref):
    levels = map_ref.shape[1]
    return unscale(dot3(states, map_ref[:levels]), map_ref[levels : levels + 1])


def join(left_ref, right_ref, out_ref):
    levels = out_ref.shape[1]
    start = levels + PAD
    both = dot3(left_ref[...], right_ref[:levels])
    count = left_ref[levels : levels + 8] + right_ref[levels : levels + 8]
    put_map(both[:levels], count, out_ref)
    out_ref[start:] = unscale(both[start:], right_ref[levels : levels + 1]) + right_ref[start:]


def block_copy(blocks_ref, held_ref, arrived, cell):
    return pltpu.make_async_copy(blocks_ref.at[cell], held_ref.at[cell], arrived.at[cell])


def fetch(blocks_ref, held_ref, arrived):
    @pl.loop(0, held_ref.shape[0])
    def _(cell):
        block_copy(blocks_ref, held_ref, arrived, cell).start()


def maps_kernel(
    upstream_ref, blocks_ref, prefix_ref, map_ref, held_ref, made_ref, last_ref, arrived, left
):
    cells, levels, _ = held_ref.shape
    fetch(blocks_ref, held_ref, arrived)
    row = lax.broadcasted_iota(jnp.int32, (levels, levels), 0)
    column = lax.broadcasted_iota(jnp.int32, (levels, levels), 1)
    first = jnp.where(row == column, -upstream_ref[0:1, :], 0.0)
    first = jnp.sum(first, axis=1, keepdims=True)
    block_copy(blocks_ref, held_ref, arrived, 0).wait()
    first = first * held_ref[0]
    last_ref[...] = first
    made_ref[0] = first
    block_copy(made_ref, prefix_ref, left, 0).start()

    @pl.loop(1, cells)
    def _(cell):
        scaled = last_ref[...] * -upstream_ref[pl.ds(cell, 1), :]
        block_copy(blocks_ref, held_ref, arrived, cell).wait()
        product = dot3(scaled, held_ref[cell])
        last_ref[...] = product
        made_ref[cell] = product
        block_copy(made_ref, prefix_ref, left, cell).start()

    put_map(last_ref[...], jnp.zeros((8, levels), F32), map_ref)

    @pl.loop(0, cells)
    def _(cell):
        block_copy(made_ref, prefix_ref, left, cell).wait()


def prefix_maps(blocks, upstream):
    cells, levels, _ = blocks.shape
    return call(
        maps_kernel,
        [VMEM, HBM],
        [shape(*blocks.shape), shape(levels + PAD, levels)],
        12 * cells * levels**3,
        [
            pltpu.VMEM(blocks.shape, F32),
            pltpu.VMEM(blocks.shape, F32),
            pltpu.VMEM((levels, levels), F32),
            pltpu.SemaphoreType.DMA((cells,)),
            pltpu.SemaphoreType.DMA((cells,)),
        ],
        [HBM, VMEM],
        LARGE,
    )(upstream, blocks)


def cut_kernel(code_ref, forcing_ref, *part_refs):
    cells = part_refs[0].shape[1]
    for turn, part_ref in enumerate(part_refs):
        first = pl.multiple_of((code_ref[0] ^ turn) * cells, cells)
        part_ref[...] = forcing_ref[:, pl.ds(first, cells), :]


def cut(here, forcing, parts):
    share, length, levels = forcing.shape
    return call(cut_kernel, [SMEM, VMEM], [shape(share, length // parts, levels)] * parts, 1)(
        here, forcing
    )


def assemble_kernel(code_ref, *refs):
    *part_refs, whole_ref = refs
    cells = part_refs[0].shape[1]
    for turn, part_ref in enumerate(part_refs):
        first = pl.multiple_of((code_ref[0] ^ turn) * cells, cells)
        whole_ref[:, pl.ds(first, cells), :] = part_ref[...]


def assemble(here, parts):
    share, cells, levels = parts[0].shape
    return call(
        assemble_kernel, [SMEM] + [VMEM] * len(parts), shape(share, len(parts) * cells, levels), 1
    )(here, *parts)


def states_kernel(code_ref, upstream_ref, blocks_ref, *refs):
    *part_refs, trial_ref, states_ref, forcing_ref = refs
    share = part_refs[0].shape[0]
    for turn, part_ref in enumerate(part_refs):
        forcing_ref[pl.ds((code_ref[0] ^ turn) * share, share)] = part_ref[...]
    states_ref[...] = jnp.zeros_like(states_ref)

    @pl.loop(0, blocks_ref.shape[0])
    def _(cell):
        forced = forcing_ref[:, cell, :] - upstream_ref[pl.ds(cell, 1), :] * states_ref[...]
        state = dot3(forced, blocks_ref[cell])
        states_ref[...] = state
        trial_ref[cell] = state


def trial_states(here, blocks, upstream, parts):
    cells, levels, _ = blocks.shape
    lines = len(parts) * parts[0].shape[0]
    return call(
        states_kernel,
        [SMEM] + [VMEM] * (2 + len(parts)),
        [shape(cells, lines, levels), shape(lines, levels)],
        12 * cells * lines * levels**2,
        [pltpu.VMEM((lines, cells, levels), F32)],
    )(here, upstream, blocks, *parts)


def later(code_ref, then, otherwise):
    upper = lax.rem(code_ref[0], 2)
    pl.when(upper == 1)(then)
    pl.when(upper == 0)(otherwise)


def merge_states_kernel(code_ref, mine_ref, theirs_ref, my_map_ref, their_map_ref, out_ref):
    def then():
        out_ref[...] = move_states(theirs_ref[...], my_map_ref) + mine_ref[...]

    def otherwise():
        out_ref[...] = move_states(mine_ref[...], their_map_ref) + theirs_ref[...]

    later(code_ref, then, otherwise)


def merge_states(code, mine, theirs, my_map, their_map):
    lines, levels = mine.shape
    return call(
        merge_states_kernel, [SMEM] + [VMEM] * 4, shape(lines, levels), 12 * lines * levels**2
    )(code, mine, theirs, my_map, their_map)


def merge_kernel(start, kind, apart, halves, half, code_ref, *refs):
    refs = list(refs)
    mine_map = refs.pop(0)
    if apart and kind != "maps":
        mine_states = refs.pop(0)
    else:
        mine_states = None if kind == "maps" else mine_map.at[start:]
    here = refs.pop(0)
    there = refs.pop(0) if halves else None
    their_states = refs.pop(0) if apart and kind != "maps" else None
    out = refs.pop(0)
    core = code_ref[0] // 2
    their_map = here
    if halves:
        their_map = refs.pop(0)
        rows = here.shape[0]

        @pl.when(core == 0)
        def _():
            their_map[:rows] = here[...]
            their_map[rows:] = there[...]

        @pl.when(core == 1)
        def _():
            their_map[:rows] = there[...]
            their_map[rows:] = here[...]

    if their_states is None and kind != "maps":
        their_states = their_map.at[start:]

    def joined(left_map, left_states, right_map, right_states):
        if kind == "both" and not apart:
            join(left_map, right_map, out)
            return
        if kind != "states":
            join_maps(left_map, right_map, out)
        if kind == "maps":
            return
        states = move_states(left_states[...], right_map) + right_states[...]
        if kind == "both":
            out[start:] = states
        else:
            out[...] = states

    later(
        code_ref,
        lambda: joined(their_map, their_states, mine_map, mine_states),
        lambda: joined(mine_map, mine_states, their_map, their_states),
    )
    if half:
        half_ref = refs.pop(0)
        rows = half_ref.shape[0]

        @pl.when(core == 0)
        def _():
            half_ref[...] = out[:rows]

        @pl.when(core == 1)
        def _():
            half_ref[...] = out[rows:]


def merge(code, mine, theirs, kind, lines, apart, halves, half):
    levels = mine[0].shape[1]
    start = levels + PAD
    rows = {"maps": start, "both": start + lines, "states": lines}[kind]
    out = [shape(rows, levels)]
    if halves:
        out.append(shape(2 * theirs[0].shape[0], levels))
    if half:
        out.append(shape(rows // 2, levels))
    operands = (*mine, *theirs)
    got = call(
        functools.partial(merge_kernel, start, kind, apart, halves, half),
        [SMEM] + [VMEM] * len(operands),
        out,
        12 * rows * levels**2,
    )(code, *operands)
    return got[0], got[1] if halves else theirs[0], got[-1]


def four_kernel(
    code_ref, mine_ref, here_ref, there_ref, this_ref, that_ref,
    total_ref, beside_ref, front_ref, half_ref, four_ref, back_ref,
):
    core = lax.rem(code_ref[0], 2)
    place = code_ref[0] // 2
    rows = half_ref.shape[0]
    four_ref[place] = mine_ref[...]
    four_ref[place ^ (1 + core)] = here_ref[...]
    four_ref[place ^ (2 - core)] = there_ref[...]
    four_ref[place ^ 3, pl.ds(core * rows, rows)] = this_ref[...]
    four_ref[place ^ 3, pl.ds((1 - core) * rows, rows)] = that_ref[...]
    join(four_ref.at[0], four_ref.at[1], front_ref)
    join(four_ref.at[2], four_ref.at[3], back_ref)
    join(front_ref, back_ref, total_ref)
    half_ref[...] = total_ref[pl.ds(core * rows, rows)]
    beside_ref[...] = four_ref[place ^ 1]


def join_four(code, mine, here, there, this, that):
    rows, levels = mine.shape
    whole = shape(rows, levels)
    return call(
        four_kernel,
        [SMEM] + [VMEM] * 5,
        [whole, whole, whole, shape(rows // 2, levels)],
        36 * rows * levels**2,
        [pltpu.VMEM((4, rows, levels), F32), pltpu.VMEM((rows, levels), F32)],
    )(code, mine, here, there, this, that)


def extend_kernel(first, apart, code_ref, *refs):
    refs = list(refs)
    their_map = refs.pop(0)
    levels = their_map.shape[1]
    start = levels + PAD
    their_states = refs.pop(0)[...] if apart else their_map[start:]
    if first:
        (ahead_ref,) = refs
    else:
        before_ref, ahead_ref = refs

    def then():
        if first:
            ahead_ref[:start] = their_map[:start]
            ahead_ref[start:] = their_states
        else:
            join(their_map, before_ref, ahead_ref)

    def otherwise():
        if first:
            row = lax.broadcasted_iota(jnp.int32, ahead_ref.shape, 0)
            column = lax.broadcasted_iota(jnp.int32, ahead_ref.shape, 1)
            ahead_ref[...] = jnp.where(row == column, 1.0, 0.0).astype(F32)
        else:
            ahead_ref[...] = before_ref[...]

    later(code_ref, then, otherwise)


def extend(code, theirs, before):
    levels = theirs[0].shape[1]
    apart = len(theirs) == 2
    rows = levels + PAD + (theirs[1].shape[0] if apart else theirs[0].shape[0] - levels - PAD)
    first = before is None
    operands = theirs if first else (*theirs, before)
    return call(
        functools.partial(extend_kernel, first, apart),
        [SMEM] + [VMEM] * len(operands),
        shape(rows, levels),
        12 * rows * levels**2,
    )(code, *operands)


def enter_kernel(from_ref, map_ref, own_ref, out_ref):
    out_ref[...] = move_states(from_ref[...], map_ref) + own_ref[...]


def enter(states, total, own):
    lines, levels = own.shape
    return call(enter_kernel, [VMEM] * 3, shape(lines, levels), 12 * lines * levels**2)(
        states, total, own
    )


def plane_total_kernel(code_ref, mine_ref, theirs_ref, total_ref):
    @pl.when(code_ref[0] < 4)
    def _():
        total_ref[...] = jnp.zeros_like(total_ref)

    @pl.when(code_ref[0] >= 4)
    def _():
        later(
            code_ref,
            lambda: join(theirs_ref, mine_ref, total_ref),
            lambda: join(mine_ref, theirs_ref, total_ref),
        )


def plane_total(code, mine, theirs):
    rows, levels = mine.shape
    return call(
        plane_total_kernel, [SMEM, VMEM, VMEM], shape(rows, levels), 12 * rows * levels**2
    )(code, mine, theirs)


def settle_planes_kernel(code_ref, beside_ref, from_ref, before_ref, ahead_ref):
    start = before_ref.shape[1] + PAD

    def then():
        join(beside_ref, before_ref, ahead_ref)

    def otherwise():
        ahead_ref[:start] = before_ref[:start]
        ahead_ref[start:] = move_states(from_ref[...], before_ref) + before_ref[start:]

    later(code_ref, then, otherwise)


def settle_planes(code, beside, from_first, before):
    rows, levels = before.shape
    return call(
        settle_planes_kernel, [SMEM] + [VMEM] * 3, shape(rows, levels), 12 * rows * levels**2
    )(code, beside, from_first, before)


def finish_kernel(code_ref, one_ref, two_ref, before_ref, prefix_ref, trial_ref, *refs):
    *part_refs, solved_ref, held_ref, incoming, arrived = refs
    fetch(prefix_ref, held_ref, arrived)
    start = before_ref.shape[1] + PAD
    entering = one_ref[...] + two_ref[...]
    high, low = split(move_states(entering, before_ref) + before_ref[start:])
    lines = high.shape[0]
    incoming[:lines] = high
    incoming[lines:] = low
    product = functools.partial(jnp.dot, preferred_element_type=F32)

    @pl.loop(0, held_ref.shape[0])
    def _(cell):
        block_copy(prefix_ref, held_ref, arrived, cell).wait()
        map_high, map_low = split(held_ref[cell])
        both = product(incoming[...], map_high)
        rest = both[lines:] + product(incoming[:lines], map_low)
        solved_ref[:, cell, :] = trial_ref[cell] + (both[:lines] + rest)

    share = part_refs[0].shape[0]
    for turn, part_ref in enumerate(part_refs):
        part_ref[...] = solved_ref[pl.ds((code_ref[0] ^ turn) * share, share)]


def finish(here, entering, before, prefix, trial, parts):
    cells, lines, levels = trial.shape
    return call(
        finish_kernel,
        [SMEM, VMEM, VMEM, VMEM, HBM, VMEM],
        [shape(lines // parts, cells, levels)] * parts,
        12 * (cells + 1) * lines * levels**2,
        [
            pltpu.VMEM((lines, cells, levels), F32),
            pltpu.VMEM(prefix.shape, F32),
            pltpu.VMEM((2 * lines, levels), jnp.bfloat16),
            pltpu.SemaphoreType.DMA((cells,)),
        ],
        None,
        LARGE,
    )(here, *entering, before, prefix, trial)


def shards(span_count, forcing, blocks, upstream):
    cells, levels, _ = blocks.shape
    share = forcing.shape[0]
    lines = share * span_count
    here = lax.axis_index("span").astype(jnp.int32).reshape(1)

    def trade(parts):
        kept, *sent = parts
        return [kept] + [partner(part, "span", k + 1) for k, part in enumerate(sent)]

    def partner(value, axis, mask):
        count = lax.axis_size(axis)
        return lax.ppermute(value, axis, [(i, i ^ mask) for i in range(count)])

    forcing_parts = trade(cut(here, forcing, span_count))
    prefix, maps = prefix_maps(blocks, upstream)
    forcing_parts, maps = lax.optimization_barrier((forcing_parts, maps))
    trial, states = trial_states(here, blocks, upstream, forcing_parts)

    def code_of(axis, bit):
        upper = jnp.where((lax.axis_index(axis) & bit) != 0, 1, 0)
        core = jnp.where((lax.axis_index("line") & CORE) != 0, 2, 0)
        return (upper + core).astype(jnp.int32).reshape(1)

    def along_four(total, half, before):
        device = lax.axis_index("line")
        pairs = [(i, i ^ FOUR[i & CORE]) for i in range(lax.axis_size("line"))]
        here, this = lax.ppermute(total, "line", pairs), partner(half, "line", THIRD)
        here, this, before = lax.optimization_barrier((here, this, before))
        there, that = partner(here, "line", CORE), partner(this, "line", CORE)
        code = (device & (CORE | THIRD)).astype(jnp.int32).reshape(1)
        total, beside, front, half = join_four(code, total, here, there, this, that)
        before = extend(code_of("line", FOUR[0]), (beside,), before)
        before = extend(code_of("line", FOUR[1]), (front,), before)
        return total, half, before

    total, half, before = None, None, None
    for turn, (axis, mask, bit, halves, apart) in enumerate(ROUNDS):
        code = code_of(axis, bit)
        last = turn == len(ROUNDS) - 1
        if halves:
            mine_half = partner(half, axis, mask)
            mine_half, before = lax.optimization_barrier((mine_half, before))
            theirs = (mine_half, partner(mine_half, "line", CORE))
        else:
            theirs = (partner(maps if apart else total, axis, mask),)
            if before is not None:
                theirs, before = lax.optimization_barrier((theirs, before))
        mine = (total,)
        if apart:
            their_states = partner(states, axis, mask)
            mine, theirs = (maps, states), (*theirs, their_states)
        if last:
            plane, whole, _ = merge(code, mine, theirs, "states", lines, apart, halves, False)
            inner = (lax.axis_index("line") // PLANE + 1) // 2 == 1
            total = plane_total(code + jnp.where(inner, 4, 0).astype(jnp.int32), total, whole)
        else:
            half_too = turn == len(ROUNDS) - 2
            total, whole, half = merge(code, mine, theirs, "both", lines, apart, halves, half_too)
        before = extend(code, (whole, their_states) if apart else (whole,), before)
        if turn == len(ROUNDS) - 2:
            total, half, before = along_four(total, half, before)

    def across(value, source, target):
        shift = (target - source) * PLANE
        pairs = [(i, i + shift) for i in range(source * PLANE, (source + 1) * PLANE)]
        return lax.ppermute(value, "line", pairs)

    from_first = across(plane, 0, 1)
    beside = across(total, 2, 3)
    from_first, before = lax.optimization_barrier((from_first, before))
    joined = enter(from_first, total, plane)
    two_on = across(joined, 1, 3)
    entering = (two_on, across(joined, 1, 2))
    in_last = jnp.where(lax.axis_index("line") >= 3 * PLANE, 1, 0).astype(jnp.int32).reshape(1)
    before = settle_planes(in_last, beside, from_first, before)
    return assemble(here, trade(finish(here, entering, before, prefix, trial, span_count)))


def solution(mesh):
    placed = (P("span", "line", None), P(("line", "span"), None, None), P(("line", "span"), None))
    return jax.shard_map(
        functools.partial(shards, mesh.shape["span"]),
        mesh=mesh,
        in_specs=placed,
        out_specs=P("span", "line", None),
        check_vma=False,
    )
```
